256 devices in a mesh: ctx: 16 (over y_lo, z), tp: 16 (over x, y_hi, core).
Axes of the slice: x: 4, y: 4 (y_hi: 2, y_lo: 2; y = y_hi * 2 + y_lo), z: 8, core: 2. Of those that a mesh axis runs over, the one named last changes fastest.
Arguments:
- tokens: bfloat16 [8192, 4096], P('ctx', 'tp'), may hold values from -6 to 6
- seg_ids: int32 [8192], P('ctx'), may hold values from 0 to 5, never falling along the last dimension, each value on 1 to 4096 neighbouring positions
- w_x: bfloat16 [4096, 8192], P(None, 'tp'), may hold values from -0.09375 to 0.09375
- w_z: bfloat16 [4096, 8192], P(None, 'tp'), may hold values from -0.09375 to 0.09375
- w_bc: bfloat16 [4096, 2048], P('tp'), may hold values from -0.09375 to 0.09375
- w_dt: bfloat16 [4096, 128], P('tp'), may hold values from -0.09375 to 0.09375
- conv_x: float32 [4, 8192], P(None, 'tp'), may hold values from -3 to 3
- conv_x_bias: float32 [8192], P('tp'), may hold values from -3 to 3
- conv_bc: float32 [4, 2048], replicated, may hold values from -3 to 3
- conv_bc_bias: float32 [2048], replicated, may hold values from -3 to 3
- dt_bias: float32 [128], P('tp'), may hold values from -2 to 1
- decay_rate: float32 [128], P('tp'), may hold values from 1.2207031e-06 to 0.03
- skip_gain: float32 [128], P('tp'), may hold values from 0.5 to 1.5
- norm_weight: float32 [8192], P('tp'), may hold values from 0.5 to 1.5
- w_out: bfloat16 [8192, 4096], P('tp', 'ctx'), may hold values from -0.09375 to 0.09375
Outputs:
- mixed: bfloat16 [8192, 4096], P('ctx', 'tp')
The draws below stay inside these ranges and needn't reach their ends.
Inputs may be any that keep to these rules, and one draw needn't show every extreme that they name: `seg_ids`: document ids never fall along the sequence, start at 0 and rise by one where a document starts; one document covers 8192 / 2 tokens.
All inputs are finite; a program needn't handle non-finite values.
Results may differ from the reference program's by a relative error of at most 0.015.
Values may be sent and summed in bfloat16 or wider, within the bound.
No kernel may reach another device: no remote copies, remote signals or barrier semaphores. Data moves between devices by JAX's collectives and lax.ppermute only.
A program may use at most 128 MiB of HBM per device.

```python
import math
import jax
import jax.numpy as jnp
import numpy as np
from jax import lax

D = 4096
H = 128
P_SIZE = 64
N = 128
G = 8
L = 256
CONV = 4
TOTAL = 8192
INNER = 8192


def with_spikes(result, own_key, source, target, blocks, factor):
    def block_of(dim):
        return (jnp.arange(result.shape[dim]) // (result.shape[dim] // blocks)).reshape((-1,) + (1,) * (result.ndim - 1 - dim))

    one_side = jax.random.permutation(own_key, blocks)[block_of(target)]
    other_side = (block_of(target) + blocks // 2) % blocks
    return jnp.where((block_of(source) == one_side) | (block_of(source) == other_side), factor * result, result)


def block_scale(stream_key, shape, cuts, least, high):
    gain = 1.0
    for position, blocks in cuts:
        heights = jax.random.uniform(jax.random.fold_in(jax.random.fold_in(stream_key, 6), position), (blocks,), jnp.float32, least / len(cuts), high / len(cuts))
        gain = gain * jnp.repeat(jnp.exp(heights), shape[position] // blocks).reshape((-1,) + (1,) * (len(shape) - 1 - position))
    return gain


def length_profile(amount, total, limit, slope):
    portions = [(1 << 20) // math.isqrt(grade ** slope) + 1 for grade in range(2, amount + 1)]
    rest, holding = total - limit - (amount - 1), [1] * (amount - 1)
    while rest > 0:
        free = [i for i in range(amount - 1) if holding[i] < limit]
        mass, remaining = sum([portions[i] for i in free]), rest
        for i in free:
            addition = min(limit - holding[i], max(1, remaining * portions[i] // mass), rest)
            holding[i] = holding[i] + addition
            rest = rest - addition
    return np.array([limit] + holding)


def uneven(stream_key, number_of, total, reach, skew):
    if number_of == 2:
        one = jax.random.randint(stream_key, (), max(1, total - reach), min(reach, total - 1) + 1)
        return jnp.stack([one, total - one])
    sizes = jnp.asarray(length_profile(number_of, total, reach, skew), jnp.int32)
    pairs = (number_of - 1) // 2
    source_of, sink = sizes[1:1 + 2 * pairs:2], sizes[2:2 + 2 * pairs:2]
    margin = jnp.minimum(source_of - 1, reach - sink)
    moved = jax.random.randint(jax.random.fold_in(stream_key, 1), (pairs,), 0, 1 << 20) % (margin + 1)
    sizes = sizes.at[1:1 + 2 * pairs:2].set(source_of - moved).at[2:2 + 2 * pairs:2].set(sink + moved)
    return sizes[jax.random.permutation(jax.random.fold_in(stream_key, 2), number_of)]


def normal_values(stream_key, dims, scale, reach, shards=(), dtype=jnp.bfloat16):
    array = scale * jax.random.normal(stream_key, dims, jnp.float32)
    if shards:
        array = array * block_scale(stream_key, dims, shards, -0.22, 0.18)
    return jnp.clip(array, -reach, reach).astype(dtype)


def heavy_noise(key, shape, width, limit, split, heavy, dtype=jnp.bfloat16):
    entries = width * jax.random.normal(key, shape, jnp.float32)
    if split:
        entries = entries * block_scale(key, shape, split, -0.22, 0.18)
    return jnp.clip(with_spikes(entries, jax.random.fold_in(key, 3), *heavy), -limit, limit).astype(dtype)


def setup_inputs(seed: int = 0) -> dict:
    arg_keys = jax.random.split(jax.random.key(seed), 16)
    return {
        "tokens": normal_values(arg_keys[0], (TOTAL, D), 1.0, 6.0, ((0, 16), (1, 16))),
        "seg_ids": jnp.searchsorted(jnp.cumsum(uneven(arg_keys[1], 6, TOTAL, TOTAL // 2, 0)), jnp.arange(TOTAL), side="right").astype(jnp.int32),
        "w_x": normal_values(arg_keys[2], (D, INNER), D ** -0.5, 0.09375, ((1, 16),)),
        "w_z": normal_values(arg_keys[3], (D, INNER), D ** -0.5, 0.09375, ((1, 16),)),
        "w_bc": normal_values(arg_keys[4], (D, 2 * G * N), D ** -0.5, 0.09375, ((0, 16),)),
        "w_dt": normal_values(arg_keys[5], (D, H), D ** -0.5, 0.09375, ((0, 16),)),
        "conv_x": normal_values(arg_keys[6], (CONV, INNER), CONV ** -0.5, 3.0, ((1, 16),), jnp.float32),
        "conv_x_bias": normal_values(arg_keys[7], (INNER,), 0.5, 3.0, ((0, 16),), jnp.float32),
        "conv_bc": normal_values(arg_keys[8], (CONV, 2 * G * N), CONV ** -0.5, 3.0, (), jnp.float32),
        "conv_bc_bias": normal_values(arg_keys[9], (2 * G * N,), 0.5, 3.0, (), jnp.float32),
        "dt_bias": jnp.clip(-2.0 + 3.0 * jax.random.uniform(arg_keys[10], (H,), jnp.float32) ** block_scale(arg_keys[10], (H,), ((0, 16),), -0.2, 0.2), -2.0, 1.0),
        "decay_rate": jnp.clip(jnp.exp(math.log(0.03) - 10.109526 * jax.random.uniform(arg_keys[11], (H,), jnp.float32) ** block_scale(arg_keys[11], (H,), ((0, 16),), -0.2, 0.2)), 1.220703097715159e-06, 0.03),
        "skip_gain": jnp.clip(0.5 + 1.0 * jax.random.uniform(arg_keys[12], (H,), jnp.float32) ** block_scale(arg_keys[12], (H,), ((0, 16),), -0.2, 0.2), 0.5, 1.5),
        "norm_weight": jnp.clip(1.0 + 0.1 * jax.random.normal(arg_keys[13], (INNER,), jnp.float32), 0.5, 1.5),
        "w_out": heavy_noise(arg_keys[14], (INNER, D), INNER ** -0.5, 0.09375, ((0, 16), (1, 16)), (0, 1, 16, 2.0)),
    }


NORM_EPS = 1e-05
HIGHEST_PRECISION = lax.Precision.HIGHEST

def causal_conv(values, seg_now, prior_vals, prior_seg, taps, offsets):
    padded = jnp.concatenate([prior_vals, values], axis=0).astype(jnp.float32)
    padded_seg = jnp.concatenate([prior_seg, seg_now], axis=0)
    num_rows = values.shape[0]
    summed = jnp.zeros(values.shape, jnp.float32) + offsets[None, :]
    for tap in range(taps.shape[0]):
        shifted = padded[tap:tap + num_rows]
        same_doc = (padded_seg[tap:tap + num_rows] == seg_now).astype(jnp.float32)[:, None]
        summed = summed + taps[tap][None, :] * shifted * same_doc
    return jax.nn.silu(summed).astype(jnp.bfloat16)

def stretch_pass(state_now, prior_id, x_vals, b_vals, c_vals, dt_vals, log_vals, seg_now):
    length = seg_now.shape[0]
    cum_decay = jnp.cumsum(log_vals, axis=0)
    positions = jnp.arange(length)
    causal = (positions[:, None] >= positions[None, :]) & (seg_now[:, None] == seg_now[None, :])
    causal_full = causal[:, :, None, None]
    gaps = cum_decay[:, None] - cum_decay[None, :]
    decays = jnp.where(causal_full, jnp.exp(jnp.where(causal_full, gaps, 0.0)), 0.0)
    b_float = b_vals.astype(jnp.float32)
    c_float = c_vals.astype(jnp.float32)
    x_float = x_vals.astype(jnp.float32)
    scores = jnp.einsum('tgn,sgn->tsg', c_float, b_float)
    weights = scores[:, :, :, None] * decays * dt_vals[None]
    weights_low = lax.optimization_barrier(weights.astype(jnp.bfloat16)).astype(jnp.float32)
    intra_out = jnp.einsum('tsgh,sghp->tghp', weights_low, x_float)
    carried = jnp.exp(cum_decay) * (seg_now == prior_id).astype(jnp.float32)[:, None, None]
    inter_out = jnp.einsum('tgn,ghpn->tghp', c_float, state_now, precision=HIGHEST_PRECISION) * carried[..., None]
    last_id = seg_now[length - 1]
    tail_decay = jnp.exp(cum_decay[length - 1][None] - cum_decay) * (seg_now == last_id).astype(jnp.float32)[:, None, None] * dt_vals
    scaled_x = x_float * tail_decay[..., None]
    fresh_state = jnp.einsum('sghp,sgn->ghpn', scaled_x, b_float, precision=HIGHEST_PRECISION)
    new_state = carried[length - 1][..., None, None] * state_now + fresh_state
    return (new_state, intra_out + inter_out)

def run_stretches(state_now, prior_id, x_vals, b_vals, c_vals, dt_vals, log_vals, seg_now):
    num_stretches = seg_now.shape[0] // L

    def stretch_step(carry_pair, pieces):
        new_state, outputs = stretch_pass(carry_pair[0], carry_pair[1], *pieces)
        return ((new_state, pieces[5][L - 1]), outputs)
    shaped = tuple((member.reshape((num_stretches, L) + member.shape[1:]) for member in (x_vals, b_vals, c_vals, dt_vals, log_vals, seg_now)))
    carry_end, outputs = lax.scan(stretch_step, (state_now, prior_id), shaped)
    return (carry_end[0], outputs.reshape((num_stretches * L,) + outputs.shape[2:]))

def reference(tokens, seg_ids, w_x, w_z, w_bc, w_dt, conv_x, conv_x_bias, conv_bc, conv_bc_bias, dt_bias, decay_rate, skip_gain, norm_weight, w_out):
    group_heads = H // G
    x_raw = jnp.dot(tokens, w_x, preferred_element_type=jnp.float32).astype(jnp.bfloat16)
    z_raw = jnp.dot(tokens, w_z, preferred_element_type=jnp.float32).astype(jnp.bfloat16)
    bc_raw = jnp.dot(tokens, w_bc, preferred_element_type=jnp.float32).astype(jnp.bfloat16)
    dt_raw = jnp.dot(tokens, w_dt, preferred_element_type=jnp.float32)
    rim_rows = CONV - 1
    ids_prior = jnp.full((rim_rows,), -1, jnp.int32)
    x_conv = causal_conv(x_raw, seg_ids, jnp.zeros((rim_rows, INNER), jnp.bfloat16), ids_prior, conv_x, conv_x_bias)
    bc_conv = causal_conv(bc_raw, seg_ids, jnp.zeros((rim_rows, 2 * G * N), jnp.bfloat16), ids_prior, conv_bc, conv_bc_bias)
    dt_vals = jax.nn.softplus(dt_raw + dt_bias[None, :])
    log_vals = -decay_rate[None, :] * dt_vals
    shape_heads = (TOTAL, G, group_heads)
    x_vals = x_conv.reshape(shape_heads + (P_SIZE,))
    bc_four = bc_conv.reshape(TOTAL, G, 2, N)
    zero_state = jnp.zeros((G, group_heads, P_SIZE, N), jnp.float32)
    final_state, y_ssd = run_stretches(zero_state, seg_ids[0], x_vals, bc_four[:, :, 0], bc_four[:, :, 1], dt_vals.reshape(shape_heads), log_vals.reshape(shape_heads), seg_ids)
    y_all = y_ssd + skip_gain.reshape(G, group_heads)[None, :, :, None] * x_vals.astype(jnp.float32)
    gated = y_all * jax.nn.silu(z_raw.astype(jnp.float32)).reshape(shape_heads + (P_SIZE,))
    mean_sq = lax.optimization_barrier(jnp.mean(gated * gated, axis=(2, 3)))
    normed = (gated * lax.rsqrt(mean_sq + NORM_EPS)[:, :, None, None]).reshape(TOTAL, INNER) * norm_weight[None, :]
    return jnp.dot(normed.astype(jnp.bfloat16), w_out, preferred_element_type=jnp.float32).astype(jnp.bfloat16)
```

```python
import functools

import jax
import jax.numpy as jnp
from jax import lax
from jax.experimental import pallas as pl
from jax.experimental.pallas import tpu as pltpu
from jax.sharding import PartitionSpec as P

H = 128
P_SIZE = 64
N = 128
G = 8
L = 256
CONV = 4
HALO = 16
NORM_EPS = 1e-05
HIGHEST = lax.Precision.HIGHEST

CHIPS = 8
CORES = 2
HEADS = 8
CH = HEADS * P_SIZE
ROWS = 512
FEAT = 256
X_RING = 4
VMEM = pl.BlockSpec(memory_space=pltpu.VMEM)
BF16 = jnp.bfloat16
F32 = jnp.float32


def params(mib, grid=False):
    more = {"dimension_semantics": ("arbitrary",)} if grid else {}
    return pltpu.CompilerParams(vmem_limit_bytes=mib * 2**20, **more)


def dot(a, b):
    return jnp.dot(a, b, preferred_element_type=F32)


def dot_nt(a, b):
    return lax.dot_general(a, b, (((1,), (1,)), ((), ())), preferred_element_type=F32)


def dot_tn(a, b):
    return lax.dot_general(a, b, (((0,), (0,)), ((), ())), preferred_element_type=F32)


def silu(v):
    return v / (1.0 + jnp.exp(-v))


def spread(cols, first=0, count=HEADS):
    shape = (HEADS, count * P_SIZE)
    head = lax.broadcasted_iota(jnp.int32, shape, 0)
    lane = lax.broadcasted_iota(jnp.int32, shape, 1)
    pick = (head == lane // P_SIZE + first).astype(F32)
    return jnp.dot(cols, pick, precision=HIGHEST, preferred_element_type=F32)


def my_core():
    return lax.rem(lax.axis_index("tp"), CORES)


def add_to(acc, step, value):
    @pl.when(step == 0)
    def _():
        acc[...] = value

    @pl.when(step > 0)
    def _():
        acc[...] += value


def weight_rows(ref, pair, core):
    start = pl.multiple_of(pair * 2 * FEAT + core * FEAT, FEAT)
    return ref[pl.ds(start, FEAT), :]


def conv_chunk(raw, at, rows, masks, taps, offsets):
    total = offsets + taps[CONV - 1 : CONV, :] * raw[at + HALO : at + HALO + rows, :]
    for tap in range(CONV - 1):
        first = at + HALO - (CONV - 1) + tap
        shifted = raw[first : first + rows, :]
        total = total + taps[tap : tap + 1, :] * (shifted * masks[:, tap : tap + 1])
    return silu(total).astype(BF16)


def scan_input_kernel(
    own,
    sib,
    w_x,
    w_own,
    w_sib,
    cols,
    taps_x,
    bias_x,
    taps_bc,
    bias_bc,
    dt_bias,
    decay,
    xc,
    bcc,
    hcol,
    hrow,
    s0,
    pay,
    acc_x,
    acc_bc,
):
    step = pl.program_id(0)
    core = my_core()
    part_x, part_bc = 0.0, 0.0
    for pair in range(own.shape[0]):
        part_x += dot(own[pair], weight_rows(w_x, pair, core))
        part_x += dot(sib[pair], weight_rows(w_x, pair, 1 - core))
        part_bc += dot_nt(own[pair], w_own[pair])
        part_bc += dot_nt(sib[pair], w_sib[pair])
    add_to(acc_x, step, part_x)
    add_to(acc_bc, step, part_bc)

    @pl.when(step == pl.num_programs(0) - 1)
    def _():
        raw_dt = acc_bc[HALO:, 2 * N : 2 * N + 2 * HEADS]
        raw_dt = jnp.where(core == 0, raw_dt[:, :HEADS], raw_dt[:, HEADS:])
        pre = raw_dt + dt_bias[...]
        dt = jnp.maximum(pre, 0.0) + jnp.log1p(jnp.exp(-jnp.abs(pre)))
        loga = -decay[...] * dt
        acc_x[...] = acc_x[...].astype(BF16).astype(F32)
        acc_bc[...] = acc_bc[...].astype(BF16).astype(F32)
        for at in range(0, ROWS, 64):
            masks = cols[at : at + 64, :]
            xc[at : at + 64, :] = conv_chunk(acc_x, at, 64, masks, taps_x, bias_x[...])
            bcc[at : at + 64, :] = conv_chunk(
                acc_bc.at[:, : 2 * N], at, 64, masks, taps_bc, bias_bc[...]
            )
        lower = (
            lax.broadcasted_iota(jnp.int32, (L, L), 0) >= lax.broadcasted_iota(jnp.int32, (L, L), 1)
        ).astype(F32)
        cum0 = jnp.dot(lower, loga[:L], precision=HIGHEST, preferred_element_type=F32)
        cum1 = jnp.dot(lower, loga[L:], precision=HIGHEST, preferred_element_type=F32)
        end0, end1 = cum0[L - 1 :], cum1[L - 1 :]
        slab = jnp.exp(jnp.concatenate([cum0, cum1 + end0], axis=0)) * cols[:, 3:4]
        inner = jnp.exp(cum1) * cols[L:, 5:6]
        tail0 = jnp.exp(end0 - cum0) * cols[:L, 6:7] * dt[:L]
        tail1 = jnp.exp(end1 - cum1) * cols[L:, 4:5] * dt[L:]
        cum = jnp.concatenate([cum0, cum1], axis=0)
        blank = jnp.zeros((ROWS, 128 - 4 * HEADS), F32)
        wide = jnp.concatenate(
            [cum, dt, slab, jnp.concatenate([inner, inner], axis=0), blank], axis=1
        )
        hcol[...] = wide
        hrow[...] = wide.T[: 2 * HEADS]
        scaled0 = (xc[:L, :].astype(F32) * spread(tail0)).astype(BF16)
        scaled1 = (xc[L:, :].astype(F32) * spread(tail1)).astype(BF16)
        state0 = dot_tn(bcc[:L, :N], scaled0)
        state1 = dot_tn(bcc[L:, :N], scaled1)
        s0[...] = state0.astype(BF16)
        ends = jnp.concatenate(
            [inner[L - 1 :], slab[ROWS - 1 :], jnp.zeros((6, HEADS), F32)], axis=0
        )
        ends = spread(ends)
        final = ends[0:1] * state0 + state1
        high = ends[1:2].astype(BF16).astype(F32)
        low = ends[1:2] - high
        row = lax.broadcasted_iota(jnp.int32, (8, CH), 0)
        factor = jnp.where(row == 0, high, jnp.where(row == 1, low, 0.0))
        for piece in range(16):
            pay[piece] = jnp.concatenate(
                [final[8 * piece : 8 * piece + 8], factor], axis=0
            ).astype(BF16)


def scan_input(own, sib, w_x, w_own, w_sib, cols, small):
    steps = 4
    each = CHIPS // steps
    rows = ROWS + HALO
    whole = lambda a: pl.BlockSpec(a.shape, lambda i: (0,) * a.ndim)
    blocks = lambda a: pl.BlockSpec((each,) + a.shape[1:], lambda i: (i, 0, 0))
    shapes = [
        jax.ShapeDtypeStruct((ROWS, CH), BF16),
        jax.ShapeDtypeStruct((ROWS, 2 * N), BF16),
        jax.ShapeDtypeStruct((ROWS, 128), F32),
        jax.ShapeDtypeStruct((2 * HEADS, ROWS), F32),
        jax.ShapeDtypeStruct((N, CH), BF16),
        jax.ShapeDtypeStruct((16, 16, CH), BF16),
    ]
    return pl.pallas_call(
        scan_input_kernel,
        grid=(steps,),
        in_specs=[
            blocks(own),
            blocks(sib),
            pl.BlockSpec((each * 2 * FEAT, CH), lambda i: (i, 0)),
            blocks(w_own),
            blocks(w_sib),
            whole(cols),
        ]
        + [whole(a) for a in small],
        out_specs=[whole(a) for a in shapes],
        out_shape=shapes,
        scratch_shapes=[
            pltpu.VMEM((rows, CH), F32),
            pltpu.VMEM((rows, 2 * N + 2 * HEADS), F32),
        ],
        compiler_params=params(40, True),
        cost_estimate=pl.CostEstimate(
            flops=2 * rows * 4096 * (CH + 272), bytes_accessed=12 * 2**20, transcendentals=10**6
        ),
        name="scan_input",
    )(own, sib, w_x, w_own, w_sib, cols, *small)


def intra_kernel(xc, bcc, hcol, hrow, s0, cols, seg_row, skip, y):
    for block in range(2):
        at = block * L
        b_vals, c_vals = bcc[at : at + L, :N], bcc[at : at + L, N:]
        after = lax.broadcasted_iota(jnp.int32, (L, L), 0) >= lax.broadcasted_iota(
            jnp.int32, (L, L), 1
        )
        same = cols[at : at + L, 7:8] == seg_row[0:1, at : at + L]
        scores = jnp.where(after & same, dot_nt(c_vals, b_vals), 0.0)
        for half in range(2):
            lanes = slice(half * 256, half * 256 + 256)
            weights, values = [], []
            x_half = xc[at : at + L, lanes]
            head_of = lax.broadcasted_iota(jnp.int32, (1, 256), 1) // P_SIZE
            for part in range(4):
                head = half * 4 + part
                gap = hcol[at : at + L, head : head + 1] - hrow[head : head + 1, at : at + L]
                decay = jnp.exp(jnp.minimum(gap, 0.0))
                dt_row = hrow[HEADS + head : HEADS + head + 1, at : at + L]
                weights.append((scores * decay * dt_row).astype(BF16))
                values.append(x_half * (head_of == part).astype(BF16))
            out = dot(jnp.concatenate(weights, axis=1), jnp.concatenate(values, axis=0))
            out = out + skip[:, lanes] * x_half.astype(F32)
            if block == 1:
                carried = spread(hcol[at : at + L, 3 * HEADS : 4 * HEADS], half * 4, 4)
                out = out + carried * dot(c_vals, s0[:, lanes])
            y[at : at + L, lanes] = out


def intra(*args):
    return pl.pallas_call(
        intra_kernel,
        in_specs=[VMEM] * len(args),
        out_specs=VMEM,
        out_shape=jax.ShapeDtypeStruct((ROWS, CH), F32),
        compiler_params=params(24),
        cost_estimate=pl.CostEstimate(
            flops=2 * ROWS * L * CH * 4, bytes_accessed=4 * 2**20, transcendentals=2 * 10**6
        ),
        name="intra",
    )(*args)


def gate_kernel(own, sib, w_z, out, acc):
    step = pl.program_id(0)
    core = my_core()
    part = 0.0
    for pair in range(own.shape[0]):
        part += dot(own[pair, HALO:, :], weight_rows(w_z, pair, core))
        part += dot(sib[pair, HALO:, :], weight_rows(w_z, pair, 1 - core))
    add_to(acc, step, part)

    @pl.when(step == pl.num_programs(0) - 1)
    def _():
        for at in range(0, ROWS, 64):
            out[at : at + 64, :] = silu(acc[at : at + 64, :].astype(BF16).astype(F32))


def gate(own, sib, w_z):
    steps = 4
    each = CHIPS // steps
    blocks = pl.BlockSpec((each,) + own.shape[1:], lambda i: (i, 0, 0))
    return pl.pallas_call(
        gate_kernel,
        grid=(steps,),
        in_specs=[blocks, blocks, pl.BlockSpec((each * 2 * FEAT, CH), lambda i: (i, 0))],
        out_specs=pl.BlockSpec((ROWS, CH), lambda i: (0, 0)),
        out_shape=jax.ShapeDtypeStruct((ROWS, CH), F32),
        scratch_shapes=[pltpu.VMEM((ROWS, CH), F32)],
        compiler_params=params(24, True),
        cost_estimate=pl.CostEstimate(
            flops=2 * ROWS * 4096 * CH, bytes_accessed=9 * 2**20, transcendentals=3 * 10**5
        ),
        name="gate",
    )(own, sib, w_z)


def prefix_kernel(pieces, out):
    total = jnp.zeros((8, CH), F32)
    for pair in range(8):
        held = []
        for place in (2 * pair, 2 * pair + 1):
            held.append(total)
            piece = pieces[place].astype(F32)
            total = total * (piece[8:9] + piece[9:10]) + piece[:8]
        out[16 * pair : 16 * pair + 16, :] = jnp.concatenate(held, axis=0).astype(BF16)


def prefix(pieces):
    return pl.pallas_call(
        prefix_kernel,
        in_specs=[VMEM],
        out_specs=VMEM,
        out_shape=jax.ShapeDtypeStruct((N, CH), BF16),
        compiler_params=params(8),
        name="prefix",
    )(pieces)


def join_kernel(y, gates, bcc, hcol, state, gain, out):
    for at in range(0, ROWS, 128):
        c_vals = bcc[at : at + 128, N:]
        carried = spread(hcol[at : at + 128, 2 * HEADS : 3 * HEADS])
        total = y[at : at + 128, :] + carried * dot(c_vals, state[...])
        gated = total * gates[at : at + 128, :]
        square = jnp.sum(gated * gated, axis=1, keepdims=True)
        high = square.astype(BF16).astype(F32)
        lane = lax.broadcasted_iota(jnp.int32, (128, 128), 1)
        out[at : at + 128, :CH] = (gated * gain[...]).astype(BF16)
        out[at : at + 128, CH:] = jnp.where(lane < 64, high, square - high).astype(BF16)


def join(*args):
    return pl.pallas_call(
        join_kernel,
        in_specs=[VMEM] * len(args),
        out_specs=VMEM,
        out_shape=jax.ShapeDtypeStruct((ROWS, CH + 128), BF16),
        compiler_params=params(24),
        cost_estimate=pl.CostEstimate(
            flops=2 * ROWS * N * CH, bytes_accessed=4 * 2**20, transcendentals=0
        ),
        name="join",
    )(*args)


def project_kernel(place, own, sib, w, out):
    del place
    square = own[:, CH:].astype(F32) + sib[:, CH:].astype(F32)
    mean = (square[:, 0:1] + square[:, 64:65]) / (2.0 * CH)
    part = dot(own[:, :CH], w[:CH, :]) + dot(sib[:, :CH], w[CH:, :])
    out[...] = (part * lax.rsqrt(mean + NORM_EPS)).astype(out.dtype)


def project(own, sib, w_all, place, dtype):
    width = 256
    count = w_all.shape[1] // X_RING // width
    whole = pl.BlockSpec(own.shape, lambda i, place: (0, 0))
    return pl.pallas_call(
        project_kernel,
        grid_spec=pltpu.PrefetchScalarGridSpec(
            num_scalar_prefetch=1,
            grid=(count,),
            in_specs=[
                whole,
                whole,
                pl.BlockSpec(
                    (2 * CH, width), lambda i, place: (0, place[0] * count + i)
                ),
            ],
            out_specs=pl.BlockSpec((ROWS, width), lambda i, place: (0, i)),
        ),
        out_shape=jax.ShapeDtypeStruct((ROWS, count * width), dtype),
        compiler_params=params(24, True),
        cost_estimate=pl.CostEstimate(
            flops=2 * ROWS * 2 * CH * count * width, bytes_accessed=3 * 2**20, transcendentals=0
        ),
        name="project",
    )(place, own, sib, w_all)


def swapped(value, bit):
    return lax.ppermute(value, "tp", [(i, i ^ bit) for i in range(16)])


def along_x(value, steps):
    return lax.ppermute(value, "tp", [(i, (i + 4 * steps) % 16) for i in range(16)])


def next_ctx(value):
    return lax.ppermute(value, "ctx", [(i, i + 1) for i in range(15)])


def between_chips(value):
    same_core = [[2 * chip + core for chip in range(CHIPS)] for core in range(CORES)]
    return lax.all_to_all(value, "tp", 0, 0, axis_index_groups=same_core)


def pick(core, first, second):
    return jnp.where(core == 0, first, second)


def local(
    tokens,
    seg_ids,
    w_x,
    w_z,
    w_bc,
    w_dt,
    conv_x,
    conv_x_bias,
    conv_bc,
    conv_bc_bias,
    dt_bias,
    decay_rate,
    skip_gain,
    norm_weight,
    w_out,
):
    rank = lax.axis_index("tp")
    core = rank % CORES
    chip = rank // CORES
    x_place = rank // 4
    y_place = chip % 2

    ids_row = jnp.zeros((1, FEAT), BF16).at[0, :3].set((seg_ids[-3:] + 1).astype(BF16))
    halo = next_ctx(jnp.concatenate([ids_row, tokens[1 - HALO :]], axis=0))
    ids_prior = halo[0, :3].astype(jnp.int32) - 1
    padded = jnp.concatenate([halo, tokens], axis=0)
    own = between_chips(jnp.broadcast_to(padded[None], (CHIPS,) + padded.shape))
    sib = swapped(own, 1)

    w_cols = jnp.concatenate(
        [w_bc.T.reshape(CHIPS, 2 * N, FEAT), w_dt.T.reshape(CHIPS, 2 * HEADS, FEAT)], axis=1
    )
    w_own = between_chips(w_cols)
    w_sib = swapped(w_own, 1)

    halves = (w_out[:, :128], w_out[:, 128:])
    w_pair = jnp.concatenate(
        [pick(core, *halves), swapped(pick(core, halves[1], halves[0]), 1)], axis=0
    )
    w_all = lax.all_gather(w_pair, "ctx", axis=1, tiled=True)

    ids_all = jnp.concatenate([ids_prior, seg_ids])
    prior = ids_prior[2]
    same = lambda a: (seg_ids == a).astype(F32)
    columns = [same(ids_all[tap : tap + ROWS]) for tap in range(CONV - 1)]
    columns += [same(prior), same(seg_ids[-1]), same(seg_ids[L - 1]), same(seg_ids[L - 1])]
    columns += [seg_ids.astype(F32)]
    cols = jnp.pad(jnp.stack(columns, axis=1), ((0, 0), (0, 128 - len(columns))))
    seg_row = jnp.broadcast_to(seg_ids.astype(F32)[None], (8, ROWS))

    taps_bc = lax.dynamic_slice_in_dim(conv_bc, chip * 2 * N, 2 * N, 1)
    bias_bc = lax.dynamic_slice_in_dim(conv_bc_bias, chip * 2 * N, 2 * N, 0)
    small = [conv_x, conv_x_bias[None], taps_bc, bias_bc[None], dt_bias[None], decay_rate[None]]
    xc, bcc, hcol, hrow, s0, pay = scan_input(own, sib, w_x, w_own, w_sib, cols, small)

    pieces = lax.all_to_all(pay, "ctx", 0, 0)
    skip = jnp.repeat(skip_gain, P_SIZE)[None]
    y = intra(xc, bcc, hcol, hrow, s0, cols, seg_row, skip)
    states = prefix(pieces)
    state = lax.all_to_all(states.reshape(16, 8, CH), "ctx", 0, 0).reshape(N, CH)
    own_late, sib_late, _ = lax.optimization_barrier((own, sib, hcol))
    gates = gate(own_late, sib_late, w_z)
    mine = join(y, gates, bcc, hcol, state, norm_weight[None])
    other = swapped(mine, 1)

    def outputs(ahead, dtype=BF16):
        place = ((x_place + ahead) % X_RING).astype(jnp.int32)[None]
        return project(mine, other, w_all, place, dtype)

    far = outputs(2)
    from_left = along_x(far[: ROWS // 2], 1)
    from_right = along_x(far[ROWS // 2 :], -1)
    right, left = outputs(1), outputs(3)
    right = jnp.concatenate([right[: ROWS // 2] + from_left, right[ROWS // 2 :]], axis=0)
    left = jnp.concatenate([left[: ROWS // 2], left[ROWS // 2 :] + from_right], axis=0)
    from_left, from_right = along_x(right, 1), along_x(left, -1)
    total = outputs(0, F32) + from_left.astype(F32) + from_right.astype(F32)
    parts = (total[:, :256], total[:, 256:])
    across = swapped(pick(y_place, parts[1], parts[0]).astype(BF16), 2)
    total = (pick(y_place, *parts) + across.astype(F32)).astype(BF16)
    parts = (total[:, :128], total[:, 128:])
    kept = pick(core, *parts)
    given = swapped(pick(core, parts[1], parts[0]), 1)
    return jnp.concatenate([pick(core, kept, given), pick(core, given, kept)], axis=1)


def solution(mesh):
    return jax.shard_map(
        local,
        mesh=mesh,
        in_specs=(
            P("ctx", "tp"),
            P("ctx"),
            P(None, "tp"),
            P(None, "tp"),
            P("tp", None),
            P("tp", None),
            P(None, "tp"),
            P("tp"),
            P(),
            P(),
            P("tp"),
            P("tp"),
            P("tp"),
            P("tp"),
            P("tp", "ctx"),
        ),
        out_specs=P("ctx", "tp"),
        check_vma=False,
    )
```

```python
import functools

import jax
import jax.numpy as jnp
from jax import lax
from jax.experimental import pallas as pl
from jax.experimental.pallas import tpu as pltpu
from jax.sharding import PartitionSpec as P

H = 128
P_SIZE = 64
N = 128
G = 8
L = 256
CONV = 4
HALO = 16
NORM_EPS = 1e-05
HIGHEST = lax.Precision.HIGHEST

CHIPS = 8
CORES = 2
HEADS = 8
CH = HEADS * P_SIZE
ROWS = 512
FEAT = 256
X_RING = 4
Z_RING = 8
A_ROWS = 272
B_ROWS = 256
ALL_ROWS = A_ROWS + B_ROWS
VMEM = pl.BlockSpec(memory_space=pltpu.VMEM)
BF16 = jnp.bfloat16
F32 = jnp.float32


def params(mib, grid=False):
    more = {"dimension_semantics": ("arbitrary",)} if grid else {}
    return pltpu.CompilerParams(vmem_limit_bytes=mib * 2**20, **more)


def dot(a, b):
    return jnp.dot(a, b, preferred_element_type=F32)


def dot_nt(a, b):
    return lax.dot_general(a, b, (((1,), (1,)), ((), ())), preferred_element_type=F32)


def dot_tn(a, b):
    return lax.dot_general(a, b, (((0,), (0,)), ((), ())), preferred_element_type=F32)


def silu(v):
    return v / (1.0 + jnp.exp(-v))


def spread(cols, first=0, count=HEADS):
    shape = (HEADS, count * P_SIZE)
    head = lax.broadcasted_iota(jnp.int32, shape, 0)
    lane = lax.broadcasted_iota(jnp.int32, shape, 1)
    pick = (head == lane // P_SIZE + first).astype(F32)
    return jnp.dot(cols, pick, precision=HIGHEST, preferred_element_type=F32)


def my_core():
    return lax.rem(lax.axis_index("tp"), CORES)


def add_to(acc, step, value):
    @pl.when(step == 0)
    def _():
        acc[...] = value

    @pl.when(step > 0)
    def _():
        acc[...] += value


def conv_chunk(raw, at, rows, masks, taps, offsets):
    total = offsets + taps[CONV - 1 : CONV, :] * raw[at + HALO : at + HALO + rows, :]
    for tap in range(CONV - 1):
        first = at + HALO - (CONV - 1) + tap
        shifted = raw[first : first + rows, :]
        total = total + taps[tap : tap + 1, :] * (shifted * masks[:, tap : tap + 1])
    return silu(total).astype(BF16)


def rounded(ref):
    ref[...] = ref[...].astype(BF16).astype(F32)


def step_tokens(places, first, last):
    joined = []
    for own, sib in (first, last):
        parts = [ref[slot] for slot in range(2) for ref in (own, sib)]
        joined.append(jnp.concatenate(parts, axis=1))
    return joined


def step_sources(places):
    for slot in range(2):
        chip = lax.rem(places[X_RING] + slot, 2)
        for same_core in (True, False):
            yield chip, same_core


def step_rows(places, w_ref):
    core = my_core()
    parts = []
    for chip, same_core in step_sources(places):
        from_core = core if same_core else 1 - core
        at = pl.multiple_of((chip * CORES + from_core) * FEAT, FEAT)
        parts.append(w_ref[pl.ds(at, FEAT), :])
    return jnp.concatenate(parts, axis=0)


def slot_blocks(a):
    return pl.BlockSpec((2,) + a.shape[1:], lambda i, places: (i, 0, 0))


def chip_blocks(a):
    return pl.BlockSpec((2,) + a.shape[1:], lambda i, places: (places[i], 0, 0))


def whole(a):
    return pl.BlockSpec(a.shape, lambda i, places: (0,) * len(a.shape))


def over_features(kernel, places, blocked, fixed, shapes, scratch, mib, flops, name):
    return pl.pallas_call(
        kernel,
        grid_spec=pltpu.PrefetchScalarGridSpec(
            num_scalar_prefetch=1,
            grid=(X_RING,),
            in_specs=[spec for _, spec in blocked] + [whole(a) for a in fixed],
            out_specs=[whole(a) for a in shapes],
            scratch_shapes=scratch,
        ),
        out_shape=shapes,
        compiler_params=params(mib, True),
        cost_estimate=pl.CostEstimate(
            flops=flops, bytes_accessed=8 * 2**20, transcendentals=10**6
        ),
        name=name,
    )(places, *[a for a, _ in blocked], *fixed)


def x_in_kernel(places, own_a, own_b, sib_a, sib_b, w_x, x_raw, acc):
    step = pl.program_id(0)
    toks_a, toks_b = step_tokens(places, (own_a, sib_a), (own_b, sib_b))
    rows = step_rows(places, w_x)
    add_to(acc.at[:A_ROWS], step, dot(toks_a, rows))
    add_to(acc.at[A_ROWS:], step, dot(toks_b, rows))

    @pl.when(step == pl.num_programs(0) - 1)
    def _():
        x_raw[...] = acc[...].astype(BF16)


def x_in(places, toks, w_x):
    shapes = [jax.ShapeDtypeStruct((ALL_ROWS, CH), BF16)]
    blocked = [(a, slot_blocks(a)) for a in toks]
    blocked += [(w_x, pl.BlockSpec((4 * FEAT, CH), lambda i, places: (places[i], 0)))]
    scratch = [pltpu.VMEM((ALL_ROWS, CH), F32)]
    flops = 2 * ALL_ROWS * 4096 * CH
    return over_features(x_in_kernel, places, blocked, [], shapes, scratch, 16, flops, "x_in")[0]


def scan_input_kernel(
    places,
    own_a,
    own_b,
    sib_a,
    sib_b,
    w_own,
    w_sib,
    x_raw,
    cols,
    taps_x,
    bias_x,
    taps_bc,
    bias_bc,
    dt_bias,
    decay,
    xc,
    bcc,
    hcol,
    hrow,
    s0,
    pay,
    acc_x,
    acc_bc,
    raw_bc,
):
    step = pl.program_id(0)
    core = my_core()
    toks_a, toks_b = step_tokens(places, (own_a, sib_a), (own_b, sib_b))
    w_cols = jnp.concatenate(
        [(w_own if same else w_sib)[chip] for chip, same in step_sources(places)], axis=1
    )
    add_to(acc_bc.at[:A_ROWS], step, dot_nt(toks_a, w_cols))
    add_to(acc_bc.at[A_ROWS:], step, dot_nt(toks_b, w_cols))

    @pl.when(step == 0)
    def _():
        acc_x[...] = x_raw[...].astype(F32)

    quarter = ROWS // X_RING
    for mine in range(X_RING):

        @pl.when(step == mine)
        def _():
            for at in range(mine * quarter, mine * quarter + quarter, 64):
                masks = cols[at : at + 64, :]
                xc[at : at + 64, :] = conv_chunk(acc_x, at, 64, masks, taps_x, bias_x[...])

    @pl.when(step == pl.num_programs(0) - 1)
    def _():
        raw_dt = acc_bc[HALO:, 2 * N : 2 * N + 2 * HEADS]
        raw_dt = jnp.where(core == 0, raw_dt[:, :HEADS], raw_dt[:, HEADS:])
        pre = raw_dt + dt_bias[...]
        dt = jnp.maximum(pre, 0.0) + jnp.log1p(jnp.exp(-jnp.abs(pre)))
        loga = -decay[...] * dt
        raw_bc[...] = acc_bc[:, : 2 * N].astype(BF16).astype(F32)
        for at in range(0, ROWS, 64):
            masks = cols[at : at + 64, :]
            bcc[at : at + 64, :] = conv_chunk(raw_bc, at, 64, masks, taps_bc, bias_bc[...])
        lower = (
            lax.broadcasted_iota(jnp.int32, (L, L), 0) >= lax.broadcasted_iota(jnp.int32, (L, L), 1)
        ).astype(F32)
        cum0 = jnp.dot(lower, loga[:L], precision=HIGHEST, preferred_element_type=F32)
        cum1 = jnp.dot(lower, loga[L:], precision=HIGHEST, preferred_element_type=F32)
        end0, end1 = cum0[L - 1 :], cum1[L - 1 :]
        slab = jnp.exp(jnp.concatenate([cum0, cum1 + end0], axis=0)) * cols[:, 3:4]
        inner = jnp.exp(cum1) * cols[L:, 5:6]
        tail0 = jnp.exp(end0 - cum0) * cols[:L, 6:7] * dt[:L]
        tail1 = jnp.exp(end1 - cum1) * cols[L:, 4:5] * dt[L:]
        cum = jnp.concatenate([cum0, cum1], axis=0)
        blank = jnp.zeros((ROWS, 128 - 4 * HEADS), F32)
        wide = jnp.concatenate(
            [cum, dt, slab, jnp.concatenate([inner, inner], axis=0), blank], axis=1
        )
        hcol[...] = wide
        hrow[...] = wide.T[: 2 * HEADS]
        scaled0 = (xc[:L, :].astype(F32) * spread(tail0)).astype(BF16)
        scaled1 = (xc[L:, :].astype(F32) * spread(tail1)).astype(BF16)
        state0 = dot_tn(bcc[:L, :N], scaled0)
        state1 = dot_tn(bcc[L:, :N], scaled1)
        s0[...] = state0.astype(BF16)
        ends = jnp.concatenate(
            [inner[L - 1 :], slab[ROWS - 1 :], jnp.zeros((6, HEADS), F32)], axis=0
        )
        ends = spread(ends)
        pay[:N, :] = (ends[0:1] * state0 + state1).astype(BF16)
        pay[N:, :] = factor_rows(ends[1:2])


def factor_rows(factor):
    high = factor.astype(BF16).astype(F32)
    row = lax.broadcasted_iota(jnp.int32, (16, CH), 0)
    return jnp.where(row == 0, high, jnp.where(row == 1, factor - high, 0.0)).astype(BF16)


def joined_states(refs):
    state, factor = None, None
    for ref in refs:
        tail = ref[N:, :].astype(F32)
        decay = tail[0:1] + tail[1:2]
        piece = ref[:N, :].astype(F32)
        state = piece if state is None else state + factor * piece
        factor = decay if factor is None else factor * decay
    return state, factor


def three_kernel(mine, one, two, out):
    state, factor = joined_states((mine, one, two))
    out[:N, :] = state.astype(BF16)
    out[N:, :] = factor_rows(factor)


def three(*args):
    return pl.pallas_call(
        three_kernel,
        in_specs=[VMEM] * 3,
        out_specs=VMEM,
        out_shape=jax.ShapeDtypeStruct((N + 16, CH), BF16),
        compiler_params=params(4),
        cost_estimate=pl.CostEstimate(flops=10**6, bytes_accessed=10**6, transcendentals=0),
        name="three",
    )(*args)


def scan_input(places, toks, w_own, w_sib, fixed):
    shapes = [
        jax.ShapeDtypeStruct((ROWS, CH), BF16),
        jax.ShapeDtypeStruct((ROWS, 2 * N), BF16),
        jax.ShapeDtypeStruct((ROWS, 128), F32),
        jax.ShapeDtypeStruct((2 * HEADS, ROWS), F32),
        jax.ShapeDtypeStruct((N, CH), BF16),
        jax.ShapeDtypeStruct((N + 16, CH), BF16),
    ]
    blocked = [(a, slot_blocks(a)) for a in toks]
    blocked += [(a, chip_blocks(a)) for a in (w_own, w_sib)]
    scratch = [
        pltpu.VMEM((ALL_ROWS, CH), F32),
        pltpu.VMEM((ALL_ROWS, 2 * N + 2 * HEADS), F32),
        pltpu.VMEM((ALL_ROWS, 2 * N), F32),
    ]
    flops = 2 * ALL_ROWS * 4096 * 272
    return over_features(
        scan_input_kernel, places, blocked, fixed, shapes, scratch, 20, flops, "scan_input"
    )


def gate_kernel(places, own_a, own_b, sib_a, sib_b, w_z, gates, acc):
    step = pl.program_id(0)
    toks_a, toks_b = step_tokens(places, (own_a, sib_a), (own_b, sib_b))
    rows = step_rows(places, w_z)
    add_to(acc.at[:A_ROWS], step, dot(toks_a, rows))
    add_to(acc.at[A_ROWS:], step, dot(toks_b, rows))

    @pl.when(step == pl.num_programs(0) - 1)
    def _():
        for at in range(0, ROWS, 64):
            z_raw = acc[HALO + at : HALO + at + 64, :].astype(BF16).astype(F32)
            gates[at : at + 64, :] = silu(z_raw)


def gate(places, toks, w_z):
    shapes = [jax.ShapeDtypeStruct((ROWS, CH), F32)]
    blocked = [(a, slot_blocks(a)) for a in toks]
    blocked += [(w_z, pl.BlockSpec((4 * FEAT, CH), lambda i, places: (places[i], 0)))]
    scratch = [pltpu.VMEM((ALL_ROWS, CH), F32)]
    flops = 2 * ALL_ROWS * 4096 * CH
    return over_features(gate_kernel, places, blocked, [], shapes, scratch, 16, flops, "gate")[0]


def intra_kernel(xc, bcc, hcol, hrow, s0, cols, seg_row, skip, y):
    for block in range(2):
        intra_block(block * L, xc, bcc, hcol, hrow, s0, cols, seg_row, skip, y)


def intra_block(at, xc, bcc, hcol, hrow, s0, cols, seg_row, skip, y):
    b_vals, c_vals = bcc[at : at + L, :N], bcc[at : at + L, N:]
    after = lax.broadcasted_iota(jnp.int32, (L, L), 0) >= lax.broadcasted_iota(
        jnp.int32, (L, L), 1
    )
    same = cols[at : at + L, 7:8] == seg_row[0:1, at : at + L]
    scores = jnp.where(after & same, dot_nt(c_vals, b_vals), 0.0)
    for half in range(2):
        lanes = slice(half * 256, half * 256 + 256)
        weights, values = [], []
        x_half = xc[at : at + L, lanes]
        head_of = lax.broadcasted_iota(jnp.int32, (1, 256), 1) // P_SIZE
        for part in range(4):
            head = half * 4 + part
            gap = hcol[at : at + L, head : head + 1] - hrow[head : head + 1, at : at + L]
            decay = jnp.exp(jnp.minimum(gap, 0.0))
            dt_row = hrow[HEADS + head : HEADS + head + 1, at : at + L]
            weights.append((scores * decay * dt_row).astype(BF16))
            values.append(x_half * (head_of == part).astype(BF16))
        out = dot(jnp.concatenate(weights, axis=1), jnp.concatenate(values, axis=0))
        out = out + skip[:, lanes] * x_half.astype(F32)
        if at:
            carried = spread(hcol[at : at + L, 3 * HEADS : 4 * HEADS], half * 4, 4)
            out = out + carried * dot(c_vals, s0[:, lanes])
        y[at : at + L, lanes] = out


def intra(*args):
    return pl.pallas_call(
        intra_kernel,
        in_specs=[VMEM] * len(args),
        out_specs=VMEM,
        out_shape=jax.ShapeDtypeStruct((ROWS, CH), F32),
        compiler_params=params(12),
        cost_estimate=pl.CostEstimate(
            flops=2 * ROWS * L * CH * 4, bytes_accessed=4 * 2**20, transcendentals=2 * 10**6
        ),
        name="intra",
    )(*args)


def join_kernel(y, gates, bcc, hcol, gain, one, four, seven, out, state):
    @pl.when(pl.program_id(0) == 0)
    def _():
        state[...] = joined_states((one, four, seven))[0].astype(BF16)

    rows = y.shape[0]
    carried = spread(hcol[:, 2 * HEADS : 3 * HEADS])
    total = y[...] + carried * dot(bcc[:, N:], state[...])
    gated = total * gates[...]
    square = jnp.sum(gated * gated, axis=1, keepdims=True)
    high = square.astype(BF16).astype(F32)
    lane = lax.broadcasted_iota(jnp.int32, (rows, 128), 1)
    out[:, :CH] = (gated * gain[...]).astype(BF16)
    out[:, CH:] = jnp.where(lane < 64, high, square - high).astype(BF16)


def join(y, gates, bcc, hcol, gain, pieces):
    rows = 128
    part = lambda a: pl.BlockSpec((rows, a.shape[1]), lambda i: (i, 0))
    all_of = lambda a: pl.BlockSpec(a.shape, lambda i: (0, 0))
    out = jax.ShapeDtypeStruct((ROWS, CH + 128), BF16)
    return pl.pallas_call(
        join_kernel,
        grid=(ROWS // rows,),
        in_specs=[part(a) for a in (y, gates, bcc, hcol)] + [all_of(a) for a in (gain, *pieces)],
        out_specs=part(out),
        out_shape=out,
        scratch_shapes=[pltpu.VMEM((N, CH), BF16)],
        compiler_params=params(10, True),
        cost_estimate=pl.CostEstimate(
            flops=2 * ROWS * N * CH, bytes_accessed=4 * 2**20, transcendentals=0
        ),
        name="join",
    )(y, gates, bcc, hcol, gain, *pieces)


def weight_copies(own_w, far_w, held, sems, blocks):
    y_low = lax.div(lax.axis_index("ctx"), Z_RING)

    def copy(ref, slot):
        x_place, y_place = blocks[slot]
        at = lax.rem(x_place, 2) * 4 + y_place * 2
        return pltpu.make_async_copy(ref.at[pl.ds(at, 2)], held.at[slot], sems.at[slot])

    for slot, (x_place, _) in enumerate(blocks):
        mine = lax.div(x_place, 2) == y_low

        @pl.when(mine)
        def _():
            copy(own_w, slot).start()

        @pl.when(jnp.logical_not(mine))
        def _():
            copy(far_w, slot).start()

    def ready(slot):
        copy(own_w, slot).wait()
        return column_block(held, slot)

    return ready


def column_block(held, slot):
    return jnp.concatenate([held[slot, 0], held[slot, 1]], axis=1)


def normed_rows(own, sib, rows):
    square = own[rows, CH:].astype(F32) + sib[rows, CH:].astype(F32)
    scale = lax.rsqrt((square[:, 0:1] + square[:, 64:65]) / (2.0 * CH) + NORM_EPS)
    return jnp.concatenate([own[rows, :CH], sib[rows, :CH]], axis=1), scale


def x_places():
    x_place = lax.div(lax.axis_index("tp"), 4)
    return [lax.rem(x_place + ahead, X_RING) for ahead in (0, 1, 3, 2)]


def my_y():
    return lax.rem(lax.div(lax.axis_index("tp"), CORES), 2)


def project_far_kernel(own, sib, own_w, far_w, b_sent, held, sems):
    blocks = [(x_place, 1 - my_y()) for x_place in x_places()]
    ready = weight_copies(own_w, far_w, held, sems, blocks)
    values, scale = normed_rows(own, sib, slice(ROWS // 2, ROWS))
    for n in range(X_RING):
        b_sent[:, 256 * n : 256 * n + 256] = (dot(values, ready(n)) * scale).astype(BF16)


def project_near_kernel(own, sib, own_w, far_w, *rest):
    outs, (held, sems) = rest[:5], rest[5:]
    blocks = []
    for x_place in x_places()[1:] + x_places()[:1]:
        blocks += [(x_place, my_y()), (x_place, 1 - my_y())]
    ready = weight_copies(own_w, far_w, held, sems, blocks)
    values, scale = normed_rows(own, sib, slice(0, ROWS // 2))
    low = my_y() == 0
    for n, out in enumerate(outs[:4]):
        near = dot(values, ready(2 * n)) * scale
        far = dot(values, ready(2 * n + 1)) * scale
        out[:, :256] = jnp.where(low, near, far).astype(out.dtype)
        out[:, 256:] = jnp.where(low, far, near).astype(out.dtype)
    values, scale = normed_rows(own, sib, slice(ROWS // 2, ROWS))
    for n, slot in enumerate((6, 0, 2, 4)):
        outs[4][:, 256 * n : 256 * n + 256] = dot(values, column_block(held, slot)) * scale


def project(kernel, own, sib, w_pieces, shapes, blocks, slots, name):
    return pl.pallas_call(
        kernel,
        in_specs=[VMEM] * 2 + [pl.BlockSpec(memory_space=pl.ANY)] * 2,
        out_specs=[VMEM] * len(shapes),
        out_shape=shapes,
        scratch_shapes=[
            pltpu.VMEM((slots, 2, 2 * CH, 128), BF16),
            pltpu.SemaphoreType.DMA((slots,)),
        ],
        compiler_params=params(16),
        cost_estimate=pl.CostEstimate(
            flops=2 * blocks * 256 * 256 * 2 * CH, bytes_accessed=5 * 2**20, transcendentals=0
        ),
        name=name,
    )(own, sib, *w_pieces)


def swapped(value, bit):
    return lax.ppermute(value, "tp", [(i, i ^ bit) for i in range(16)])


def along_x(value, steps):
    return lax.ppermute(value, "tp", [(i, (i + 4 * steps) % 16) for i in range(16)])


def next_ctx(value):
    return lax.ppermute(value, "ctx", [(i, i + 1) for i in range(15)])


def between_chips(value):
    same_core = [[2 * chip + core for chip in range(CHIPS)] for core in range(CORES)]
    return lax.all_to_all(value, "tp", 0, 0, axis_index_groups=same_core)


def together(*values):
    return lax.optimization_barrier(values)


def later_ctx(value, steps):
    return lax.ppermute(value, "ctx", [(i, i + steps) for i in range(16 - steps)])


def pick(core, first, second):
    return jnp.where(core == 0, first, second)


def local(
    tokens,
    seg_ids,
    w_x,
    w_z,
    w_bc,
    w_dt,
    conv_x,
    conv_x_bias,
    conv_bc,
    conv_bc_bias,
    dt_bias,
    decay_rate,
    skip_gain,
    norm_weight,
    w_out,
):
    rank = lax.axis_index("tp")
    core = rank % CORES
    chip = rank // CORES
    x_place = rank // 4
    y_place = chip % 2

    ring = jnp.stack([x_place, x_place + 3, x_place + 1, x_place + 2]) % X_RING
    places = jnp.concatenate([ring, y_place[None]]).astype(jnp.int32)
    w_cols = jnp.concatenate(
        [w_bc.T.reshape(CHIPS, 2 * N, FEAT), w_dt.T.reshape(CHIPS, 2 * HEADS, FEAT)], axis=1
    )
    taps_bc = lax.dynamic_slice_in_dim(conv_bc, chip * 2 * N, 2 * N, 1)
    bias_bc = lax.dynamic_slice_in_dim(conv_bc_bias, chip * 2 * N, 2 * N, 0)[None]
    skip = jnp.repeat(skip_gain, P_SIZE)[None]
    small = [conv_x, conv_x_bias[None], taps_bc, bias_bc, dt_bias[None], decay_rate[None]]
    halves = (w_out[:, :128], w_out[:, 128:])
    w_given, w_kept = pick(core, halves[1], halves[0]), pick(core, *halves)

    ids_row = jnp.pad((seg_ids[-3:] + 1).astype(BF16), (0, FEAT - 3))[None]
    halo = next_ctx(jnp.concatenate([ids_row, tokens[1 - HALO :]], axis=0))
    b_rows = tokens[B_ROWS:]
    b_near = [b_rows] + [along_x(b_rows, ahead) for ahead in (1, -1, 2)]
    a_rows = jnp.concatenate([halo, tokens[:B_ROWS]], axis=0)
    ids_prior = halo[0, :3].astype(jnp.int32) - 1
    a_far = swapped(a_rows, 2)
    w_pair = jnp.concatenate([w_kept, swapped(w_given, 1)], axis=0)
    same_y = [list(range(Z_RING)), list(range(Z_RING, 2 * Z_RING))]
    w_near = lax.all_to_all(
        jnp.broadcast_to(w_pair[None], (Z_RING,) + w_pair.shape),
        "ctx",
        0,
        0,
        axis_index_groups=same_y,
    )
    b_near, a_near = together(b_near, [a_rows, a_far])

    a_near, b_near = jnp.stack(a_near), jnp.stack(b_near)
    a_left, a_right, b_far = along_x(a_near, 1), along_x(a_near, -1), swapped(b_near, 2)
    early = document_columns(seg_ids, ids_prior) + (places, skip, small, w_cols)
    (a_left, a_right, b_far), early = together((a_left, a_right, b_far), early)
    cols, seg_row, places, skip, small, w_cols = early

    a_last = (along_x(a_left[0], 1), along_x(a_right[1], -1))
    a_last, w_cols = together(a_last, w_cols)
    own_a = jnp.concatenate([a_near, a_left, a_right, jnp.stack(a_last)], axis=0)
    own_b = jnp.stack([b_near, b_far], axis=1).reshape(CHIPS, B_ROWS, FEAT)
    w_own = between_chips(w_cols)
    toks = (own_a, own_b, swapped(own_a, 1), swapped(own_b, 1))
    x_raw = x_in(places, toks, w_x)
    w_own, x_raw = together(w_own, x_raw)
    xc, bcc, hcol, hrow, s0, pay = scan_input(
        places, toks, w_own, swapped(w_own, 1), [x_raw, cols] + small
    )

    pay, toks, w_near = together(pay, toks, w_near)
    one, two = later_ctx(pay, 1), later_ctx(pay, 2)
    w_far = lax.ppermute(w_near, "ctx", [(i, i ^ Z_RING) for i in range(2 * Z_RING)])
    gates = gate(places, toks, w_z)
    one, two, gates = together(one, two, gates)
    held = three(pay, one, two)
    held, xc, bcc, hcol = together(held, xc, bcc, hcol)
    pieces = [later_ctx(held, steps) for steps in (1, 4, 7)]
    y = intra(xc, bcc, hcol, hrow, s0, cols, seg_row, skip)
    y, pieces = together(y, pieces)
    mine = join(y, gates, bcc, hcol, norm_weight[None], pieces)
    other = swapped(mine, 1)
    return summed_outputs(mine, other, (w_near, w_far), y_place, core)


def document_columns(seg_ids, ids_prior):
    ids_all = jnp.concatenate([ids_prior, seg_ids])
    prior = ids_prior[2]
    same = lambda a: (seg_ids == a).astype(F32)
    columns = [same(ids_all[tap : tap + ROWS]) for tap in range(CONV - 1)]
    columns += [same(prior), same(seg_ids[-1]), same(seg_ids[L - 1]), same(seg_ids[L - 1])]
    columns += [seg_ids.astype(F32)]
    cols = jnp.pad(jnp.stack(columns, axis=1), ((0, 0), (0, 128 - len(columns))))
    return cols, jnp.broadcast_to(seg_ids.astype(F32)[None], (8, ROWS))


def summed_outputs(mine, other, w_pieces, y_place, core):
    half = ROWS // 2
    shape = lambda lanes, dtype: jax.ShapeDtypeStruct((half, lanes), dtype)
    (b_sent,) = project(
        project_far_kernel, mine, other, w_pieces, [shape(1024, BF16)], 4, 4, "project_far"
    )
    b_sent, other = together(b_sent, other)
    b_far = swapped(b_sent, 2)
    shapes = [shape(512, BF16)] * 3 + [shape(512, F32), shape(1024, F32)]
    *a_sent, a_kept, b_kept = project(
        project_near_kernel, mine, other, w_pieces, shapes, 12, 8, "project_near"
    )
    steps = (1, -1, 2)
    a_got = [along_x(part, ahead) for part, ahead in zip(a_sent, steps)]
    b_sum = b_kept + b_far.astype(F32)
    b_parts = [b_sum[:, 256 * n : 256 * n + 256] for n in range(4)]
    b_got = [along_x(part.astype(BF16), ahead) for part, ahead in zip(b_parts[1:], steps)]
    a_sum = a_kept + sum(part.astype(F32) for part in a_got)
    halves = (a_sum[:, :256], a_sum[:, 256:])
    a_far = swapped(pick(y_place, halves[1], halves[0]).astype(BF16), 2)
    a_sum = pick(y_place, *halves) + a_far.astype(F32)
    b_sum = b_parts[0] + sum(part.astype(F32) for part in b_got)
    total = jnp.concatenate([a_sum, b_sum], axis=0).astype(BF16)
    parts = (total[:, :128], total[:, 128:])
    kept = pick(core, *parts)
    given = swapped(pick(core, parts[1], parts[0]), 1)
    return jnp.concatenate([pick(core, kept, given), pick(core, given, kept)], axis=1)


def solution(mesh):
    return jax.shard_map(
        local,
        mesh=mesh,
        in_specs=(
            P("ctx", "tp"),
            P("ctx"),
            P(None, "tp"),
            P(None, "tp"),
            P("tp", None),
            P("tp", None),
            P(None, "tp"),
            P("tp"),
            P(),
            P(),
            P("tp"),
            P("tp"),
            P("tp"),
            P("tp"),
            P("tp", "ctx"),
        ),
        out_specs=P("ctx", "tp"),
        check_vma=False,
    )
```

```python
import functools

import jax
import jax.numpy as jnp
from jax import lax
from jax.experimental import pallas as pl
from jax.experimental.pallas import tpu as pltpu
from jax.sharding import PartitionSpec as P

H = 128
P_SIZE = 64
N = 128
G = 8
L = 256
CONV = 4
HALO = 16
NORM_EPS = 1e-05
HIGHEST = lax.Precision.HIGHEST

CHIPS = 8
CORES = 2
HEADS = 8
CH = HEADS * P_SIZE
ROWS = 512
FEAT = 256
X_RING = 4
Z_RING = 8
A_ROWS = 272
B_ROWS = 256
ALL_ROWS = A_ROWS + B_ROWS
VMEM = pl.BlockSpec(memory_space=pltpu.VMEM)
BF16 = jnp.bfloat16
F32 = jnp.float32


def params(mib, grid=False):
    more = {"dimension_semantics": ("arbitrary",)} if grid else {}
    return pltpu.CompilerParams(vmem_limit_bytes=mib * 2**20, **more)


def dot(a, b):
    return jnp.dot(a, b, preferred_element_type=F32)


def dot_nt(a, b):
    return lax.dot_general(a, b, (((1,), (1,)), ((), ())), preferred_element_type=F32)


def dot_tn(a, b):
    return lax.dot_general(a, b, (((0,), (0,)), ((), ())), preferred_element_type=F32)


def silu(v):
    return v / (1.0 + jnp.exp(-v))


def spread(cols, first=0, count=HEADS):
    shape = (HEADS, count * P_SIZE)
    head = lax.broadcasted_iota(jnp.int32, shape, 0)
    lane = lax.broadcasted_iota(jnp.int32, shape, 1)
    pick = (head == lane // P_SIZE + first).astype(F32)
    return jnp.dot(cols, pick, precision=HIGHEST, preferred_element_type=F32)


def my_core():
    return lax.rem(lax.axis_index("tp"), CORES)


def add_to(acc, step, value):
    @pl.when(step == 0)
    def _():
        acc[...] = value

    @pl.when(step > 0)
    def _():
        acc[...] += value


def conv_chunk(raw, at, rows, masks, taps, offsets):
    total = offsets + taps[CONV - 1 : CONV, :] * raw[at + HALO : at + HALO + rows, :]
    for tap in range(CONV - 1):
        first = at + HALO - (CONV - 1) + tap
        shifted = raw[first : first + rows, :]
        total = total + taps[tap : tap + 1, :] * (shifted * masks[:, tap : tap + 1])
    return silu(total).astype(BF16)


def rounded(ref):
    ref[...] = ref[...].astype(BF16).astype(F32)


def step_tokens(places, first, last):
    joined = []
    for own, sib in (first, last):
        parts = [ref[slot] for slot in range(2) for ref in (own, sib)]
        joined.append(jnp.concatenate(parts, axis=1))
    return joined


def step_sources(places):
    for slot in range(2):
        chip = lax.rem(places[X_RING] + slot, 2)
        for same_core in (True, False):
            yield chip, same_core


def step_rows(places, w_ref):
    core = my_core()
    parts = []
    for chip, same_core in step_sources(places):
        from_core = core if same_core else 1 - core
        at = pl.multiple_of((chip * CORES + from_core) * FEAT, FEAT)
        parts.append(w_ref[pl.ds(at, FEAT), :])
    return jnp.concatenate(parts, axis=0)


def slot_blocks(a):
    return pl.BlockSpec((2,) + a.shape[1:], lambda i, places: (i, 0, 0))


def whole(a):
    return pl.BlockSpec(a.shape, lambda i, places: (0,) * len(a.shape))


def over_features(kernel, places, blocked, fixed, shapes, scratch, mib, flops, name):
    return pl.pallas_call(
        kernel,
        grid_spec=pltpu.PrefetchScalarGridSpec(
            num_scalar_prefetch=1,
            grid=(X_RING,),
            in_specs=[spec for _, spec in blocked] + [whole(a) for a in fixed],
            out_specs=[whole(a) for a in shapes],
            scratch_shapes=scratch,
        ),
        out_shape=shapes,
        compiler_params=params(mib, True),
        cost_estimate=pl.CostEstimate(
            flops=flops, bytes_accessed=8 * 2**20, transcendentals=10**6
        ),
        name=name,
    )(places, *[a for a, _ in blocked], *fixed)


def x_in_kernel(places, own_a, own_b, sib_a, sib_b, w_x, x_raw, acc):
    step = pl.program_id(0)
    toks_a, toks_b = step_tokens(places, (own_a, sib_a), (own_b, sib_b))
    rows = step_rows(places, w_x)
    add_to(acc.at[:A_ROWS], step, dot(toks_a, rows))
    add_to(acc.at[A_ROWS:], step, dot(toks_b, rows))

    @pl.when(step == pl.num_programs(0) - 1)
    def _():
        x_raw[...] = acc[...].astype(BF16)


def x_in(places, toks, w_x):
    shapes = [jax.ShapeDtypeStruct((ALL_ROWS, CH), BF16)]
    blocked = [(a, slot_blocks(a)) for a in toks]
    blocked += [(w_x, pl.BlockSpec((4 * FEAT, CH), lambda i, places: (places[i], 0)))]
    scratch = [pltpu.VMEM((ALL_ROWS, CH), F32)]
    flops = 2 * ALL_ROWS * 4096 * CH
    return over_features(x_in_kernel, places, blocked, [], shapes, scratch, 16, flops, "x_in")[0]


def scan_input_kernel(
    places,
    own_a,
    own_b,
    sib_a,
    sib_b,
    w_own,
    w_sib,
    x_raw,
    cols,
    taps_x,
    bias_x,
    taps_bc,
    bias_bc,
    dt_bias,
    decay,
    xc,
    bcc,
    hcol,
    hrow,
    s0,
    pay,
    acc_x,
    acc_bc,
    raw_bc,
):
    step = pl.program_id(0)
    core = my_core()
    toks_a, toks_b = step_tokens(places, (own_a, sib_a), (own_b, sib_b))
    w_cols = jnp.concatenate([ref[slot] for slot in range(2) for ref in (w_own, w_sib)], axis=1)
    add_to(acc_bc.at[:A_ROWS], step, dot_nt(toks_a, w_cols))
    add_to(acc_bc.at[A_ROWS:], step, dot_nt(toks_b, w_cols))

    @pl.when(step == 0)
    def _():
        acc_x[...] = x_raw[...].astype(F32)

    quarter = ROWS // X_RING
    for mine in range(X_RING):

        @pl.when(step == mine)
        def _():
            for at in range(mine * quarter, mine * quarter + quarter, 64):
                masks = cols[at : at + 64, :]
                xc[at : at + 64, :] = conv_chunk(acc_x, at, 64, masks, taps_x, bias_x[...])

    @pl.when(step == pl.num_programs(0) - 1)
    def _():
        raw_dt = acc_bc[HALO:, 2 * N : 2 * N + 2 * HEADS]
        raw_dt = jnp.where(core == 0, raw_dt[:, :HEADS], raw_dt[:, HEADS:])
        pre = raw_dt + dt_bias[...]
        dt = jnp.maximum(pre, 0.0) + jnp.log1p(jnp.exp(-jnp.abs(pre)))
        loga = -decay[...] * dt
        raw_bc[...] = acc_bc[:, : 2 * N].astype(BF16).astype(F32)
        for at in range(0, ROWS, 64):
            masks = cols[at : at + 64, :]
            bcc[at : at + 64, :] = conv_chunk(raw_bc, at, 64, masks, taps_bc, bias_bc[...])
        lower = (
            lax.broadcasted_iota(jnp.int32, (L, L), 0) >= lax.broadcasted_iota(jnp.int32, (L, L), 1)
        ).astype(F32)
        cum0 = jnp.dot(lower, loga[:L], precision=HIGHEST, preferred_element_type=F32)
        cum1 = jnp.dot(lower, loga[L:], precision=HIGHEST, preferred_element_type=F32)
        end0, end1 = cum0[L - 1 :], cum1[L - 1 :]
        slab = jnp.exp(jnp.concatenate([cum0, cum1 + end0], axis=0)) * cols[:, 3:4]
        inner = jnp.exp(cum1) * cols[L:, 5:6]
        tail0 = jnp.exp(end0 - cum0) * cols[:L, 6:7] * dt[:L]
        tail1 = jnp.exp(end1 - cum1) * cols[L:, 4:5] * dt[L:]
        cum = jnp.concatenate([cum0, cum1], axis=0)
        blank = jnp.zeros((ROWS, 128 - 4 * HEADS), F32)
        wide = jnp.concatenate(
            [cum, dt, slab, jnp.concatenate([inner, inner], axis=0), blank], axis=1
        )
        hcol[...] = wide
        hrow[...] = wide.T[: 2 * HEADS]
        scaled0 = (xc[:L, :].astype(F32) * spread(tail0)).astype(BF16)
        scaled1 = (xc[L:, :].astype(F32) * spread(tail1)).astype(BF16)
        state0 = dot_tn(bcc[:L, :N], scaled0)
        state1 = dot_tn(bcc[L:, :N], scaled1)
        s0[...] = state0.astype(BF16)
        ends = jnp.concatenate(
            [inner[L - 1 :], slab[ROWS - 1 :], jnp.zeros((6, HEADS), F32)], axis=0
        )
        ends = spread(ends)
        pay[:N, :] = (ends[0:1] * state0 + state1).astype(BF16)
        pay[N:, :] = factor_rows(ends[1:2])


def factor_rows(factor):
    high = factor.astype(BF16).astype(F32)
    row = lax.broadcasted_iota(jnp.int32, (16, CH), 0)
    return jnp.where(row == 0, high, jnp.where(row == 1, factor - high, 0.0)).astype(BF16)


def joined_states(refs):
    state, factor = None, None
    for ref in refs:
        tail = ref[N:, :].astype(F32)
        decay = tail[0:1] + tail[1:2]
        piece = ref[:N, :].astype(F32)
        state = piece if state is None else state + factor * piece
        factor = decay if factor is None else factor * decay
    return state, factor


def three_kernel(mine, one, two, out):
    state, factor = joined_states((mine, one, two))
    out[:N, :] = state.astype(BF16)
    out[N:, :] = factor_rows(factor)


def three(*args):
    return pl.pallas_call(
        three_kernel,
        in_specs=[VMEM] * 3,
        out_specs=VMEM,
        out_shape=jax.ShapeDtypeStruct((N + 16, CH), BF16),
        compiler_params=params(4),
        cost_estimate=pl.CostEstimate(flops=10**6, bytes_accessed=10**6, transcendentals=0),
        name="three",
    )(*args)


def scan_input(places, toks, w_own, w_sib, fixed):
    shapes = [
        jax.ShapeDtypeStruct((ROWS, CH), BF16),
        jax.ShapeDtypeStruct((ROWS, 2 * N), BF16),
        jax.ShapeDtypeStruct((ROWS, 128), F32),
        jax.ShapeDtypeStruct((2 * HEADS, ROWS), F32),
        jax.ShapeDtypeStruct((N, CH), BF16),
        jax.ShapeDtypeStruct((N + 16, CH), BF16),
    ]
    blocked = [(a, slot_blocks(a)) for a in toks]
    blocked += [(a, slot_blocks(a)) for a in (w_own, w_sib)]
    scratch = [
        pltpu.VMEM((ALL_ROWS, CH), F32),
        pltpu.VMEM((ALL_ROWS, 2 * N + 2 * HEADS), F32),
        pltpu.VMEM((ALL_ROWS, 2 * N), F32),
    ]
    flops = 2 * ALL_ROWS * 4096 * 272
    return over_features(
        scan_input_kernel, places, blocked, fixed, shapes, scratch, 20, flops, "scan_input"
    )


def gate_kernel(places, own_a, own_b, sib_a, sib_b, w_z, gates, acc):
    step = pl.program_id(0)
    toks_a, toks_b = step_tokens(places, (own_a, sib_a), (own_b, sib_b))
    rows = step_rows(places, w_z)
    add_to(acc.at[:A_ROWS], step, dot(toks_a, rows))
    add_to(acc.at[A_ROWS:], step, dot(toks_b, rows))

    @pl.when(step == pl.num_programs(0) - 1)
    def _():
        for at in range(0, ROWS, 64):
            z_raw = acc[HALO + at : HALO + at + 64, :].astype(BF16).astype(F32)
            gates[at : at + 64, :] = silu(z_raw)


def gate(places, toks, w_z):
    shapes = [jax.ShapeDtypeStruct((ROWS, CH), F32)]
    blocked = [(a, slot_blocks(a)) for a in toks]
    blocked += [(w_z, pl.BlockSpec((4 * FEAT, CH), lambda i, places: (places[i], 0)))]
    scratch = [pltpu.VMEM((ALL_ROWS, CH), F32)]
    flops = 2 * ALL_ROWS * 4096 * CH
    return over_features(gate_kernel, places, blocked, [], shapes, scratch, 16, flops, "gate")[0]


def intra_kernel(xc, bcc, hcol, hrow, s0, cols, seg_row, skip, y):
    for block in range(2):
        intra_block(block * L, xc, bcc, hcol, hrow, s0, cols, seg_row, skip, y)


def intra_block(at, xc, bcc, hcol, hrow, s0, cols, seg_row, skip, y):
    b_vals, c_vals = bcc[at : at + L, :N], bcc[at : at + L, N:]
    after = lax.broadcasted_iota(jnp.int32, (L, L), 0) >= lax.broadcasted_iota(
        jnp.int32, (L, L), 1
    )
    same = cols[at : at + L, 7:8] == seg_row[0:1, at : at + L]
    scores = jnp.where(after & same, dot_nt(c_vals, b_vals), 0.0)
    for half in range(2):
        lanes = slice(half * 256, half * 256 + 256)
        weights, values = [], []
        x_half = xc[at : at + L, lanes]
        head_of = lax.broadcasted_iota(jnp.int32, (1, 256), 1) // P_SIZE
        for part in range(4):
            head = half * 4 + part
            gap = hcol[at : at + L, head : head + 1] - hrow[head : head + 1, at : at + L]
            decay = jnp.exp(jnp.minimum(gap, 0.0))
            dt_row = hrow[HEADS + head : HEADS + head + 1, at : at + L]
            weights.append((scores * decay * dt_row).astype(BF16))
            values.append(x_half * (head_of == part).astype(BF16))
        out = dot(jnp.concatenate(weights, axis=1), jnp.concatenate(values, axis=0))
        out = out + skip[:, lanes] * x_half.astype(F32)
        if at:
            carried = spread(hcol[at : at + L, 3 * HEADS : 4 * HEADS], half * 4, 4)
            out = out + carried * dot(c_vals, s0[:, lanes])
        y[at : at + L, lanes] = out


def intra(*args):
    return pl.pallas_call(
        intra_kernel,
        in_specs=[VMEM] * len(args),
        out_specs=VMEM,
        out_shape=jax.ShapeDtypeStruct((ROWS, CH), F32),
        compiler_params=params(12),
        cost_estimate=pl.CostEstimate(
            flops=2 * ROWS * L * CH * 4, bytes_accessed=4 * 2**20, transcendentals=2 * 10**6
        ),
        name="intra",
    )(*args)


def join_kernel(y, gates, bcc, hcol, gain, one, four, seven, out, state):
    @pl.when(pl.program_id(0) == 0)
    def _():
        state[...] = joined_states((one, four, seven))[0].astype(BF16)

    rows = y.shape[0]
    carried = spread(hcol[:, 2 * HEADS : 3 * HEADS])
    total = y[...] + carried * dot(bcc[:, N:], state[...])
    gated = total * gates[...]
    square = jnp.sum(gated * gated, axis=1, keepdims=True)
    high = square.astype(BF16).astype(F32)
    lane = lax.broadcasted_iota(jnp.int32, (rows, 128), 1)
    out[:, :CH] = (gated * gain[...]).astype(BF16)
    out[:, CH:] = jnp.where(lane < 64, high, square - high).astype(BF16)


def join(y, gates, bcc, hcol, gain, pieces):
    rows = 128
    part = lambda a: pl.BlockSpec((rows, a.shape[1]), lambda i: (i, 0))
    all_of = lambda a: pl.BlockSpec(a.shape, lambda i: (0, 0))
    out = jax.ShapeDtypeStruct((ROWS, CH + 128), BF16)
    return pl.pallas_call(
        join_kernel,
        grid=(ROWS // rows,),
        in_specs=[part(a) for a in (y, gates, bcc, hcol)] + [all_of(a) for a in (gain, *pieces)],
        out_specs=part(out),
        out_shape=out,
        scratch_shapes=[pltpu.VMEM((N, CH), BF16)],
        compiler_params=params(10, True),
        cost_estimate=pl.CostEstimate(
            flops=2 * ROWS * N * CH, bytes_accessed=4 * 2**20, transcendentals=0
        ),
        name="join",
    )(y, gates, bcc, hcol, gain, *pieces)


def weight_copies(w_all, held, sems, blocks):
    y_low = lax.div(lax.axis_index("ctx"), Z_RING)

    def copy(slot):
        x_place, y_place = blocks[slot]
        at = lax.rem(x_place, 2) * 4 + y_place * 2
        row = pl.multiple_of(lax.rem(lax.div(x_place, 2) + y_low, 2) * 2 * CH, 2 * CH)
        part = w_all.at[pl.ds(at, 2), pl.ds(row, 2 * CH), :]
        return pltpu.make_async_copy(part, held.at[slot], sems.at[slot])

    for slot in range(len(blocks)):
        copy(slot).start()

    def ready(slot):
        copy(slot).wait()
        return column_block(held, slot)

    return ready


def column_block(held, slot):
    return jnp.concatenate([held[slot, 0], held[slot, 1]], axis=1)


def normed_rows(own, sib, rows):
    square = own[rows, CH:].astype(F32) + sib[rows, CH:].astype(F32)
    scale = lax.rsqrt((square[:, 0:1] + square[:, 64:65]) / (2.0 * CH) + NORM_EPS)
    return jnp.concatenate([own[rows, :CH], sib[rows, :CH]], axis=1), scale


def x_places():
    x_place = lax.div(lax.axis_index("tp"), 4)
    return [lax.rem(x_place + ahead, X_RING) for ahead in (0, 1, 3, 2)]


def my_y():
    return lax.rem(lax.div(lax.axis_index("tp"), CORES), 2)


def project_far_kernel(own, sib, w_all, b_sent, held, sems):
    blocks = [(x_place, 1 - my_y()) for x_place in x_places()]
    ready = weight_copies(w_all, held, sems, blocks)
    values, scale = normed_rows(own, sib, slice(ROWS // 2, ROWS))
    for n in range(X_RING):
        b_sent[:, 256 * n : 256 * n + 256] = (dot(values, ready(n)) * scale).astype(BF16)


def project_a_kernel(own, sib, w_all, *rest):
    outs, (held, sems) = rest[:4], rest[4:]
    blocks = []
    for x_place in x_places()[1:] + x_places()[:1]:
        blocks += [(x_place, 0), (x_place, 1)]
    ready = weight_copies(w_all, held, sems, blocks)
    values, scale = normed_rows(own, sib, slice(0, ROWS // 2))
    for n, out in enumerate(outs):
        for side in range(2):
            part = dot(values, ready(2 * n + side)) * scale
            out[:, 256 * side : 256 * side + 256] = part.astype(out.dtype)


def project_b_kernel(own, sib, w_all, b_far, *rest):
    outs, (held, sems) = rest[:4], rest[4:]
    blocks = [(x_place, my_y()) for x_place in x_places()]
    ready = weight_copies(w_all, held, sems, blocks)
    values, scale = normed_rows(own, sib, slice(ROWS // 2, ROWS))
    for n in (1, 2, 3, 0):
        part = dot(values, ready(n)) * scale
        part = part + b_far[:, 256 * n : 256 * n + 256].astype(F32)
        outs[n][...] = part.astype(outs[n].dtype)


def project(kernel, own, sib, w_all, more, shapes, blocks, slots, name):
    return pl.pallas_call(
        kernel,
        in_specs=[VMEM] * 2 + [pl.BlockSpec(memory_space=pl.ANY)] + [VMEM] * len(more),
        out_specs=[VMEM] * len(shapes),
        out_shape=shapes,
        scratch_shapes=[
            pltpu.VMEM((slots, 2, 2 * CH, 128), BF16),
            pltpu.SemaphoreType.DMA((slots,)),
        ],
        compiler_params=params(58),
        cost_estimate=pl.CostEstimate(
            flops=2 * blocks * 256 * 256 * 2 * CH, bytes_accessed=5 * 2**20, transcendentals=0
        ),
        name=name,
    )(own, sib, w_all, *more)


def swapped(value, bit):
    return lax.ppermute(value, "tp", [(i, i ^ bit) for i in range(16)])


def along_x(value, steps):
    return lax.ppermute(value, "tp", [(i, (i + 4 * steps) % 16) for i in range(16)])


def next_ctx(value):
    return lax.ppermute(value, "ctx", [(i, i + 1) for i in range(15)])


def together(*values):
    return lax.optimization_barrier(values)


def later_ctx(value, steps):
    return lax.ppermute(value, "ctx", [(i, i + steps) for i in range(16 - steps)])


def pick(core, first, second):
    return jnp.where(core == 0, first, second)


def local(
    tokens,
    seg_ids,
    w_x,
    w_z,
    w_bc,
    w_dt,
    conv_x,
    conv_x_bias,
    conv_bc,
    conv_bc_bias,
    dt_bias,
    decay_rate,
    skip_gain,
    norm_weight,
    w_out,
):
    rank = lax.axis_index("tp")
    core = rank % CORES
    chip = rank // CORES
    x_place = rank // 4
    y_place = chip % 2

    ring = jnp.stack([x_place, x_place + 3, x_place + 1, x_place + 2]) % X_RING
    places = jnp.concatenate([ring, y_place[None]]).astype(jnp.int32)
    w_cols = jnp.concatenate(
        [w_bc.T.reshape(CHIPS, 2 * N, FEAT), w_dt.T.reshape(CHIPS, 2 * HEADS, FEAT)], axis=1
    )
    x_ahead = [(x_place + ahead) % X_RING for ahead in (0, 1, 3, 2)]
    cols_for = lambda side: [
        lax.dynamic_index_in_dim(w_cols, 2 * place + side, 0, False) for place in x_ahead
    ]
    w_given_cols, w_kept_cols = jnp.stack(cols_for(1 - y_place)), jnp.stack(cols_for(y_place))
    taps_bc = lax.dynamic_slice_in_dim(conv_bc, chip * 2 * N, 2 * N, 1)
    bias_bc = lax.dynamic_slice_in_dim(conv_bc_bias, chip * 2 * N, 2 * N, 0)[None]
    skip = jnp.repeat(skip_gain, P_SIZE)[None]
    small = [conv_x, conv_x_bias[None], taps_bc, bias_bc, dt_bias[None], decay_rate[None]]
    halves = (w_out[:, :128], w_out[:, 128:])
    w_given, w_kept = pick(core, halves[1], halves[0]), pick(core, *halves)

    ids_row = jnp.pad((seg_ids[-3:] + 1).astype(BF16), (0, FEAT - 3))[None]
    halo = next_ctx(jnp.concatenate([ids_row, tokens[1 - HALO :]], axis=0))
    b_rows = tokens[B_ROWS:]
    b_near = [b_rows] + [along_x(b_rows, ahead) for ahead in (1, -1, 2)]
    a_rows = jnp.concatenate([halo, tokens[:B_ROWS]], axis=0)
    ids_prior = halo[0, :3].astype(jnp.int32) - 1
    a_far = swapped(a_rows, 2)
    w_pair = jnp.concatenate([w_kept, swapped(w_given, 1)], axis=0)
    w_far_cols = swapped(w_given_cols, 2)
    b_near, a_near, w_far_cols = together(b_near, [a_rows, a_far], w_far_cols)

    a_near, b_near = jnp.stack(a_near), jnp.stack(b_near)
    a_left, a_right, b_far = along_x(a_near, 1), along_x(a_near, -1), swapped(b_near, 2)
    early = document_columns(seg_ids, ids_prior) + (places, skip, small, w_kept_cols, w_pair)
    (a_left, a_right, b_far), early = together((a_left, a_right, b_far), early)
    cols, seg_row, places, skip, small, w_kept_cols, w_pair = early

    a_last = (along_x(a_left[0], 1), along_x(a_right[1], -1))
    w_far = lax.ppermute(w_pair, "ctx", [(i, i ^ Z_RING) for i in range(2 * Z_RING)])
    a_last, w_both = together(a_last, [w_pair, w_far])
    same_y = [list(range(Z_RING)), list(range(Z_RING, 2 * Z_RING))]
    w_all = lax.all_gather(
        jnp.concatenate(w_both, axis=0), "ctx", axis=0, axis_index_groups=same_y
    )
    own_a = jnp.concatenate([a_near, a_left, a_right, jnp.stack(a_last)], axis=0)
    own_b = jnp.stack([b_near, b_far], axis=1).reshape(CHIPS, B_ROWS, FEAT)
    toks = (own_a, own_b, swapped(own_a, 1), swapped(own_b, 1))
    toks, w_kept_cols, w_far_cols = together(toks, w_kept_cols, w_far_cols)
    w_pairs = [jnp.stack(pair) for pair in zip(w_kept_cols, w_far_cols)]
    w_moved = [along_x(pair, ahead) for pair, ahead in zip(w_pairs[1:], (1, -1, 2))]
    x_raw = x_in(places, toks, w_x)
    gates = gate(places, toks, w_z)
    w_moved, x_raw, gates = together(w_moved, x_raw, gates)
    w_own = jnp.concatenate([w_pairs[0]] + list(w_moved), axis=0)
    xc, bcc, hcol, hrow, s0, pay = scan_input(
        places, toks, w_own, swapped(w_own, 1), [x_raw, cols] + small
    )
    one, two = later_ctx(pay, 1), later_ctx(pay, 2)
    held = three(pay, one, two)
    held, xc, bcc, hcol = together(held, xc, bcc, hcol)
    pieces = [later_ctx(held, steps) for steps in (1, 4, 7)]
    y = intra(xc, bcc, hcol, hrow, s0, cols, seg_row, skip)
    y, pieces = together(y, pieces)
    mine = join(y, gates, bcc, hcol, norm_weight[None], pieces)
    other = swapped(mine, 1)
    return summed_outputs(mine, other, w_all, y_place, core)


def document_columns(seg_ids, ids_prior):
    ids_all = jnp.concatenate([ids_prior, seg_ids])
    prior = ids_prior[2]
    same = lambda a: (seg_ids == a).astype(F32)
    columns = [same(ids_all[tap : tap + ROWS]) for tap in range(CONV - 1)]
    columns += [same(prior), same(seg_ids[-1]), same(seg_ids[L - 1]), same(seg_ids[L - 1])]
    columns += [seg_ids.astype(F32)]
    cols = jnp.pad(jnp.stack(columns, axis=1), ((0, 0), (0, 128 - len(columns))))
    return cols, jnp.broadcast_to(seg_ids.astype(F32)[None], (8, ROWS))


def summed_outputs(mine, other, w_all, y_place, core):
    shape = lambda lanes, dtype: jax.ShapeDtypeStruct((ROWS // 2, lanes), dtype)
    steps = (1, -1, 2)
    (b_sent,) = project(
        project_far_kernel, mine, other, w_all, [], [shape(1024, BF16)], 4, 4, "project_far"
    )
    b_sent, mine, other = together(b_sent, mine, other)
    b_far = swapped(b_sent, 2)
    shapes = [shape(512, BF16)] * 3 + [shape(512, F32)]
    *a_sent, a_kept = project(
        project_a_kernel, mine, other, w_all, [], shapes, 8, 8, "project_a"
    )
    a_got = [along_x(part, ahead) for part, ahead in zip(a_sent, steps)]
    b_far, a_kept = together(b_far, a_kept)
    shapes = [shape(256, F32)] + [shape(256, BF16)] * 3
    b_kept, *b_sent = project(
        project_b_kernel, mine, other, w_all, [b_far], shapes, 4, 4, "project_b"
    )
    b_got = [along_x(part, ahead) for part, ahead in zip(b_sent, steps)]
    a_sum = a_kept + sum(part.astype(F32) for part in a_got)
    halves = (a_sum[:, :256], a_sum[:, 256:])
    a_far = swapped(pick(y_place, halves[1], halves[0]).astype(BF16), 2)
    a_sum = pick(y_place, *halves) + a_far.astype(F32)
    b_sum = b_kept + sum(part.astype(F32) for part in b_got)
    total = jnp.concatenate([a_sum, b_sum], axis=0).astype(BF16)
    parts = (total[:, :128], total[:, 128:])
    kept = pick(core, *parts)
    given = swapped(pick(core, parts[1], parts[0]), 1)
    return jnp.concatenate([pick(core, kept, given), pick(core, given, kept)], axis=1)


def solution(mesh):
    return jax.shard_map(
        local,
        mesh=mesh,
        in_specs=(
            P("ctx", "tp"),
            P("ctx"),
            P(None, "tp"),
            P(None, "tp"),
            P("tp", None),
            P("tp", None),
            P(None, "tp"),
            P("tp"),
            P(),
            P(),
            P("tp"),
            P("tp"),
            P("tp"),
            P("tp"),
            P("tp", "ctx"),
        ),
        out_specs=P("ctx", "tp"),
        check_vma=False,
    )
```

```python
import functools

import jax
import jax.numpy as jnp
from jax import lax
from jax.experimental import pallas as pl
from jax.experimental.pallas import tpu as pltpu
from jax.sharding import PartitionSpec as P

H = 128
P_SIZE = 64
N = 128
G = 8
L = 256
CONV = 4
HALO = 16
NORM_EPS = 1e-05
HIGHEST = lax.Precision.HIGHEST

CHIPS = 8
CORES = 2
HEADS = 8
CH = HEADS * P_SIZE
ROWS = 512
FEAT = 256
Z_RING = 8
CTX = 16
ALL_ROWS = HALO + ROWS
COLS = 2 * N + 2 * HEADS
VMEM = pl.BlockSpec(memory_space=pltpu.VMEM)
BF16 = jnp.bfloat16
F32 = jnp.float32


def params(mib, grid=False):
    more = {"dimension_semantics": ("arbitrary",)} if grid else {}
    return pltpu.CompilerParams(vmem_limit_bytes=mib * 2**20, **more)


def dot(a, b):
    return jnp.dot(a, b, preferred_element_type=F32)


def dot_nt(a, b):
    return lax.dot_general(a, b, (((1,), (1,)), ((), ())), preferred_element_type=F32)


def dot_tn(a, b):
    return lax.dot_general(a, b, (((0,), (0,)), ((), ())), preferred_element_type=F32)


def silu(v):
    return v / (1.0 + jnp.exp(-v))


def spread(cols, first=0, count=HEADS):
    shape = (HEADS, count * P_SIZE)
    head = lax.broadcasted_iota(jnp.int32, shape, 0)
    lane = lax.broadcasted_iota(jnp.int32, shape, 1)
    pick = (head == lane // P_SIZE + first).astype(F32)
    return jnp.dot(cols, pick, precision=HIGHEST, preferred_element_type=F32)


def my_core():
    return lax.rem(lax.axis_index("tp"), CORES)


def add_to(acc, step, value):
    @pl.when(step == 0)
    def _():
        acc[...] = value

    @pl.when(step > 0)
    def _():
        acc[...] += value


def conv_chunk(raw, at, rows, masks, taps, offsets):
    total = offsets + taps[CONV - 1 : CONV, :] * raw[at + HALO : at + HALO + rows, :]
    for tap in range(CONV - 1):
        first = at + HALO - (CONV - 1) + tap
        shifted = raw[first : first + rows, :]
        total = total + taps[tap : tap + 1, :] * (shifted * masks[:, tap : tap + 1])
    return silu(total).astype(BF16)


def rounded(ref):
    ref[...] = ref[...].astype(BF16).astype(F32)


def step_sources():
    for slot in range(2):
        for same_core in (True, False):
            yield slot, same_core


def step_tokens(own, sib, halo_own=None, halo_sib=None):
    parts = []
    for slot, same_core in step_sources():
        part = (own if same_core else sib)[slot, :ROWS]
        if halo_own is not None:
            part = jnp.concatenate([(halo_own if same_core else halo_sib)[slot], part], axis=0)
        parts.append(part)
    return jnp.concatenate(parts, axis=1)


def step_cols(own, sib):
    parts = [(own if same_core else sib)[slot, ROWS:] for slot, same_core in step_sources()]
    return jnp.concatenate(parts, axis=1)


def step_rows(w_ref):
    core = my_core()
    parts = []
    for slot, same_core in step_sources():
        from_core = core if same_core else 1 - core
        at = pl.multiple_of((slot * CORES + from_core) * FEAT, FEAT)
        parts.append(w_ref[pl.ds(at, FEAT), :])
    return jnp.concatenate(parts, axis=0)


def scan_input_kernel(
    own,
    sib,
    halo_own,
    halo_sib,
    w_x,
    cols,
    taps_x,
    bias_x,
    taps_bc,
    bias_bc,
    dt_bias,
    decay,
    xc,
    bcc,
    hcol,
    hrow,
    s0,
    pay,
    acc_x,
    acc_bc,
    raw_bc,
):
    step = pl.program_id(0)
    core = my_core()
    toks = step_tokens(own, sib, halo_own, halo_sib)
    add_to(acc_x, step, dot(toks, step_rows(w_x)))
    add_to(acc_bc, step, dot_nt(toks, step_cols(own, sib)))

    @pl.when(step == pl.num_programs(0) - 1)
    def _():
        raw_dt = acc_bc[HALO:, 2 * N :]
        raw_dt = jnp.where(core == 0, raw_dt[:, :HEADS], raw_dt[:, HEADS:])
        pre = raw_dt + dt_bias[...]
        dt = jnp.maximum(pre, 0.0) + jnp.log1p(jnp.exp(-jnp.abs(pre)))
        loga = -decay[...] * dt
        acc_x[...] = acc_x[...].astype(BF16).astype(F32)
        raw_bc[...] = acc_bc[:, : 2 * N].astype(BF16).astype(F32)
        for at in range(0, ROWS, 64):
            masks = cols[at : at + 64, :]
            xc[at : at + 64, :] = conv_chunk(acc_x, at, 64, masks, taps_x, bias_x[...])
            bcc[at : at + 64, :] = conv_chunk(raw_bc, at, 64, masks, taps_bc, bias_bc[...])
        lower = (
            lax.broadcasted_iota(jnp.int32, (L, L), 0) >= lax.broadcasted_iota(jnp.int32, (L, L), 1)
        ).astype(F32)
        cum0 = jnp.dot(lower, loga[:L], precision=HIGHEST, preferred_element_type=F32)
        cum1 = jnp.dot(lower, loga[L:], precision=HIGHEST, preferred_element_type=F32)
        end0, end1 = cum0[L - 1 :], cum1[L - 1 :]
        slab = jnp.exp(jnp.concatenate([cum0, cum1 + end0], axis=0)) * cols[:, 3:4]
        inner = jnp.exp(cum1) * cols[L:, 5:6]
        tail0 = jnp.exp(end0 - cum0) * cols[:L, 6:7] * dt[:L]
        tail1 = jnp.exp(end1 - cum1) * cols[L:, 4:5] * dt[L:]
        cum = jnp.concatenate([cum0, cum1], axis=0)
        blank = jnp.zeros((ROWS, 128 - 4 * HEADS), F32)
        wide = jnp.concatenate(
            [cum, dt, slab, jnp.concatenate([inner, inner], axis=0), blank], axis=1
        )
        hcol[...] = wide
        hrow[...] = wide.T[: 2 * HEADS]
        scaled0 = (xc[:L, :].astype(F32) * spread(tail0)).astype(BF16)
        scaled1 = (xc[L:, :].astype(F32) * spread(tail1)).astype(BF16)
        state0 = dot_tn(bcc[:L, :N], scaled0)
        state1 = dot_tn(bcc[L:, :N], scaled1)
        s0[...] = state0.astype(BF16)
        ends = jnp.concatenate(
            [inner[L - 1 :], slab[ROWS - 1 :], jnp.zeros((6, HEADS), F32)], axis=0
        )
        ends = spread(ends)
        final = ends[0:1] * state0 + state1
        factor = factor_rows(ends[1:2])
        for piece in range(CTX):
            part = final[8 * piece : 8 * piece + 8]
            pay[piece] = jnp.concatenate([part, factor], axis=0).astype(BF16)


def factor_rows(factor):
    high = factor.astype(BF16).astype(F32)
    row = lax.broadcasted_iota(jnp.int32, (8, CH), 0)
    return jnp.where(row == 0, high, jnp.where(row == 1, factor - high, 0.0))


def over_chips(kernel, blocked, fixed, shapes, scratch, mib, flops, name):
    whole = lambda a: pl.BlockSpec(a.shape, lambda i: (0,) * len(a.shape))
    return pl.pallas_call(
        kernel,
        grid=(CHIPS // 2,),
        in_specs=[spec for _, spec in blocked] + [whole(a) for a in fixed],
        out_specs=[whole(a) for a in shapes],
        out_shape=shapes,
        scratch_shapes=scratch,
        compiler_params=params(mib, True),
        cost_estimate=pl.CostEstimate(
            flops=flops, bytes_accessed=8 * 2**20, transcendentals=10**6
        ),
        name=name,
    )(*[a for a, _ in blocked], *fixed)


def two_chips(a, rows):
    return a, pl.BlockSpec((2, rows, FEAT), lambda i: (i, 0, 0))


def their_rows(w):
    return w, pl.BlockSpec((4 * FEAT, CH), lambda i: (i, 0))


def scan_input(own, sib, halo_own, halo_sib, w_x, fixed):
    shapes = [
        jax.ShapeDtypeStruct((ROWS, CH), BF16),
        jax.ShapeDtypeStruct((ROWS, 2 * N), BF16),
        jax.ShapeDtypeStruct((ROWS, 128), F32),
        jax.ShapeDtypeStruct((2 * HEADS, ROWS), F32),
        jax.ShapeDtypeStruct((N, CH), BF16),
        jax.ShapeDtypeStruct((CTX, 16, CH), BF16),
    ]
    blocked = [two_chips(a, ROWS + COLS) for a in (own, sib)]
    blocked += [two_chips(a, HALO) for a in (halo_own, halo_sib)] + [their_rows(w_x)]
    scratch = [
        pltpu.VMEM((ALL_ROWS, CH), F32),
        pltpu.VMEM((ALL_ROWS, COLS), F32),
        pltpu.VMEM((ALL_ROWS, 2 * N), F32),
    ]
    flops = 2 * ALL_ROWS * 4096 * (CH + COLS)
    return over_chips(
        scan_input_kernel, blocked, fixed, shapes, scratch, 24, flops, "scan_input"
    )


def gate_kernel(own, sib, w_z, gates, acc):
    step = pl.program_id(0)
    add_to(acc, step, dot(step_tokens(own, sib), step_rows(w_z)))

    @pl.when(step == pl.num_programs(0) - 1)
    def _():
        for at in range(0, ROWS, 64):
            gates[at : at + 64, :] = silu(acc[at : at + 64, :].astype(BF16).astype(F32))


def gate(own, sib, w_z):
    shapes = [jax.ShapeDtypeStruct((ROWS, CH), F32)]
    blocked = [two_chips(a, ROWS) for a in (own, sib)] + [their_rows(w_z)]
    scratch = [pltpu.VMEM((ROWS, CH), F32)]
    flops = 2 * ROWS * 4096 * CH
    return over_chips(gate_kernel, blocked, [], shapes, scratch, 16, flops, "gate")[0]


def intra_kernel(xc, bcc, hcol, hrow, s0, cols, seg_row, skip, y):
    for block in range(2):
        intra_block(block * L, xc, bcc, hcol, hrow, s0, cols, seg_row, skip, y)


def intra_block(at, xc, bcc, hcol, hrow, s0, cols, seg_row, skip, y):
    b_vals, c_vals = bcc[at : at + L, :N], bcc[at : at + L, N:]
    after = lax.broadcasted_iota(jnp.int32, (L, L), 0) >= lax.broadcasted_iota(
        jnp.int32, (L, L), 1
    )
    same = cols[at : at + L, 7:8] == seg_row[0:1, at : at + L]
    scores = jnp.where(after & same, dot_nt(c_vals, b_vals), 0.0)
    for half in range(2):
        lanes = slice(half * 256, half * 256 + 256)
        weights, values = [], []
        x_half = xc[at : at + L, lanes]
        head_of = lax.broadcasted_iota(jnp.int32, (1, 256), 1) // P_SIZE
        for part in range(4):
            head = half * 4 + part
            gap = hcol[at : at + L, head : head + 1] - hrow[head : head + 1, at : at + L]
            decay = jnp.exp(jnp.minimum(gap, 0.0))
            dt_row = hrow[HEADS + head : HEADS + head + 1, at : at + L]
            weights.append((scores * decay * dt_row).astype(BF16))
            values.append(x_half * (head_of == part).astype(BF16))
        out = dot(jnp.concatenate(weights, axis=1), jnp.concatenate(values, axis=0))
        out = out + skip[:, lanes] * x_half.astype(F32)
        if at:
            carried = spread(hcol[at : at + L, 3 * HEADS : 4 * HEADS], half * 4, 4)
            out = out + carried * dot(c_vals, s0[:, lanes])
        y[at : at + L, lanes] = out


def intra(*args):
    return pl.pallas_call(
        intra_kernel,
        in_specs=[VMEM] * len(args),
        out_specs=VMEM,
        out_shape=jax.ShapeDtypeStruct((ROWS, CH), F32),
        compiler_params=params(12),
        cost_estimate=pl.CostEstimate(
            flops=2 * ROWS * L * CH * 4, bytes_accessed=4 * 2**20, transcendentals=2 * 10**6
        ),
        name="intra",
    )(*args)


def prefix_kernel(pieces, out):
    total = jnp.zeros((8, CH), F32)
    for pair in range(8):
        held = []
        for place in (2 * pair, 2 * pair + 1):
            held.append(total)
            piece = pieces[place].astype(F32)
            total = total * (piece[8:9] + piece[9:10]) + piece[:8]
        out[16 * pair : 16 * pair + 16, :] = jnp.concatenate(held, axis=0).astype(BF16)


def prefix(pieces):
    return pl.pallas_call(
        prefix_kernel,
        in_specs=[VMEM],
        out_specs=VMEM,
        out_shape=jax.ShapeDtypeStruct((N, CH), BF16),
        compiler_params=params(8),
        name="prefix",
    )(pieces)


def join_kernel(y, gates, bcc, hcol, state, gain, out):
    for at in range(0, ROWS, 128):
        c_vals = bcc[at : at + 128, N:]
        carried = spread(hcol[at : at + 128, 2 * HEADS : 3 * HEADS])
        total = y[at : at + 128, :] + carried * dot(c_vals, state[...])
        gated = total * gates[at : at + 128, :]
        square = jnp.sum(gated * gated, axis=1, keepdims=True)
        high = square.astype(BF16).astype(F32)
        lane = lax.broadcasted_iota(jnp.int32, (128, 128), 1)
        out[at : at + 128, :CH] = (gated * gain[...]).astype(BF16)
        out[at : at + 128, CH:] = jnp.where(lane < 64, high, square - high).astype(BF16)


def join(*args):
    return pl.pallas_call(
        join_kernel,
        in_specs=[VMEM] * len(args),
        out_specs=VMEM,
        out_shape=jax.ShapeDtypeStruct((ROWS, CH + 128), BF16),
        compiler_params=params(12),
        cost_estimate=pl.CostEstimate(
            flops=2 * ROWS * N * CH, bytes_accessed=4 * 2**20, transcendentals=0
        ),
        name="join",
    )(*args)


def project_kernel(place, own, sib, w, out):
    del place
    square = own[:, CH:].astype(F32) + sib[:, CH:].astype(F32)
    scale = lax.rsqrt((square[:, 0:1] + square[:, 64:65]) / (2.0 * CH) + NORM_EPS)
    values = jnp.concatenate([own[:, :CH], sib[:, :CH]], axis=1)
    rows = jnp.concatenate([w[0], w[1]], axis=1)
    out[0] = (dot(values, rows) * scale).astype(BF16)


def project(own, sib, w_all, y_low):
    def columns(chip, place):
        return lax.rem(chip, 4), lax.rem(lax.div(chip, 4) + place[0], 2), 0

    whole = pl.BlockSpec(own.shape, lambda i, place: (0, 0))
    return pl.pallas_call(
        project_kernel,
        grid_spec=pltpu.PrefetchScalarGridSpec(
            num_scalar_prefetch=1,
            grid=(CHIPS,),
            in_specs=[whole, whole, pl.BlockSpec((2, 2 * CH, 128), columns)],
            out_specs=pl.BlockSpec((1, ROWS, 256), lambda i, place: (i, 0, 0)),
        ),
        out_shape=jax.ShapeDtypeStruct((CHIPS, ROWS, 256), BF16),
        compiler_params=params(14, True),
        cost_estimate=pl.CostEstimate(
            flops=8 * ROWS * CH * 2048, bytes_accessed=8 * 2**20, transcendentals=0
        ),
        name="project",
    )(y_low[None], own, sib, w_all)


def swapped(value, bit):
    return lax.ppermute(value, "tp", [(i, i ^ bit) for i in range(16)])


def next_ctx(value):
    return lax.ppermute(value, "ctx", [(i, i + 1) for i in range(15)])


def between_chips(value):
    same_core = [[2 * chip + core for chip in range(CHIPS)] for core in range(CORES)]
    return lax.all_to_all(value, "tp", 0, 0, axis_index_groups=same_core)


def between_slabs(value):
    return lax.all_to_all(value, "ctx", 0, 0)


def together(*values):
    return lax.optimization_barrier(values)


def pick(core, first, second):
    return jnp.where(core == 0, first, second)


def document_columns(seg_ids, ids_prior):
    ids_all = jnp.concatenate([ids_prior, seg_ids])
    prior = ids_prior[2]
    same = lambda a: (seg_ids == a).astype(F32)
    columns = [same(ids_all[tap : tap + ROWS]) for tap in range(CONV - 1)]
    columns += [same(prior), same(seg_ids[-1]), same(seg_ids[L - 1]), same(seg_ids[L - 1])]
    columns += [seg_ids.astype(F32)]
    cols = jnp.pad(jnp.stack(columns, axis=1), ((0, 0), (0, 128 - len(columns))))
    return cols, jnp.broadcast_to(seg_ids.astype(F32)[None], (8, ROWS))


def local(
    tokens,
    seg_ids,
    w_x,
    w_z,
    w_bc,
    w_dt,
    conv_x,
    conv_x_bias,
    conv_bc,
    conv_bc_bias,
    dt_bias,
    decay_rate,
    skip_gain,
    norm_weight,
    w_out,
):
    rank = lax.axis_index("tp")
    core = rank % CORES
    chip = rank // CORES
    y_low = (lax.axis_index("ctx") // Z_RING).astype(jnp.int32)

    w_cols = jnp.concatenate(
        [w_bc.T.reshape(CHIPS, 2 * N, FEAT), w_dt.T.reshape(CHIPS, 2 * HEADS, FEAT)], axis=1
    )
    shared = jnp.broadcast_to(tokens[None], (CHIPS, ROWS, FEAT))
    own = between_chips(jnp.concatenate([shared, w_cols], axis=1))

    ids_row = jnp.pad((seg_ids[-3:] + 1).astype(BF16), (0, FEAT - 3))[None]
    halo = next_ctx(jnp.concatenate([ids_row, tokens[1 - HALO :]], axis=0))
    ids_prior = halo[0, :3].astype(jnp.int32) - 1
    halo_own = between_chips(jnp.broadcast_to(halo[None], (CHIPS, HALO, FEAT)))
    halo_sib = swapped(halo_own, 1)

    halves = (w_out[:, :128], w_out[:, 128:])
    w_pair = jnp.concatenate(
        [pick(core, *halves), swapped(pick(core, halves[1], halves[0]), 1)], axis=0
    )
    w_far = lax.ppermute(w_pair, "ctx", [(i, i ^ Z_RING) for i in range(2 * Z_RING)])
    same_y = [list(range(Z_RING)), list(range(Z_RING, 2 * Z_RING))]
    w_both = jnp.concatenate([w_pair, w_far], axis=0)
    w_all = lax.all_gather(w_both, "ctx", axis=0, axis_index_groups=same_y)

    cols, seg_row = document_columns(seg_ids, ids_prior)
    taps_bc = lax.dynamic_slice_in_dim(conv_bc, chip * 2 * N, 2 * N, 1)
    bias_bc = lax.dynamic_slice_in_dim(conv_bc_bias, chip * 2 * N, 2 * N, 0)[None]
    skip = jnp.repeat(skip_gain, P_SIZE)[None]
    fixed = [cols, conv_x, conv_x_bias[None], taps_bc, bias_bc, dt_bias[None], decay_rate[None]]
    own, fixed, seg_row, skip, halo_own, halo_sib = together(
        own, fixed, seg_row, skip, halo_own, halo_sib
    )
    sib = swapped(own, 1)
    xc, bcc, hcol, hrow, s0, pay = scan_input(own, sib, halo_own, halo_sib, w_x, fixed)
    own, sib, pay = together(own, sib, pay)
    pieces = between_slabs(pay)
    gates = gate(own, sib, w_z)
    pieces, gates, xc, bcc = together(pieces, gates, xc, bcc)
    state = between_slabs(prefix(pieces).reshape(CTX, 8, CH)).reshape(N, CH)
    y = intra(xc, bcc, hcol, hrow, s0, fixed[0], seg_row, skip)
    mine = join(y, gates, bcc, hcol, state, norm_weight[None])
    parts = between_chips(project(mine, swapped(mine, 1), w_all, y_low))
    total = jnp.sum(parts.astype(F32), axis=0).astype(BF16)
    parts = (total[:, :128], total[:, 128:])
    kept = pick(core, *parts)
    given = swapped(pick(core, parts[1], parts[0]), 1)
    return jnp.concatenate([pick(core, kept, given), pick(core, given, kept)], axis=1)


def solution(mesh):
    return jax.shard_map(
        local,
        mesh=mesh,
        in_specs=(
            P("ctx", "tp"),
            P("ctx"),
            P(None, "tp"),
            P(None, "tp"),
            P("tp", None),
            P("tp", None),
            P(None, "tp"),
            P("tp"),
            P(),
            P(),
            P("tp"),
            P("tp"),
            P("tp"),
            P("tp"),
            P("tp", "ctx"),
        ),
        out_specs=P("ctx", "tp"),
        check_vma=False,
    )
```

```python
import functools

import jax
import jax.numpy as jnp
from jax import lax
from jax.experimental import pallas as pl
from jax.experimental.pallas import tpu as pltpu
from jax.sharding import PartitionSpec as P

H = 128
P_SIZE = 64
N = 128
G = 8
L = 256
CONV = 4
HALO = 16
NORM_EPS = 1e-05
HIGHEST = lax.Precision.HIGHEST

CHIPS = 8
CORES = 2
HEADS = 8
CH = HEADS * P_SIZE
ROWS = 512
FEAT = 256
Z_RING = 8
CTX = 16
ALL_ROWS = HALO + ROWS
COLS = 2 * N + 2 * HEADS
VMEM = pl.BlockSpec(memory_space=pltpu.VMEM)
BF16 = jnp.bfloat16
F32 = jnp.float32


def params(mib, grid=False):
    more = {"dimension_semantics": ("arbitrary",)} if grid else {}
    return pltpu.CompilerParams(vmem_limit_bytes=mib * 2**20, **more)


def dot(a, b):
    return jnp.dot(a, b, preferred_element_type=F32)


def dot_nt(a, b):
    return lax.dot_general(a, b, (((1,), (1,)), ((), ())), preferred_element_type=F32)


def dot_tn(a, b):
    return lax.dot_general(a, b, (((0,), (0,)), ((), ())), preferred_element_type=F32)


def silu(v):
    return v / (1.0 + jnp.exp(-v))


def spread(cols, first=0, count=HEADS):
    shape = (HEADS, count * P_SIZE)
    head = lax.broadcasted_iota(jnp.int32, shape, 0)
    lane = lax.broadcasted_iota(jnp.int32, shape, 1)
    pick = (head == lane // P_SIZE + first).astype(F32)
    return jnp.dot(cols, pick, precision=HIGHEST, preferred_element_type=F32)


def my_core():
    return lax.rem(lax.axis_index("tp"), CORES)


def add_to(acc, step, value):
    @pl.when(step == 0)
    def _():
        acc[...] = value

    @pl.when(step > 0)
    def _():
        acc[...] += value


def conv_chunk(raw, at, rows, masks, taps, offsets):
    total = offsets + taps[CONV - 1 : CONV, :] * raw[at + HALO : at + HALO + rows, :]
    for tap in range(CONV - 1):
        first = at + HALO - (CONV - 1) + tap
        shifted = raw[first : first + rows, :]
        total = total + taps[tap : tap + 1, :] * (shifted * masks[:, tap : tap + 1])
    return silu(total).astype(BF16)


def rounded(ref):
    ref[...] = ref[...].astype(BF16).astype(F32)


def step_sources():
    for slot in range(2):
        for same_core in (True, False):
            yield slot, same_core


def step_tokens(own, sib, halo_own=None, halo_sib=None):
    parts = []
    for slot, same_core in step_sources():
        part = (own if same_core else sib)[slot, :ROWS]
        if halo_own is not None:
            part = jnp.concatenate([(halo_own if same_core else halo_sib)[slot], part], axis=0)
        parts.append(part)
    return jnp.concatenate(parts, axis=1)


def step_cols(own, sib):
    refs = [(own if same_core else sib, slot) for slot, same_core in step_sources()]
    w_bc = [ref[slot, ROWS : ROWS + FEAT] for ref, slot in refs]
    w_dt = [ref[slot, ROWS + FEAT :] for ref, slot in refs]
    return jnp.concatenate(w_bc, axis=0), jnp.concatenate(w_dt, axis=1)


def step_rows(w_ref):
    core = my_core()
    parts = []
    for slot, same_core in step_sources():
        from_core = core if same_core else 1 - core
        at = pl.multiple_of((slot * CORES + from_core) * FEAT, FEAT)
        parts.append(w_ref[pl.ds(at, FEAT), :])
    return jnp.concatenate(parts, axis=0)


def scan_input_kernel(
    own,
    sib,
    halo_own,
    halo_sib,
    w_x,
    cols,
    taps_x,
    bias_x,
    taps_bc,
    bias_bc,
    dt_bias,
    decay,
    xc,
    bcc,
    hcol,
    hrow,
    s0,
    pay,
    acc_x,
    acc_bc,
    acc_dt,
):
    step = pl.program_id(0)
    core = my_core()
    toks = step_tokens(own, sib, halo_own, halo_sib)
    add_to(acc_x, step, dot(toks, step_rows(w_x)))
    w_bc, w_dt = step_cols(own, sib)
    add_to(acc_bc, step, dot(toks, w_bc))
    add_to(acc_dt, step, dot_nt(toks, w_dt))

    @pl.when(step == pl.num_programs(0) - 1)
    def _():
        raw_dt = acc_dt[HALO:, :]
        raw_dt = jnp.where(core == 0, raw_dt[:, :HEADS], raw_dt[:, HEADS:])
        pre = raw_dt + dt_bias[...]
        dt = jnp.maximum(pre, 0.0) + jnp.log1p(jnp.exp(-jnp.abs(pre)))
        loga = -decay[...] * dt
        acc_x[...] = acc_x[...].astype(BF16).astype(F32)
        acc_bc[...] = acc_bc[...].astype(BF16).astype(F32)
        for at in range(0, ROWS, 64):
            masks = cols[at : at + 64, :]
            xc[at : at + 64, :] = conv_chunk(acc_x, at, 64, masks, taps_x, bias_x[...])
            bcc[at : at + 64, :] = conv_chunk(acc_bc, at, 64, masks, taps_bc, bias_bc[...])
        lower = (
            lax.broadcasted_iota(jnp.int32, (L, L), 0) >= lax.broadcasted_iota(jnp.int32, (L, L), 1)
        ).astype(F32)
        cum0 = jnp.dot(lower, loga[:L], precision=HIGHEST, preferred_element_type=F32)
        cum1 = jnp.dot(lower, loga[L:], precision=HIGHEST, preferred_element_type=F32)
        end0, end1 = cum0[L - 1 :], cum1[L - 1 :]
        slab = jnp.exp(jnp.concatenate([cum0, cum1 + end0], axis=0)) * cols[:, 3:4]
        inner = jnp.exp(cum1) * cols[L:, 5:6]
        tail0 = jnp.exp(end0 - cum0) * cols[:L, 6:7] * dt[:L]
        tail1 = jnp.exp(end1 - cum1) * cols[L:, 4:5] * dt[L:]
        cum = jnp.concatenate([cum0, cum1], axis=0)
        blank = jnp.zeros((ROWS, 128 - 4 * HEADS), F32)
        wide = jnp.concatenate(
            [cum, dt, slab, jnp.concatenate([inner, inner], axis=0), blank], axis=1
        )
        hcol[...] = wide
        hrow[...] = wide.T[: 2 * HEADS]
        scaled0 = (xc[:L, :].astype(F32) * spread(tail0)).astype(BF16)
        scaled1 = (xc[L:, :].astype(F32) * spread(tail1)).astype(BF16)
        state0 = dot_tn(bcc[:L, :N], scaled0)
        state1 = dot_tn(bcc[L:, :N], scaled1)
        s0[...] = state0.astype(BF16)
        ends = jnp.concatenate(
            [inner[L - 1 :], slab[ROWS - 1 :], jnp.zeros((6, HEADS), F32)], axis=0
        )
        ends = spread(ends)
        final = ends[0:1] * state0 + state1
        factor = factor_rows(ends[1:2])
        for piece in range(CTX):
            part = final[8 * piece : 8 * piece + 8]
            pay[piece] = jnp.concatenate([part, factor], axis=0).astype(BF16)


def factor_rows(factor):
    high = factor.astype(BF16).astype(F32)
    row = lax.broadcasted_iota(jnp.int32, (8, CH), 0)
    return jnp.where(row == 0, high, jnp.where(row == 1, factor - high, 0.0))


def over_chips(kernel, blocked, fixed, shapes, scratch, mib, flops, name):
    whole = lambda a: pl.BlockSpec(a.shape, lambda i: (0,) * len(a.shape))
    return pl.pallas_call(
        kernel,
        grid=(CHIPS // 2,),
        in_specs=[spec for _, spec in blocked] + [whole(a) for a in fixed],
        out_specs=[whole(a) for a in shapes],
        out_shape=shapes,
        scratch_shapes=scratch,
        compiler_params=params(mib, True),
        cost_estimate=pl.CostEstimate(
            flops=flops, bytes_accessed=8 * 2**20, transcendentals=10**6
        ),
        name=name,
    )(*[a for a, _ in blocked], *fixed)


def two_chips(a, rows):
    return a, pl.BlockSpec((2, rows, FEAT), lambda i: (i, 0, 0))


def their_rows(w):
    return w, pl.BlockSpec((4 * FEAT, CH), lambda i: (i, 0))


def scan_input(own, sib, halo_own, halo_sib, w_x, fixed):
    shapes = [
        jax.ShapeDtypeStruct((ROWS, CH), BF16),
        jax.ShapeDtypeStruct((ROWS, 2 * N), BF16),
        jax.ShapeDtypeStruct((ROWS, 128), F32),
        jax.ShapeDtypeStruct((2 * HEADS, ROWS), F32),
        jax.ShapeDtypeStruct((N, CH), BF16),
        jax.ShapeDtypeStruct((CTX, 16, CH), BF16),
    ]
    blocked = [two_chips(a, ROWS + COLS) for a in (own, sib)]
    blocked += [two_chips(a, HALO) for a in (halo_own, halo_sib)] + [their_rows(w_x)]
    scratch = [
        pltpu.VMEM((ALL_ROWS, CH), F32),
        pltpu.VMEM((ALL_ROWS, 2 * N), F32),
        pltpu.VMEM((ALL_ROWS, 2 * HEADS), F32),
    ]
    flops = 2 * ALL_ROWS * 4096 * (CH + COLS)
    return over_chips(
        scan_input_kernel, blocked, fixed, shapes, scratch, 58, flops, "scan_input"
    )


def gate_kernel(own, sib, w_z, gates, acc):
    step = pl.program_id(0)
    add_to(acc, step, dot(step_tokens(own, sib), step_rows(w_z)))

    @pl.when(step == pl.num_programs(0) - 1)
    def _():
        for at in range(0, ROWS, 64):
            gates[at : at + 64, :] = silu(acc[at : at + 64, :].astype(BF16).astype(F32))


def gate(own, sib, w_z):
    shapes = [jax.ShapeDtypeStruct((ROWS, CH), F32)]
    blocked = [two_chips(a, ROWS) for a in (own, sib)] + [their_rows(w_z)]
    scratch = [pltpu.VMEM((ROWS, CH), F32)]
    flops = 2 * ROWS * 4096 * CH
    return over_chips(gate_kernel, blocked, [], shapes, scratch, 16, flops, "gate")[0]


def intra_kernel(xc, bcc, hcol, hrow, s0, cols, seg_row, skip, y):
    for block in range(2):
        intra_block(block * L, xc, bcc, hcol, hrow, s0, cols, seg_row, skip, y)


def intra_block(at, xc, bcc, hcol, hrow, s0, cols, seg_row, skip, y):
    b_vals, c_vals = bcc[at : at + L, :N], bcc[at : at + L, N:]
    after = lax.broadcasted_iota(jnp.int32, (L, L), 0) >= lax.broadcasted_iota(
        jnp.int32, (L, L), 1
    )
    same = cols[at : at + L, 7:8] == seg_row[0:1, at : at + L]
    scores = jnp.where(after & same, dot_nt(c_vals, b_vals), 0.0)
    for half in range(2):
        lanes = slice(half * 256, half * 256 + 256)
        weights, values = [], []
        x_half = xc[at : at + L, lanes]
        head_of = lax.broadcasted_iota(jnp.int32, (1, 256), 1) // P_SIZE
        for part in range(4):
            head = half * 4 + part
            gap = hcol[at : at + L, head : head + 1] - hrow[head : head + 1, at : at + L]
            decay = jnp.exp(jnp.minimum(gap, 0.0))
            dt_row = hrow[HEADS + head : HEADS + head + 1, at : at + L]
            weights.append((scores * decay * dt_row).astype(BF16))
            values.append(x_half * (head_of == part).astype(BF16))
        out = dot(jnp.concatenate(weights, axis=1), jnp.concatenate(values, axis=0))
        out = out + skip[:, lanes] * x_half.astype(F32)
        if at:
            carried = spread(hcol[at : at + L, 3 * HEADS : 4 * HEADS], half * 4, 4)
            out = out + carried * dot(c_vals, s0[:, lanes])
        y[at : at + L, lanes] = out


def intra(*args):
    return pl.pallas_call(
        intra_kernel,
        in_specs=[VMEM] * len(args),
        out_specs=VMEM,
        out_shape=jax.ShapeDtypeStruct((ROWS, CH), F32),
        compiler_params=params(12),
        cost_estimate=pl.CostEstimate(
            flops=2 * ROWS * L * CH * 4, bytes_accessed=4 * 2**20, transcendentals=2 * 10**6
        ),
        name="intra",
    )(*args)


def prefix_kernel(pieces, out):
    total = jnp.zeros((8, CH), F32)
    for pair in range(8):
        held = []
        for place in (2 * pair, 2 * pair + 1):
            held.append(total)
            piece = pieces[place].astype(F32)
            total = total * (piece[8:9] + piece[9:10]) + piece[:8]
        out[16 * pair : 16 * pair + 16, :] = jnp.concatenate(held, axis=0).astype(BF16)


def prefix(pieces):
    return pl.pallas_call(
        prefix_kernel,
        in_specs=[VMEM],
        out_specs=VMEM,
        out_shape=jax.ShapeDtypeStruct((N, CH), BF16),
        compiler_params=params(8),
        name="prefix",
    )(pieces)


def join_kernel(y, gates, bcc, hcol, state, gain, out):
    for at in range(0, ROWS, 128):
        c_vals = bcc[at : at + 128, N:]
        carried = spread(hcol[at : at + 128, 2 * HEADS : 3 * HEADS])
        total = y[at : at + 128, :] + carried * dot(c_vals, state[...])
        gated = total * gates[at : at + 128, :]
        square = jnp.sum(gated * gated, axis=1, keepdims=True)
        high = square.astype(BF16).astype(F32)
        lane = lax.broadcasted_iota(jnp.int32, (128, 128), 1)
        out[at : at + 128, :CH] = (gated * gain[...]).astype(BF16)
        out[at : at + 128, CH:] = jnp.where(lane < 64, high, square - high).astype(BF16)


def join(*args):
    return pl.pallas_call(
        join_kernel,
        in_specs=[VMEM] * len(args),
        out_specs=VMEM,
        out_shape=jax.ShapeDtypeStruct((ROWS, CH + 128), BF16),
        compiler_params=params(12),
        cost_estimate=pl.CostEstimate(
            flops=2 * ROWS * N * CH, bytes_accessed=4 * 2**20, transcendentals=0
        ),
        name="join",
    )(*args)


def project_kernel(place, own, sib, w, out):
    del place
    square = own[:, CH:].astype(F32) + sib[:, CH:].astype(F32)
    scale = lax.rsqrt((square[:, 0:1] + square[:, 64:65]) / (2.0 * CH) + NORM_EPS)
    values = jnp.concatenate([own[:, :CH], sib[:, :CH]], axis=1)
    rows = jnp.concatenate([w[0], w[1]], axis=1)
    out[0] = (dot(values, rows) * scale).astype(BF16)


def project(own, sib, w_all, y_low):
    def columns(chip, place):
        return lax.rem(chip, 4), lax.rem(lax.div(chip, 4) + place[0], 2), 0

    whole = pl.BlockSpec(own.shape, lambda i, place: (0, 0))
    return pl.pallas_call(
        project_kernel,
        grid_spec=pltpu.PrefetchScalarGridSpec(
            num_scalar_prefetch=1,
            grid=(CHIPS,),
            in_specs=[whole, whole, pl.BlockSpec((2, 2 * CH, 128), columns)],
            out_specs=pl.BlockSpec((1, ROWS, 256), lambda i, place: (i, 0, 0)),
        ),
        out_shape=jax.ShapeDtypeStruct((CHIPS, ROWS, 256), BF16),
        compiler_params=params(58, True),
        cost_estimate=pl.CostEstimate(
            flops=8 * ROWS * CH * 2048, bytes_accessed=8 * 2**20, transcendentals=0
        ),
        name="project",
    )(y_low[None], own, sib, w_all)


def swapped(value, bit):
    return lax.ppermute(value, "tp", [(i, i ^ bit) for i in range(16)])


def next_ctx(value):
    return lax.ppermute(value, "ctx", [(i, i + 1) for i in range(15)])


def between_chips(value):
    same_core = [[2 * chip + core for chip in range(CHIPS)] for core in range(CORES)]
    return lax.all_to_all(value, "tp", 0, 0, axis_index_groups=same_core)


def between_slabs(value):
    return lax.all_to_all(value, "ctx", 0, 0)


def together(*values):
    return lax.optimization_barrier(values)


def pick(core, first, second):
    return jnp.where(core == 0, first, second)


def document_columns(seg_ids, ids_prior):
    ids_all = jnp.concatenate([ids_prior, seg_ids])
    prior = ids_prior[2]
    same = lambda a: (seg_ids == a).astype(F32)
    columns = [same(ids_all[tap : tap + ROWS]) for tap in range(CONV - 1)]
    columns += [same(prior), same(seg_ids[-1]), same(seg_ids[L - 1]), same(seg_ids[L - 1])]
    columns += [seg_ids.astype(F32)]
    cols = jnp.pad(jnp.stack(columns, axis=1), ((0, 0), (0, 128 - len(columns))))
    return cols, jnp.broadcast_to(seg_ids.astype(F32)[None], (8, ROWS))


def local(
    tokens,
    seg_ids,
    w_x,
    w_z,
    w_bc,
    w_dt,
    conv_x,
    conv_x_bias,
    conv_bc,
    conv_bc_bias,
    dt_bias,
    decay_rate,
    skip_gain,
    norm_weight,
    w_out,
):
    rank = lax.axis_index("tp")
    core = rank % CORES
    chip = rank // CORES
    y_low = (lax.axis_index("ctx") // Z_RING).astype(jnp.int32)

    w_groups = jnp.stack([w_bc[:, 2 * N * n : 2 * N * (n + 1)] for n in range(CHIPS)])
    w_steps = w_dt.T.reshape(CHIPS, 2 * HEADS, FEAT)
    shared = jnp.broadcast_to(tokens[None], (CHIPS, ROWS, FEAT))
    sent = jnp.concatenate([shared, w_groups, w_steps], axis=1)
    sent, tokens, seg_ids, w_out = together(sent, tokens, seg_ids, w_out)
    own = between_chips(sent)

    ids_row = jnp.pad((seg_ids[-3:] + 1).astype(BF16), (0, FEAT - 3))[None]
    halo = next_ctx(jnp.concatenate([ids_row, tokens[1 - HALO :]], axis=0))
    ids_prior = halo[0, :3].astype(jnp.int32) - 1
    halo_own = between_chips(jnp.broadcast_to(halo[None], (CHIPS, HALO, FEAT)))
    halo_sib = swapped(halo_own, 1)

    halves = (w_out[:, :128], w_out[:, 128:])
    w_pair = jnp.concatenate(
        [pick(core, *halves), swapped(pick(core, halves[1], halves[0]), 1)], axis=0
    )
    w_far = lax.ppermute(w_pair, "ctx", [(i, i ^ Z_RING) for i in range(2 * Z_RING)])
    same_y = [list(range(Z_RING)), list(range(Z_RING, 2 * Z_RING))]
    w_both = jnp.concatenate([w_pair, w_far], axis=0)
    w_all = lax.all_gather(w_both, "ctx", axis=0, axis_index_groups=same_y)

    cols, seg_row = document_columns(seg_ids, ids_prior)
    taps_bc = lax.dynamic_slice_in_dim(conv_bc, chip * 2 * N, 2 * N, 1)
    bias_bc = lax.dynamic_slice_in_dim(conv_bc_bias, chip * 2 * N, 2 * N, 0)[None]
    skip = jnp.repeat(skip_gain, P_SIZE)[None]
    fixed = [cols, conv_x, conv_x_bias[None], taps_bc, bias_bc, dt_bias[None], decay_rate[None]]
    own, fixed, seg_row, skip, halo_own, halo_sib = together(
        own, fixed, seg_row, skip, halo_own, halo_sib
    )
    sib = swapped(own, 1)
    xc, bcc, hcol, hrow, s0, pay = scan_input(own, sib, halo_own, halo_sib, w_x, fixed)
    own, sib, pay = together(own, sib, pay)
    pieces = between_slabs(pay)
    gates = gate(own, sib, w_z)
    pieces, gates, xc, bcc = together(pieces, gates, xc, bcc)
    state = between_slabs(prefix(pieces).reshape(CTX, 8, CH)).reshape(N, CH)
    y = intra(xc, bcc, hcol, hrow, s0, fixed[0], seg_row, skip)
    y, state, w_all = together(y, state, w_all)
    mine = join(y, gates, bcc, hcol, state, norm_weight[None])
    parts = between_chips(project(mine, swapped(mine, 1), w_all, y_low))
    total = jnp.sum(parts.astype(F32), axis=0).astype(BF16)
    parts = (total[:, :128], total[:, 128:])
    kept = pick(core, *parts)
    given = swapped(pick(core, parts[1], parts[0]), 1)
    return jnp.concatenate([pick(core, kept, given), pick(core, given, kept)], axis=1)


def solution(mesh):
    return jax.shard_map(
        local,
        mesh=mesh,
        in_specs=(
            P("ctx", "tp"),
            P("ctx"),
            P(None, "tp"),
            P(None, "tp"),
            P("tp", None),
            P("tp", None),
            P(None, "tp"),
            P("tp"),
            P(),
            P(),
            P("tp"),
            P("tp"),
            P("tp"),
            P("tp"),
            P("tp", "ctx"),
        ),
        out_specs=P("ctx", "tp"),
        check_vma=False,
    )
```

```python
import functools

import jax
import jax.numpy as jnp
from jax import lax
from jax.experimental import pallas as pl
from jax.experimental.pallas import tpu as pltpu
from jax.sharding import PartitionSpec as P

H = 128
P_SIZE = 64
N = 128
G = 8
L = 256
CONV = 4
HALO = 16
NORM_EPS = 1e-05
HIGHEST = lax.Precision.HIGHEST

CHIPS = 8
CORES = 2
HEADS = 8
CH = HEADS * P_SIZE
ROWS = 512
FEAT = 256
Z_RING = 8
CTX = 16
ALL_ROWS = HALO + ROWS
COLS = 2 * N + 2 * HEADS
VMEM = pl.BlockSpec(memory_space=pltpu.VMEM)
BF16 = jnp.bfloat16
F32 = jnp.float32


def params(mib, grid=False):
    more = {"dimension_semantics": ("arbitrary",)} if grid else {}
    return pltpu.CompilerParams(vmem_limit_bytes=mib * 2**20, **more)


def dot(a, b):
    return jnp.dot(a, b, preferred_element_type=F32)


def dot_nt(a, b):
    return lax.dot_general(a, b, (((1,), (1,)), ((), ())), preferred_element_type=F32)


def dot_tn(a, b):
    return lax.dot_general(a, b, (((0,), (0,)), ((), ())), preferred_element_type=F32)


def silu(v):
    return v / (1.0 + jnp.exp(-v))


def spread(cols, first=0, count=HEADS):
    shape = (HEADS, count * P_SIZE)
    head = lax.broadcasted_iota(jnp.int32, shape, 0)
    lane = lax.broadcasted_iota(jnp.int32, shape, 1)
    pick = (head == lane // P_SIZE + first).astype(F32)
    return jnp.dot(cols, pick, precision=HIGHEST, preferred_element_type=F32)


def my_core():
    return lax.rem(lax.axis_index("tp"), CORES)


def add_to(acc, step, value):
    @pl.when(step == 0)
    def _():
        acc[...] = value

    @pl.when(step > 0)
    def _():
        acc[...] += value


def conv_chunk(raw, at, rows, masks, taps, offsets):
    total = offsets + taps[CONV - 1 : CONV, :] * raw[at + HALO : at + HALO + rows, :]
    for tap in range(CONV - 1):
        first = at + HALO - (CONV - 1) + tap
        shifted = raw[first : first + rows, :]
        total = total + taps[tap : tap + 1, :] * (shifted * masks[:, tap : tap + 1])
    return silu(total).astype(BF16)


def rounded(ref):
    ref[...] = ref[...].astype(BF16).astype(F32)


def step_sources():
    for slot in range(2):
        for same_core in (True, False):
            yield slot, same_core


def step_tokens(own, sib, first=0):
    refs = [(own if same_core else sib, slot) for slot, same_core in step_sources()]
    return jnp.concatenate([ref[slot, first:ALL_ROWS] for ref, slot in refs], axis=1)


def step_cols(own, sib):
    refs = [(own if same_core else sib, slot) for slot, same_core in step_sources()]
    return jnp.concatenate([ref[slot, ALL_ROWS:] for ref, slot in refs], axis=1)


def step_rows(w_ref, first):
    core = my_core()
    parts = []
    for slot, same_core in step_sources():
        from_core = core if same_core else 1 - core
        at = pl.multiple_of(first + (slot * CORES + from_core) * FEAT, FEAT)
        parts.append(w_ref[pl.ds(at, FEAT), :])
    return jnp.concatenate(parts, axis=0)


def scan_input_kernel(
    own,
    sib,
    w_x,
    cols,
    taps_x,
    bias_x,
    taps_bc,
    bias_bc,
    dt_bias,
    decay,
    xc,
    bcc,
    hcol,
    hrow,
    s0,
    pay,
    acc_x,
    acc_bc,
    raw_bc,
    held,
    sems,
):
    step = pl.program_id(0)
    core = my_core()
    rows = 4 * FEAT

    def copy(n):
        at = pl.ds(n * rows, rows)
        return pltpu.make_async_copy(w_x.at[at], held.at[at], sems.at[n])

    for n in range(CHIPS // 2):

        @pl.when(step == 0)
        def _():
            copy(n).start()

    for n in range(CHIPS // 2):

        @pl.when(step == n)
        def _():
            copy(n).wait()

    toks = step_tokens(own, sib)
    add_to(acc_x, step, dot(toks, step_rows(held, step * rows)))
    add_to(acc_bc, step, dot_nt(toks, step_cols(own, sib)))

    @pl.when(step == pl.num_programs(0) - 1)
    def _():
        raw_dt = acc_bc[HALO:, 2 * N :]
        raw_dt = jnp.where(core == 0, raw_dt[:, :HEADS], raw_dt[:, HEADS:])
        pre = raw_dt + dt_bias[...]
        dt = jnp.maximum(pre, 0.0) + jnp.log1p(jnp.exp(-jnp.abs(pre)))
        loga = -decay[...] * dt
        acc_x[...] = acc_x[...].astype(BF16).astype(F32)
        raw_bc[...] = acc_bc[:, : 2 * N].astype(BF16).astype(F32)
        for at in range(0, ROWS, 64):
            masks = cols[at : at + 64, :]
            xc[at : at + 64, :] = conv_chunk(acc_x, at, 64, masks, taps_x, bias_x[...])
            bcc[at : at + 64, :] = conv_chunk(raw_bc, at, 64, masks, taps_bc, bias_bc[...])
        lower = (
            lax.broadcasted_iota(jnp.int32, (L, L), 0) >= lax.broadcasted_iota(jnp.int32, (L, L), 1)
        ).astype(F32)
        cum0 = jnp.dot(lower, loga[:L], precision=HIGHEST, preferred_element_type=F32)
        cum1 = jnp.dot(lower, loga[L:], precision=HIGHEST, preferred_element_type=F32)
        end0, end1 = cum0[L - 1 :], cum1[L - 1 :]
        slab = jnp.exp(jnp.concatenate([cum0, cum1 + end0], axis=0)) * cols[:, 3:4]
        inner = jnp.exp(cum1) * cols[L:, 5:6]
        tail0 = jnp.exp(end0 - cum0) * cols[:L, 6:7] * dt[:L]
        tail1 = jnp.exp(end1 - cum1) * cols[L:, 4:5] * dt[L:]
        cum = jnp.concatenate([cum0, cum1], axis=0)
        blank = jnp.zeros((ROWS, 128 - 4 * HEADS), F32)
        wide = jnp.concatenate(
            [cum, dt, slab, jnp.concatenate([inner, inner], axis=0), blank], axis=1
        )
        hcol[...] = wide
        hrow[...] = wide.T[: 2 * HEADS]
        scaled0 = (xc[:L, :].astype(F32) * spread(tail0)).astype(BF16)
        scaled1 = (xc[L:, :].astype(F32) * spread(tail1)).astype(BF16)
        state0 = dot_tn(bcc[:L, :N], scaled0)
        state1 = dot_tn(bcc[L:, :N], scaled1)
        s0[...] = state0.astype(BF16)
        ends = jnp.concatenate(
            [inner[L - 1 :], slab[ROWS - 1 :], jnp.zeros((6, HEADS), F32)], axis=0
        )
        ends = spread(ends)
        final = ends[0:1] * state0 + state1
        factor = factor_rows(ends[1:2])
        for piece in range(CTX):
            part = final[8 * piece : 8 * piece + 8]
            pay[piece] = jnp.concatenate([part, factor], axis=0).astype(BF16)


def factor_rows(factor):
    high = factor.astype(BF16).astype(F32)
    row = lax.broadcasted_iota(jnp.int32, (8, CH), 0)
    return jnp.where(row == 0, high, jnp.where(row == 1, factor - high, 0.0))


def over_chips(kernel, blocked, fixed, shapes, scratch, mib, flops, name):
    whole = lambda a: pl.BlockSpec(a.shape, lambda i: (0,) * len(a.shape))
    return pl.pallas_call(
        kernel,
        grid=(CHIPS // 2,),
        in_specs=[spec for _, spec in blocked] + [whole(a) for a in fixed],
        out_specs=[whole(a) for a in shapes],
        out_shape=[pltpu.HBM(a.shape, a.dtype) for a in shapes],
        scratch_shapes=scratch,
        compiler_params=params(mib, True),
        cost_estimate=pl.CostEstimate(
            flops=flops, bytes_accessed=8 * 2**20, transcendentals=10**6
        ),
        name=name,
    )(*[a for a, _ in blocked], *fixed)


def two_chips(a, rows):
    return a, pl.BlockSpec((2, rows, FEAT), lambda i: (i, 0, 0))


def their_rows(w):
    return w, pl.BlockSpec((4 * FEAT, CH), lambda i: (i, 0))


def scan_input(own, sib, w_x, fixed):
    shapes = [
        jax.ShapeDtypeStruct((ROWS, CH), BF16),
        jax.ShapeDtypeStruct((ROWS, 2 * N), BF16),
        jax.ShapeDtypeStruct((ROWS, 128), F32),
        jax.ShapeDtypeStruct((2 * HEADS, ROWS), F32),
        jax.ShapeDtypeStruct((N, CH), BF16),
        jax.ShapeDtypeStruct((CTX, 16, CH), BF16),
    ]
    blocked = [two_chips(a, ALL_ROWS + COLS) for a in (own, sib)]
    blocked += [(w_x, pl.BlockSpec(memory_space=pltpu.HBM))]
    scratch = [
        pltpu.VMEM((ALL_ROWS, CH), F32),
        pltpu.VMEM((ALL_ROWS, COLS), F32),
        pltpu.VMEM((ALL_ROWS, 2 * N), F32),
        pltpu.VMEM((CHIPS * 2 * FEAT, CH), BF16),
        pltpu.SemaphoreType.DMA((CHIPS // 2,)),
    ]
    flops = 2 * ALL_ROWS * 4096 * (CH + COLS)
    return over_chips(
        scan_input_kernel, blocked, fixed, shapes, scratch, 52, flops, "scan_input"
    )


def gate_kernel(own, sib, w_z, gates, acc):
    step = pl.program_id(0)
    add_to(acc, step, dot(step_tokens(own, sib, HALO), step_rows(w_z, 0)))

    @pl.when(step == pl.num_programs(0) - 1)
    def _():
        for at in range(0, ROWS, 64):
            gates[at : at + 64, :] = silu(acc[at : at + 64, :].astype(BF16).astype(F32))


def gate(own, sib, w_z):
    shapes = [jax.ShapeDtypeStruct((ROWS, CH), F32)]
    blocked = [two_chips(a, ALL_ROWS) for a in (own, sib)] + [their_rows(w_z)]
    scratch = [pltpu.VMEM((ROWS, CH), F32)]
    flops = 2 * ROWS * 4096 * CH
    return over_chips(gate_kernel, blocked, [], shapes, scratch, 16, flops, "gate")[0]


def intra_kernel(xc, bcc, hcol, hrow, s0, cols, seg_row, skip, y):
    for block in range(2):
        intra_block(block * L, xc, bcc, hcol, hrow, s0, cols, seg_row, skip, y)


def intra_block(at, xc, bcc, hcol, hrow, s0, cols, seg_row, skip, y):
    b_vals, c_vals = bcc[at : at + L, :N], bcc[at : at + L, N:]
    after = lax.broadcasted_iota(jnp.int32, (L, L), 0) >= lax.broadcasted_iota(
        jnp.int32, (L, L), 1
    )
    same = cols[at : at + L, 7:8] == seg_row[0:1, at : at + L]
    scores = jnp.where(after & same, dot_nt(c_vals, b_vals), 0.0)
    for half in range(2):
        lanes = slice(half * 256, half * 256 + 256)
        weights, values = [], []
        x_half = xc[at : at + L, lanes]
        head_of = lax.broadcasted_iota(jnp.int32, (1, 256), 1) // P_SIZE
        for part in range(4):
            head = half * 4 + part
            gap = hcol[at : at + L, head : head + 1] - hrow[head : head + 1, at : at + L]
            decay = jnp.exp(jnp.minimum(gap, 0.0))
            dt_row = hrow[HEADS + head : HEADS + head + 1, at : at + L]
            weights.append((scores * decay * dt_row).astype(BF16))
            values.append(x_half * (head_of == part).astype(BF16))
        out = dot(jnp.concatenate(weights, axis=1), jnp.concatenate(values, axis=0))
        out = out + skip[:, lanes] * x_half.astype(F32)
        if at:
            carried = spread(hcol[at : at + L, 3 * HEADS : 4 * HEADS], half * 4, 4)
            out = out + carried * dot(c_vals, s0[:, lanes])
        y[at : at + L, lanes] = out


def intra(*args):
    return pl.pallas_call(
        intra_kernel,
        in_specs=[VMEM] * len(args),
        out_specs=VMEM,
        out_shape=jax.ShapeDtypeStruct((ROWS, CH), F32),
        compiler_params=params(12),
        cost_estimate=pl.CostEstimate(
            flops=2 * ROWS * L * CH * 4, bytes_accessed=4 * 2**20, transcendentals=2 * 10**6
        ),
        name="intra",
    )(*args)


def prefix_kernel(pieces, out):
    total = jnp.zeros((8, CH), F32)
    for pair in range(8):
        held = []
        for place in (2 * pair, 2 * pair + 1):
            held.append(total)
            piece = pieces[place].astype(F32)
            total = total * (piece[8:9] + piece[9:10]) + piece[:8]
        out[16 * pair : 16 * pair + 16, :] = jnp.concatenate(held, axis=0).astype(BF16)


def prefix(pieces):
    return pl.pallas_call(
        prefix_kernel,
        in_specs=[VMEM],
        out_specs=VMEM,
        out_shape=jax.ShapeDtypeStruct((N, CH), BF16),
        compiler_params=params(8),
        name="prefix",
    )(pieces)


def join_kernel(y, gates, bcc, hcol, state, gain, out):
    for at in range(0, ROWS, 128):
        c_vals = bcc[at : at + 128, N:]
        carried = spread(hcol[at : at + 128, 2 * HEADS : 3 * HEADS])
        total = y[at : at + 128, :] + carried * dot(c_vals, state[...])
        gated = total * gates[at : at + 128, :]
        square = jnp.sum(gated * gated, axis=1, keepdims=True)
        high = square.astype(BF16).astype(F32)
        lane = lax.broadcasted_iota(jnp.int32, (128, 128), 1)
        out[at : at + 128, :CH] = (gated * gain[...]).astype(BF16)
        out[at : at + 128, CH:] = jnp.where(lane < 64, high, square - high).astype(BF16)


def join(*args):
    return pl.pallas_call(
        join_kernel,
        in_specs=[VMEM] * len(args),
        out_specs=VMEM,
        out_shape=jax.ShapeDtypeStruct((ROWS, CH + 128), BF16),
        compiler_params=params(12),
        cost_estimate=pl.CostEstimate(
            flops=2 * ROWS * N * CH, bytes_accessed=4 * 2**20, transcendentals=0
        ),
        name="join",
    )(*args)


def project_kernel(own, sib, w_all, out, held, sems):
    step = pl.program_id(0)
    y_low = lax.div(lax.axis_index("ctx"), Z_RING)

    def copy(chip):
        row = pl.multiple_of(lax.rem(y_low + chip // 4, 2) * 2 * CH, 2 * CH)
        part = w_all.at[pl.ds(chip % 4 * 2, 2), pl.ds(row, 2 * CH), :]
        return pltpu.make_async_copy(part, held.at[chip], sems.at[chip])

    for chip in range(CHIPS):

        @pl.when(step == 0)
        def _():
            copy(chip).start()

    for chip in range(CHIPS):

        @pl.when(step == chip)
        def _():
            copy(chip).wait()

    square = own[:, CH:].astype(F32) + sib[:, CH:].astype(F32)
    scale = lax.rsqrt((square[:, 0:1] + square[:, 64:65]) / (2.0 * CH) + NORM_EPS)
    values = jnp.concatenate([own[:, :CH], sib[:, :CH]], axis=1)
    rows = jnp.concatenate([held[step, 0], held[step, 1]], axis=1)
    out[0] = (dot(values, rows) * scale).astype(BF16)


def project(own, sib, w_all):
    whole = pl.BlockSpec(own.shape, lambda i: (0, 0))
    return pl.pallas_call(
        project_kernel,
        grid=(CHIPS,),
        in_specs=[whole, whole, pl.BlockSpec(memory_space=pltpu.HBM)],
        out_specs=pl.BlockSpec((1, ROWS, 256), lambda i: (i, 0, 0)),
        out_shape=jax.ShapeDtypeStruct((CHIPS, ROWS, 256), BF16),
        scratch_shapes=[
            pltpu.VMEM((CHIPS, 2, 2 * CH, 128), BF16),
            pltpu.SemaphoreType.DMA((CHIPS,)),
        ],
        compiler_params=params(57, True),
        cost_estimate=pl.CostEstimate(
            flops=8 * ROWS * CH * 2048, bytes_accessed=8 * 2**20, transcendentals=0
        ),
        name="project",
    )(own, sib, w_all)


def swapped(value, bit):
    return lax.ppermute(value, "tp", [(i, i ^ bit) for i in range(16)])


def next_ctx(value):
    return lax.ppermute(value, "ctx", [(i, i + 1) for i in range(15)])


def between_chips(value):
    same_core = [[2 * chip + core for chip in range(CHIPS)] for core in range(CORES)]
    return lax.all_to_all(value, "tp", 0, 0, axis_index_groups=same_core)


def between_slabs(value):
    return lax.all_to_all(value, "ctx", 0, 0)


def together(*values):
    return lax.optimization_barrier(values)


def pick(core, first, second):
    return jnp.where(core == 0, first, second)


def document_columns(seg_ids, ids_prior):
    ids_all = jnp.concatenate([ids_prior, seg_ids])
    prior = ids_prior[2]
    same = lambda a: (seg_ids == a).astype(F32)
    columns = [same(ids_all[tap : tap + ROWS]) for tap in range(CONV - 1)]
    columns += [same(prior), same(seg_ids[-1]), same(seg_ids[L - 1]), same(seg_ids[L - 1])]
    columns += [seg_ids.astype(F32)]
    cols = jnp.pad(jnp.stack(columns, axis=1), ((0, 0), (0, 128 - len(columns))))
    return cols, jnp.broadcast_to(seg_ids.astype(F32)[None], (8, ROWS))


def local(
    tokens,
    seg_ids,
    w_x,
    w_z,
    w_bc,
    w_dt,
    conv_x,
    conv_x_bias,
    conv_bc,
    conv_bc_bias,
    dt_bias,
    decay_rate,
    skip_gain,
    norm_weight,
    w_out,
):
    rank = lax.axis_index("tp")
    core = rank % CORES
    chip = rank // CORES

    w_cols = jnp.concatenate(
        [w_bc.T.reshape(CHIPS, 2 * N, FEAT), w_dt.T.reshape(CHIPS, 2 * HEADS, FEAT)], axis=1
    )
    ids_row = jnp.pad((seg_ids[-3:] + 1).astype(BF16), (0, FEAT - 3))[None]
    halo = next_ctx(jnp.concatenate([ids_row, tokens[1 - HALO :]], axis=0))
    ids_prior = halo[0, :3].astype(jnp.int32) - 1
    shared = jnp.concatenate([halo, tokens], axis=0)
    shared = jnp.broadcast_to(shared[None], (CHIPS, ALL_ROWS, FEAT))
    own = between_chips(jnp.concatenate([shared, w_cols], axis=1))

    halves = (w_out[:, :128], w_out[:, 128:])
    w_pair = jnp.concatenate(
        [pick(core, *halves), swapped(pick(core, halves[1], halves[0]), 1)], axis=0
    )
    w_far = lax.ppermute(w_pair, "ctx", [(i, i ^ Z_RING) for i in range(2 * Z_RING)])
    same_y = [list(range(Z_RING)), list(range(Z_RING, 2 * Z_RING))]
    w_both = jnp.concatenate([w_pair, w_far], axis=0)
    w_all = lax.all_gather(w_both, "ctx", axis=0, axis_index_groups=same_y)

    cols, seg_row = document_columns(seg_ids, ids_prior)
    taps_bc = lax.dynamic_slice_in_dim(conv_bc, chip * 2 * N, 2 * N, 1)
    bias_bc = lax.dynamic_slice_in_dim(conv_bc_bias, chip * 2 * N, 2 * N, 0)[None]
    skip = jnp.repeat(skip_gain, P_SIZE)[None]
    fixed = [cols, conv_x, conv_x_bias[None], taps_bc, bias_bc, dt_bias[None], decay_rate[None]]
    own, fixed, seg_row, skip = together(own, fixed, seg_row, skip)
    sib = swapped(own, 1)
    xc, bcc, hcol, hrow, s0, pay = scan_input(own, sib, w_x, fixed)
    own, sib, pay = together(own, sib, pay)
    pieces = between_slabs(pay)
    gates = gate(own, sib, w_z)
    pieces, gates, xc, bcc = together(pieces, gates, xc, bcc)
    state = between_slabs(prefix(pieces).reshape(CTX, 8, CH)).reshape(N, CH)
    y = intra(xc, bcc, hcol, hrow, s0, fixed[0], seg_row, skip)
    y, state, w_all = together(y, state, w_all)
    mine = join(y, gates, bcc, hcol, state, norm_weight[None])
    parts = between_chips(project(mine, swapped(mine, 1), w_all))
    total = jnp.sum(parts.astype(F32), axis=0).astype(BF16)
    parts = (total[:, :128], total[:, 128:])
    kept = pick(core, *parts)
    given = swapped(pick(core, parts[1], parts[0]), 1)
    return jnp.concatenate([pick(core, kept, given), pick(core, given, kept)], axis=1)


def solution(mesh):
    return jax.shard_map(
        local,
        mesh=mesh,
        in_specs=(
            P("ctx", "tp"),
            P("ctx"),
            P(None, "tp"),
            P(None, "tp"),
            P("tp", None),
            P("tp", None),
            P(None, "tp"),
            P("tp"),
            P(),
            P(),
            P("tp"),
            P("tp"),
            P("tp"),
            P("tp"),
            P("tp", "ctx"),
        ),
        out_specs=P("ctx", "tp"),
        check_vma=False,
    )
```

```python
import functools

import jax
import jax.numpy as jnp
from jax import lax
from jax.experimental import pallas as pl
from jax.experimental.pallas import tpu as pltpu
from jax.sharding import PartitionSpec as P

H = 128
P_SIZE = 64
N = 128
G = 8
L = 256
CONV = 4
HALO = 16
NORM_EPS = 1e-05
HIGHEST = lax.Precision.HIGHEST

CHIPS = 8
CORES = 2
HEADS = 8
CH = HEADS * P_SIZE
ROWS = 512
FEAT = 256
Z_RING = 8
CTX = 16
ALL_ROWS = HALO + ROWS
COLS = 2 * N + 2 * HEADS
VMEM = pl.BlockSpec(memory_space=pltpu.VMEM)
BF16 = jnp.bfloat16
F32 = jnp.float32


def params(mib, grid=False):
    more = {"dimension_semantics": ("arbitrary",)} if grid else {}
    return pltpu.CompilerParams(vmem_limit_bytes=mib * 2**20, **more)


def dot(a, b):
    return jnp.dot(a, b, preferred_element_type=F32)


def dot_nt(a, b):
    return lax.dot_general(a, b, (((1,), (1,)), ((), ())), preferred_element_type=F32)


def dot_tn(a, b):
    return lax.dot_general(a, b, (((0,), (0,)), ((), ())), preferred_element_type=F32)


def silu(v):
    return v / (1.0 + jnp.exp(-v))


def spread(cols, first=0, count=HEADS):
    shape = (HEADS, count * P_SIZE)
    head = lax.broadcasted_iota(jnp.int32, shape, 0)
    lane = lax.broadcasted_iota(jnp.int32, shape, 1)
    pick = (head == lane // P_SIZE + first).astype(F32)
    return jnp.dot(cols, pick, precision=HIGHEST, preferred_element_type=F32)


def my_core():
    return lax.rem(lax.axis_index("tp"), CORES)


def add_to(acc, step, value):
    @pl.when(step == 0)
    def _():
        acc[...] = value

    @pl.when(step > 0)
    def _():
        acc[...] += value


def conv_chunk(raw, at, rows, masks, taps, offsets):
    total = offsets + taps[CONV - 1 : CONV, :] * raw[at + HALO : at + HALO + rows, :]
    for tap in range(CONV - 1):
        first = at + HALO - (CONV - 1) + tap
        shifted = raw[first : first + rows, :]
        total = total + taps[tap : tap + 1, :] * (shifted * masks[:, tap : tap + 1])
    return silu(total).astype(BF16)


def rounded(ref):
    ref[...] = ref[...].astype(BF16).astype(F32)


def step_sources():
    for slot in range(2):
        for same_core in (True, False):
            yield slot, same_core


def step_tokens(own, sib, first=0):
    refs = [(own if same_core else sib, slot) for slot, same_core in step_sources()]
    return jnp.concatenate([ref[slot, first:ALL_ROWS] for ref, slot in refs], axis=1)


def step_cols(own, sib):
    refs = [(own if same_core else sib, slot) for slot, same_core in step_sources()]
    return jnp.concatenate([ref[slot, ALL_ROWS:] for ref, slot in refs], axis=1)


def step_rows(w_ref):
    core = my_core()
    parts = []
    for slot, same_core in step_sources():
        from_core = core if same_core else 1 - core
        at = pl.multiple_of((slot * CORES + from_core) * FEAT, FEAT)
        parts.append(w_ref[pl.ds(at, FEAT), :])
    return jnp.concatenate(parts, axis=0)


def scan_input_kernel(
    own,
    sib,
    w_x,
    cols,
    taps_x,
    bias_x,
    taps_bc,
    bias_bc,
    dt_bias,
    decay,
    xc,
    bcc,
    hcol,
    hrow,
    s0,
    pay,
    acc_x,
    acc_bc,
    raw_bc,
):
    step = pl.program_id(0)
    core = my_core()
    toks = step_tokens(own, sib)
    add_to(acc_x, step, dot(toks, step_rows(w_x)))
    add_to(acc_bc, step, dot_nt(toks, step_cols(own, sib)))

    @pl.when(step == pl.num_programs(0) - 1)
    def _():
        raw_dt = acc_bc[HALO:, 2 * N :]
        raw_dt = jnp.where(core == 0, raw_dt[:, :HEADS], raw_dt[:, HEADS:])
        pre = raw_dt + dt_bias[...]
        dt = jnp.maximum(pre, 0.0) + jnp.log1p(jnp.exp(-jnp.abs(pre)))
        loga = -decay[...] * dt
        acc_x[...] = acc_x[...].astype(BF16).astype(F32)
        raw_bc[...] = acc_bc[:, : 2 * N].astype(BF16).astype(F32)
        for at in range(0, ROWS, 64):
            masks = cols[at : at + 64, :]
            xc[at : at + 64, :] = conv_chunk(acc_x, at, 64, masks, taps_x, bias_x[...])
            bcc[at : at + 64, :] = conv_chunk(raw_bc, at, 64, masks, taps_bc, bias_bc[...])
        lower = (
            lax.broadcasted_iota(jnp.int32, (L, L), 0) >= lax.broadcasted_iota(jnp.int32, (L, L), 1)
        ).astype(F32)
        cum0 = jnp.dot(lower, loga[:L], precision=HIGHEST, preferred_element_type=F32)
        cum1 = jnp.dot(lower, loga[L:], precision=HIGHEST, preferred_element_type=F32)
        end0, end1 = cum0[L - 1 :], cum1[L - 1 :]
        slab = jnp.exp(jnp.concatenate([cum0, cum1 + end0], axis=0)) * cols[:, 3:4]
        inner = jnp.exp(cum1) * cols[L:, 5:6]
        tail0 = jnp.exp(end0 - cum0) * cols[:L, 6:7] * dt[:L]
        tail1 = jnp.exp(end1 - cum1) * cols[L:, 4:5] * dt[L:]
        cum = jnp.concatenate([cum0, cum1], axis=0)
        blank = jnp.zeros((ROWS, 128 - 4 * HEADS), F32)
        wide = jnp.concatenate(
            [cum, dt, slab, jnp.concatenate([inner, inner], axis=0), blank], axis=1
        )
        hcol[...] = wide
        hrow[...] = wide.T[: 2 * HEADS]
        scaled0 = (xc[:L, :].astype(F32) * spread(tail0)).astype(BF16)
        scaled1 = (xc[L:, :].astype(F32) * spread(tail1)).astype(BF16)
        state0 = dot_tn(bcc[:L, :N], scaled0)
        state1 = dot_tn(bcc[L:, :N], scaled1)
        s0[...] = state0.astype(BF16)
        ends = jnp.concatenate(
            [inner[L - 1 :], slab[ROWS - 1 :], jnp.zeros((6, HEADS), F32)], axis=0
        )
        ends = spread(ends)
        final = ends[0:1] * state0 + state1
        factor = factor_rows(ends[1:2])
        for piece in range(CTX):
            part = final[8 * piece : 8 * piece + 8]
            pay[piece] = jnp.concatenate([part, factor], axis=0).astype(BF16)


def factor_rows(factor):
    high = factor.astype(BF16).astype(F32)
    row = lax.broadcasted_iota(jnp.int32, (8, CH), 0)
    return jnp.where(row == 0, high, jnp.where(row == 1, factor - high, 0.0))


def over_chips(kernel, blocked, fixed, shapes, scratch, mib, flops, name):
    whole = lambda a: pl.BlockSpec(a.shape, lambda i: (0,) * len(a.shape))
    return pl.pallas_call(
        kernel,
        grid=(CHIPS // 2,),
        in_specs=[spec for _, spec in blocked] + [whole(a) for a in fixed],
        out_specs=[whole(a) for a in shapes],
        out_shape=[pltpu.HBM(a.shape, a.dtype) for a in shapes],
        scratch_shapes=scratch,
        compiler_params=params(mib, True),
        cost_estimate=pl.CostEstimate(
            flops=flops, bytes_accessed=8 * 2**20, transcendentals=10**6
        ),
        name=name,
    )(*[a for a, _ in blocked], *fixed)


def two_chips(a, rows):
    return a, pl.BlockSpec((2, rows, FEAT), lambda i: (i, 0, 0))


def their_rows(w):
    return w, pl.BlockSpec((4 * FEAT, CH), lambda i: (i, 0))


def scan_input(own, sib, w_x, fixed):
    shapes = [
        jax.ShapeDtypeStruct((ROWS, CH), BF16),
        jax.ShapeDtypeStruct((ROWS, 2 * N), BF16),
        jax.ShapeDtypeStruct((ROWS, 128), F32),
        jax.ShapeDtypeStruct((2 * HEADS, ROWS), F32),
        jax.ShapeDtypeStruct((N, CH), BF16),
        jax.ShapeDtypeStruct((CTX, 16, CH), BF16),
    ]
    blocked = [two_chips(a, ALL_ROWS + COLS) for a in (own, sib)]
    blocked += [their_rows(w_x)]
    scratch = [
        pltpu.VMEM((ALL_ROWS, CH), F32),
        pltpu.VMEM((ALL_ROWS, COLS), F32),
        pltpu.VMEM((ALL_ROWS, 2 * N), F32),
    ]
    flops = 2 * ALL_ROWS * 4096 * (CH + COLS)
    return over_chips(
        scan_input_kernel, blocked, fixed, shapes, scratch, 22, flops, "scan_input"
    )


def gate_kernel(own, sib, w_z, gates, acc):
    step = pl.program_id(0)
    add_to(acc, step, dot(step_tokens(own, sib, HALO), step_rows(w_z)))

    @pl.when(step == pl.num_programs(0) - 1)
    def _():
        for at in range(0, ROWS, 64):
            gates[at : at + 64, :] = silu(acc[at : at + 64, :].astype(BF16).astype(F32))


def gate(own, sib, w_z):
    shapes = [jax.ShapeDtypeStruct((ROWS, CH), F32)]
    blocked = [two_chips(a, ALL_ROWS) for a in (own, sib)] + [their_rows(w_z)]
    scratch = [pltpu.VMEM((ROWS, CH), F32)]
    flops = 2 * ROWS * 4096 * CH
    return over_chips(gate_kernel, blocked, [], shapes, scratch, 16, flops, "gate")[0]


def intra_kernel(xc, bcc, hcol, hrow, s0, cols, seg_row, skip, y):
    for block in range(2):
        intra_block(block * L, xc, bcc, hcol, hrow, s0, cols, seg_row, skip, y)


def intra_block(at, xc, bcc, hcol, hrow, s0, cols, seg_row, skip, y):
    b_vals, c_vals = bcc[at : at + L, :N], bcc[at : at + L, N:]
    after = lax.broadcasted_iota(jnp.int32, (L, L), 0) >= lax.broadcasted_iota(
        jnp.int32, (L, L), 1
    )
    same = cols[at : at + L, 7:8] == seg_row[0:1, at : at + L]
    scores = jnp.where(after & same, dot_nt(c_vals, b_vals), 0.0)
    for half in range(2):
        lanes = slice(half * 256, half * 256 + 256)
        weights, values = [], []
        x_half = xc[at : at + L, lanes]
        head_of = lax.broadcasted_iota(jnp.int32, (1, 256), 1) // P_SIZE
        for part in range(4):
            head = half * 4 + part
            gap = hcol[at : at + L, head : head + 1] - hrow[head : head + 1, at : at + L]
            decay = jnp.exp(jnp.minimum(gap, 0.0))
            dt_row = hrow[HEADS + head : HEADS + head + 1, at : at + L]
            weights.append((scores * decay * dt_row).astype(BF16))
            values.append(x_half * (head_of == part).astype(BF16))
        out = dot(jnp.concatenate(weights, axis=1), jnp.concatenate(values, axis=0))
        out = out + skip[:, lanes] * x_half.astype(F32)
        if at:
            carried = spread(hcol[at : at + L, 3 * HEADS : 4 * HEADS], half * 4, 4)
            out = out + carried * dot(c_vals, s0[:, lanes])
        y[at : at + L, lanes] = out


def intra(*args):
    return pl.pallas_call(
        intra_kernel,
        in_specs=[VMEM] * len(args),
        out_specs=VMEM,
        out_shape=jax.ShapeDtypeStruct((ROWS, CH), F32),
        compiler_params=params(12),
        cost_estimate=pl.CostEstimate(
            flops=2 * ROWS * L * CH * 4, bytes_accessed=4 * 2**20, transcendentals=2 * 10**6
        ),
        name="intra",
    )(*args)


def prefix_kernel(pieces, out):
    total = jnp.zeros((8, CH), F32)
    for pair in range(8):
        held = []
        for place in (2 * pair, 2 * pair + 1):
            held.append(total)
            piece = pieces[place].astype(F32)
            total = total * (piece[8:9] + piece[9:10]) + piece[:8]
        out[16 * pair : 16 * pair + 16, :] = jnp.concatenate(held, axis=0).astype(BF16)


def prefix(pieces):
    return pl.pallas_call(
        prefix_kernel,
        in_specs=[VMEM],
        out_specs=VMEM,
        out_shape=jax.ShapeDtypeStruct((N, CH), BF16),
        compiler_params=params(8),
        name="prefix",
    )(pieces)


def join_kernel(y, gates, bcc, hcol, state, gain, out):
    for at in range(0, ROWS, 128):
        c_vals = bcc[at : at + 128, N:]
        carried = spread(hcol[at : at + 128, 2 * HEADS : 3 * HEADS])
        total = y[at : at + 128, :] + carried * dot(c_vals, state[...])
        gated = total * gates[at : at + 128, :]
        square = jnp.sum(gated * gated, axis=1, keepdims=True)
        high = square.astype(BF16).astype(F32)
        lane = lax.broadcasted_iota(jnp.int32, (128, 128), 1)
        out[at : at + 128, :CH] = (gated * gain[...]).astype(BF16)
        out[at : at + 128, CH:] = jnp.where(lane < 64, high, square - high).astype(BF16)


def join(*args):
    return pl.pallas_call(
        join_kernel,
        in_specs=[VMEM] * len(args),
        out_specs=VMEM,
        out_shape=jax.ShapeDtypeStruct((ROWS, CH + 128), BF16),
        compiler_params=params(12),
        cost_estimate=pl.CostEstimate(
            flops=2 * ROWS * N * CH, bytes_accessed=4 * 2**20, transcendentals=0
        ),
        name="join",
    )(*args)


def project_kernel(place, own, sib, w, out):
    del place
    square = own[:, CH:].astype(F32) + sib[:, CH:].astype(F32)
    scale = lax.rsqrt((square[:, 0:1] + square[:, 64:65]) / (2.0 * CH) + NORM_EPS)
    values = jnp.concatenate([own[:, :CH], sib[:, :CH]], axis=1)
    rows = jnp.concatenate([w[0], w[1]], axis=1)
    out[0] = (dot(values, rows) * scale).astype(BF16)


def project(own, sib, w_all, y_low):
    def columns(chip, place):
        return lax.rem(chip, 4), lax.rem(lax.div(chip, 4) + place[0], 2), 0

    whole = pl.BlockSpec(own.shape, lambda i, place: (0, 0))
    return pl.pallas_call(
        project_kernel,
        grid_spec=pltpu.PrefetchScalarGridSpec(
            num_scalar_prefetch=1,
            grid=(CHIPS,),
            in_specs=[whole, whole, pl.BlockSpec((2, 2 * CH, 128), columns)],
            out_specs=pl.BlockSpec((1, ROWS, 256), lambda i, place: (i, 0, 0)),
        ),
        out_shape=jax.ShapeDtypeStruct((CHIPS, ROWS, 256), BF16),
        compiler_params=params(14, True),
        cost_estimate=pl.CostEstimate(
            flops=8 * ROWS * CH * 2048, bytes_accessed=8 * 2**20, transcendentals=0
        ),
        name="project",
    )(y_low[None], own, sib, w_all)


def swapped(value, bit):
    return lax.ppermute(value, "tp", [(i, i ^ bit) for i in range(16)])


def next_ctx(value):
    return lax.ppermute(value, "ctx", [(i, i + 1) for i in range(15)])


def between_chips(value):
    same_core = [[2 * chip + core for chip in range(CHIPS)] for core in range(CORES)]
    return lax.all_to_all(value, "tp", 0, 0, axis_index_groups=same_core)


def along_z(value, steps):
    pairs = [(i, i // Z_RING * Z_RING + (i + steps) % Z_RING) for i in range(CTX)]
    return lax.ppermute(value, "ctx", pairs)


def gathered_along_z(mine):
    rows, lanes = mine.shape
    z_place = lax.axis_index("ctx") % Z_RING
    held = jnp.zeros((Z_RING, rows, lanes), mine.dtype)

    def put(held, piece, distance, row=0):
        at = ((z_place + distance) % Z_RING, row, 0)
        return lax.dynamic_update_slice(held, piece[None], at)

    held = put(held, mine, 0)
    above, below = mine, mine
    for distance in range(1, Z_RING // 2):
        below, above = along_z(below, 1), along_z(above, -1)
        held = put(put(held, below, -distance), above, distance)
    half = rows // 2
    below, above = along_z(below[:half], 1), along_z(above[half:], -1)
    return put(put(held, below, Z_RING // 2), above, Z_RING // 2, half)


def between_slabs(value):
    return lax.all_to_all(value, "ctx", 0, 0)


def together(*values):
    return lax.optimization_barrier(values)


def pick(core, first, second):
    return jnp.where(core == 0, first, second)


def document_columns(seg_ids, ids_prior):
    ids_all = jnp.concatenate([ids_prior, seg_ids])
    prior = ids_prior[2]
    same = lambda a: (seg_ids == a).astype(F32)
    columns = [same(ids_all[tap : tap + ROWS]) for tap in range(CONV - 1)]
    columns += [same(prior), same(seg_ids[-1]), same(seg_ids[L - 1]), same(seg_ids[L - 1])]
    columns += [seg_ids.astype(F32)]
    cols = jnp.pad(jnp.stack(columns, axis=1), ((0, 0), (0, 128 - len(columns))))
    return cols, jnp.broadcast_to(seg_ids.astype(F32)[None], (8, ROWS))


def local(
    tokens,
    seg_ids,
    w_x,
    w_z,
    w_bc,
    w_dt,
    conv_x,
    conv_x_bias,
    conv_bc,
    conv_bc_bias,
    dt_bias,
    decay_rate,
    skip_gain,
    norm_weight,
    w_out,
):
    rank = lax.axis_index("tp")
    core = rank % CORES
    chip = rank // CORES
    y_low = (lax.axis_index("ctx") // Z_RING).astype(jnp.int32)

    w_cols = jnp.concatenate(
        [w_bc.T.reshape(CHIPS, 2 * N, FEAT), w_dt.T.reshape(CHIPS, 2 * HEADS, FEAT)], axis=1
    )
    ids_row = jnp.pad((seg_ids[-3:] + 1).astype(BF16), (0, FEAT - 3))[None]
    halo = next_ctx(jnp.concatenate([ids_row, tokens[1 - HALO :]], axis=0))
    ids_prior = halo[0, :3].astype(jnp.int32) - 1
    shared = jnp.concatenate([halo, tokens], axis=0)
    shared = jnp.broadcast_to(shared[None], (CHIPS, ALL_ROWS, FEAT))
    sent = jnp.concatenate([shared, w_cols], axis=1)
    sent, w_out = together(sent, w_out)
    own = between_chips(sent)

    halves = (w_out[:, :128], w_out[:, 128:])
    w_pair = jnp.concatenate(
        [pick(core, *halves), swapped(pick(core, halves[1], halves[0]), 1)], axis=0
    )
    w_far = lax.ppermute(w_pair, "ctx", [(i, i ^ Z_RING) for i in range(2 * Z_RING)])
    w_all = gathered_along_z(jnp.concatenate([w_pair, w_far], axis=0))

    cols, seg_row = document_columns(seg_ids, ids_prior)
    taps_bc = lax.dynamic_slice_in_dim(conv_bc, chip * 2 * N, 2 * N, 1)
    bias_bc = lax.dynamic_slice_in_dim(conv_bc_bias, chip * 2 * N, 2 * N, 0)[None]
    skip = jnp.repeat(skip_gain, P_SIZE)[None]
    fixed = [cols, conv_x, conv_x_bias[None], taps_bc, bias_bc, dt_bias[None], decay_rate[None]]
    own, w_all, fixed, seg_row, skip = together(own, w_all, fixed, seg_row, skip)
    sib = swapped(own, 1)
    xc, bcc, hcol, hrow, s0, pay = scan_input(own, sib, w_x, fixed)
    own, sib, pay = together(own, sib, pay)
    pieces = between_slabs(pay)
    gates = gate(own, sib, w_z)
    pieces, gates, xc, bcc = together(pieces, gates, xc, bcc)
    state = between_slabs(prefix(pieces).reshape(CTX, 8, CH)).reshape(N, CH)
    y = intra(xc, bcc, hcol, hrow, s0, fixed[0], seg_row, skip)
    mine = join(y, gates, bcc, hcol, state, norm_weight[None])
    parts = between_chips(project(mine, swapped(mine, 1), w_all, y_low))
    total = jnp.sum(parts.astype(F32), axis=0).astype(BF16)
    parts = (total[:, :128], total[:, 128:])
    kept = pick(core, *parts)
    given = swapped(pick(core, parts[1], parts[0]), 1)
    return jnp.concatenate([pick(core, kept, given), pick(core, given, kept)], axis=1)


def solution(mesh):
    return jax.shard_map(
        local,
        mesh=mesh,
        in_specs=(
            P("ctx", "tp"),
            P("ctx"),
            P(None, "tp"),
            P(None, "tp"),
            P("tp", None),
            P("tp", None),
            P(None, "tp"),
            P("tp"),
            P(),
            P(),
            P("tp"),
            P("tp"),
            P("tp"),
            P("tp"),
            P("tp", "ctx"),
        ),
        out_specs=P("ctx", "tp"),
        check_vma=False,
    )
```

```python
import functools

import jax
import jax.numpy as jnp
from jax import lax
from jax.experimental import pallas as pl
from jax.experimental.pallas import tpu as pltpu
from jax.sharding import PartitionSpec as P

H = 128
P_SIZE = 64
N = 128
G = 8
L = 256
CONV = 4
HALO = 16
NORM_EPS = 1e-05
HIGHEST = lax.Precision.HIGHEST

CHIPS = 8
CORES = 2
HEADS = 8
CH = HEADS * P_SIZE
ROWS = 512
FEAT = 256
Z_RING = 8
CTX = 16
ALL_ROWS = HALO + ROWS
COLS = 2 * N + 2 * HEADS
VMEM = pl.BlockSpec(memory_space=pltpu.VMEM)
BF16 = jnp.bfloat16
F32 = jnp.float32


def params(mib, grid=False):
    more = {"dimension_semantics": ("arbitrary",)} if grid else {}
    return pltpu.CompilerParams(vmem_limit_bytes=mib * 2**20, **more)


def dot(a, b):
    return jnp.dot(a, b, preferred_element_type=F32)


def dot_nt(a, b):
    return lax.dot_general(a, b, (((1,), (1,)), ((), ())), preferred_element_type=F32)


def dot_tn(a, b):
    return lax.dot_general(a, b, (((0,), (0,)), ((), ())), preferred_element_type=F32)


def silu(v):
    return v / (1.0 + jnp.exp(-v))


def spread(cols, first=0, count=HEADS):
    shape = (HEADS, count * P_SIZE)
    head = lax.broadcasted_iota(jnp.int32, shape, 0)
    lane = lax.broadcasted_iota(jnp.int32, shape, 1)
    pick = (head == lane // P_SIZE + first).astype(F32)
    return jnp.dot(cols, pick, precision=HIGHEST, preferred_element_type=F32)


def my_core():
    return lax.rem(lax.axis_index("tp"), CORES)


def add_to(acc, step, value):
    @pl.when(step == 0)
    def _():
        acc[...] = value

    @pl.when(step > 0)
    def _():
        acc[...] += value


def conv_chunk(raw, at, rows, masks, taps, offsets):
    total = offsets + taps[CONV - 1 : CONV, :] * raw[at + HALO : at + HALO + rows, :]
    for tap in range(CONV - 1):
        first = at + HALO - (CONV - 1) + tap
        shifted = raw[first : first + rows, :]
        total = total + taps[tap : tap + 1, :] * (shifted * masks[:, tap : tap + 1])
    return silu(total).astype(BF16)


def rounded(ref):
    ref[...] = ref[...].astype(BF16).astype(F32)


def step_sources():
    for slot in range(2):
        for same_core in (True, False):
            yield slot, same_core


def step_tokens(own, sib, first=0):
    refs = [(own if same_core else sib, slot) for slot, same_core in step_sources()]
    return jnp.concatenate([ref[slot, first:ALL_ROWS] for ref, slot in refs], axis=1)


def step_cols(own, sib):
    refs = [(own if same_core else sib, slot) for slot, same_core in step_sources()]
    return jnp.concatenate([ref[slot, ALL_ROWS:] for ref, slot in refs], axis=1)


def step_rows(w_ref):
    core = my_core()
    parts = []
    for slot, same_core in step_sources():
        from_core = core if same_core else 1 - core
        at = pl.multiple_of((slot * CORES + from_core) * FEAT, FEAT)
        parts.append(w_ref[pl.ds(at, FEAT), :])
    return jnp.concatenate(parts, axis=0)


def scan_input_kernel(
    own,
    sib,
    w_x,
    cols,
    taps_x,
    bias_x,
    taps_bc,
    bias_bc,
    dt_bias,
    decay,
    xc,
    bcc,
    hcol,
    hrow,
    s0,
    pay,
    acc_x,
    acc_bc,
    raw_bc,
):
    step = pl.program_id(0)
    core = my_core()
    toks = step_tokens(own, sib)
    add_to(acc_x, step, dot(toks, step_rows(w_x)))
    add_to(acc_bc, step, dot_nt(toks, step_cols(own, sib)))

    @pl.when(step == pl.num_programs(0) - 1)
    def _():
        raw_dt = acc_bc[HALO:, 2 * N :]
        raw_dt = jnp.where(core == 0, raw_dt[:, :HEADS], raw_dt[:, HEADS:])
        pre = raw_dt + dt_bias[...]
        dt = jnp.maximum(pre, 0.0) + jnp.log1p(jnp.exp(-jnp.abs(pre)))
        loga = -decay[...] * dt
        acc_x[...] = acc_x[...].astype(BF16).astype(F32)
        raw_bc[...] = acc_bc[:, : 2 * N].astype(BF16).astype(F32)
        for at in range(0, ROWS, 64):
            masks = cols[at : at + 64, :]
            xc[at : at + 64, :] = conv_chunk(acc_x, at, 64, masks, taps_x, bias_x[...])
            bcc[at : at + 64, :] = conv_chunk(raw_bc, at, 64, masks, taps_bc, bias_bc[...])
        lower = (
            lax.broadcasted_iota(jnp.int32, (L, L), 0) >= lax.broadcasted_iota(jnp.int32, (L, L), 1)
        ).astype(F32)
        cum0 = jnp.dot(lower, loga[:L], precision=HIGHEST, preferred_element_type=F32)
        cum1 = jnp.dot(lower, loga[L:], precision=HIGHEST, preferred_element_type=F32)
        end0, end1 = cum0[L - 1 :], cum1[L - 1 :]
        slab = jnp.exp(jnp.concatenate([cum0, cum1 + end0], axis=0)) * cols[:, 3:4]
        inner = jnp.exp(cum1) * cols[L:, 5:6]
        tail0 = jnp.exp(end0 - cum0) * cols[:L, 6:7] * dt[:L]
        tail1 = jnp.exp(end1 - cum1) * cols[L:, 4:5] * dt[L:]
        cum = jnp.concatenate([cum0, cum1], axis=0)
        blank = jnp.zeros((ROWS, 128 - 4 * HEADS), F32)
        wide = jnp.concatenate(
            [cum, dt, slab, jnp.concatenate([inner, inner], axis=0), blank], axis=1
        )
        hcol[...] = wide
        hrow[...] = wide.T[: 2 * HEADS]
        scaled0 = (xc[:L, :].astype(F32) * spread(tail0)).astype(BF16)
        scaled1 = (xc[L:, :].astype(F32) * spread(tail1)).astype(BF16)
        state0 = dot_tn(bcc[:L, :N], scaled0)
        state1 = dot_tn(bcc[L:, :N], scaled1)
        s0[...] = state0.astype(BF16)
        ends = jnp.concatenate(
            [inner[L - 1 :], slab[ROWS - 1 :], jnp.zeros((6, HEADS), F32)], axis=0
        )
        ends = spread(ends)
        final = ends[0:1] * state0 + state1
        factor = factor_rows(ends[1:2])
        for piece in range(CTX):
            part = final[8 * piece : 8 * piece + 8]
            pay[piece] = jnp.concatenate([part, factor], axis=0).astype(BF16)


def factor_rows(factor):
    high = factor.astype(BF16).astype(F32)
    row = lax.broadcasted_iota(jnp.int32, (8, CH), 0)
    return jnp.where(row == 0, high, jnp.where(row == 1, factor - high, 0.0))


def over_chips(kernel, blocked, fixed, shapes, scratch, mib, flops, name):
    whole = lambda a: pl.BlockSpec(a.shape, lambda i: (0,) * len(a.shape))
    return pl.pallas_call(
        kernel,
        grid=(CHIPS // 2,),
        in_specs=[spec for _, spec in blocked] + [whole(a) for a in fixed],
        out_specs=[whole(a) for a in shapes],
        out_shape=[pltpu.HBM(a.shape, a.dtype) for a in shapes],
        scratch_shapes=scratch,
        compiler_params=params(mib, True),
        cost_estimate=pl.CostEstimate(
            flops=flops, bytes_accessed=8 * 2**20, transcendentals=10**6
        ),
        name=name,
    )(*[a for a, _ in blocked], *fixed)


def two_chips(a, rows):
    return a, pl.BlockSpec((2, rows, FEAT), lambda i: (i, 0, 0))


def their_rows(w):
    return w, pl.BlockSpec((4 * FEAT, CH), lambda i: (i, 0))


def scan_input(own, sib, w_x, fixed):
    shapes = [
        jax.ShapeDtypeStruct((ROWS, CH), BF16),
        jax.ShapeDtypeStruct((ROWS, 2 * N), BF16),
        jax.ShapeDtypeStruct((ROWS, 128), F32),
        jax.ShapeDtypeStruct((2 * HEADS, ROWS), F32),
        jax.ShapeDtypeStruct((N, CH), BF16),
        jax.ShapeDtypeStruct((CTX, 16, CH), BF16),
    ]
    blocked = [two_chips(a, ALL_ROWS + COLS) for a in (own, sib)]
    blocked += [their_rows(w_x)]
    scratch = [
        pltpu.VMEM((ALL_ROWS, CH), F32),
        pltpu.VMEM((ALL_ROWS, COLS), F32),
        pltpu.VMEM((ALL_ROWS, 2 * N), F32),
    ]
    flops = 2 * ALL_ROWS * 4096 * (CH + COLS)
    return over_chips(
        scan_input_kernel, blocked, fixed, shapes, scratch, 22, flops, "scan_input"
    )


def gate_kernel(own, sib, w_z, gates, acc):
    step = pl.program_id(0)
    add_to(acc, step, dot(step_tokens(own, sib, HALO), step_rows(w_z)))

    @pl.when(step == pl.num_programs(0) - 1)
    def _():
        for at in range(0, ROWS, 64):
            gates[at : at + 64, :] = silu(acc[at : at + 64, :].astype(BF16).astype(F32))


def gate(own, sib, w_z):
    shapes = [jax.ShapeDtypeStruct((ROWS, CH), F32)]
    blocked = [two_chips(a, ALL_ROWS) for a in (own, sib)] + [their_rows(w_z)]
    scratch = [pltpu.VMEM((ROWS, CH), F32)]
    flops = 2 * ROWS * 4096 * CH
    return over_chips(gate_kernel, blocked, [], shapes, scratch, 16, flops, "gate")[0]


def intra_kernel(xc, bcc, hcol, hrow, s0, cols, seg_row, skip, y, c_out, decays):
    c_out[...] = bcc[:, N:]
    decays[...] = hcol[...]
    for block in range(2):
        intra_block(block * L, xc, bcc, hcol, hrow, s0, cols, seg_row, skip, y)


def intra_block(at, xc, bcc, hcol, hrow, s0, cols, seg_row, skip, y):
    b_vals, c_vals = bcc[at : at + L, :N], bcc[at : at + L, N:]
    after = lax.broadcasted_iota(jnp.int32, (L, L), 0) >= lax.broadcasted_iota(
        jnp.int32, (L, L), 1
    )
    same = cols[at : at + L, 7:8] == seg_row[0:1, at : at + L]
    scores = jnp.where(after & same, dot_nt(c_vals, b_vals), 0.0)
    for half in range(2):
        lanes = slice(half * 256, half * 256 + 256)
        weights, values = [], []
        x_half = xc[at : at + L, lanes]
        head_of = lax.broadcasted_iota(jnp.int32, (1, 256), 1) // P_SIZE
        for part in range(4):
            head = half * 4 + part
            gap = hcol[at : at + L, head : head + 1] - hrow[head : head + 1, at : at + L]
            decay = jnp.exp(jnp.minimum(gap, 0.0))
            dt_row = hrow[HEADS + head : HEADS + head + 1, at : at + L]
            weights.append((scores * decay * dt_row).astype(BF16))
            values.append(x_half * (head_of == part).astype(BF16))
        out = dot(jnp.concatenate(weights, axis=1), jnp.concatenate(values, axis=0))
        out = out + skip[:, lanes] * x_half.astype(F32)
        if at:
            carried = spread(hcol[at : at + L, 3 * HEADS : 4 * HEADS], half * 4, 4)
            out = out + carried * dot(c_vals, s0[:, lanes])
        y[at : at + L, lanes] = out


def intra(*args):
    shapes = [((ROWS, CH), F32), ((ROWS, N), BF16), ((ROWS, 128), F32)]
    return pl.pallas_call(
        intra_kernel,
        in_specs=[VMEM] * len(args),
        out_specs=[VMEM] * len(shapes),
        out_shape=[jax.ShapeDtypeStruct(*shape) for shape in shapes],
        compiler_params=params(12),
        cost_estimate=pl.CostEstimate(
            flops=2 * ROWS * L * CH * 4, bytes_accessed=4 * 2**20, transcendentals=2 * 10**6
        ),
        name="intra",
    )(*args)


def prefix_kernel(pieces, out):
    total = jnp.zeros((8, CH), F32)
    for pair in range(8):
        held = []
        for place in (2 * pair, 2 * pair + 1):
            held.append(total)
            piece = pieces[place].astype(F32)
            total = total * (piece[8:9] + piece[9:10]) + piece[:8]
        out[16 * pair : 16 * pair + 16, :] = jnp.concatenate(held, axis=0).astype(BF16)


def prefix(pieces):
    return pl.pallas_call(
        prefix_kernel,
        in_specs=[VMEM],
        out_specs=VMEM,
        out_shape=jax.ShapeDtypeStruct((N, CH), BF16),
        compiler_params=params(8),
        name="prefix",
    )(pieces)


def join_kernel(y, gates, cc, hcol, state, gain, out):
    for at in range(0, ROWS, 128):
        c_vals = cc[at : at + 128, :]
        carried = spread(hcol[at : at + 128, 2 * HEADS : 3 * HEADS])
        total = y[at : at + 128, :] + carried * dot(c_vals, state[...])
        gated = total * gates[at : at + 128, :]
        square = jnp.sum(gated * gated, axis=1, keepdims=True)
        high = square.astype(BF16).astype(F32)
        lane = lax.broadcasted_iota(jnp.int32, (128, 128), 1)
        out[at : at + 128, :CH] = (gated * gain[...]).astype(BF16)
        out[at : at + 128, CH:] = jnp.where(lane < 64, high, square - high).astype(BF16)


def join(*args):
    return pl.pallas_call(
        join_kernel,
        in_specs=[VMEM] * len(args),
        out_specs=VMEM,
        out_shape=jax.ShapeDtypeStruct((ROWS, CH + 128), BF16),
        compiler_params=params(12),
        cost_estimate=pl.CostEstimate(
            flops=2 * ROWS * N * CH, bytes_accessed=4 * 2**20, transcendentals=0
        ),
        name="join",
    )(*args)


def project_kernel(place, own, sib, near, far, out):
    del place
    square = own[:, CH:].astype(F32) + sib[:, CH:].astype(F32)
    scale = lax.rsqrt((square[:, 0:1] + square[:, 64:65]) / (2.0 * CH) + NORM_EPS)
    values = jnp.concatenate([own[:, :CH], sib[:, :CH]], axis=1)
    is_near = pl.program_id(0) < CHIPS // 2
    for wanted, ref in ((is_near, near), (jnp.logical_not(is_near), far)):

        @pl.when(wanted)
        def _():
            rows = jnp.concatenate([ref[0], ref[1]], axis=1)
            out[0] = (dot(values, rows) * scale).astype(BF16)


def project(own, sib, near, far, y_low):
    half = CHIPS // 2
    whole = pl.BlockSpec(own.shape, lambda i, place: (0, 0))
    columns = lambda at: pl.BlockSpec((2, 2 * CH, 128), at)

    def sent(i, place):
        return lax.rem(i, half) + half * lax.rem(lax.div(i, half) + place[0], 2), 0, 0

    return pl.pallas_call(
        project_kernel,
        grid_spec=pltpu.PrefetchScalarGridSpec(
            num_scalar_prefetch=1,
            grid=(CHIPS,),
            in_specs=[
                whole,
                whole,
                columns(lambda i, place: (jnp.minimum(i, half - 1), 0, 0)),
                columns(lambda i, place: (jnp.maximum(i - half, 0), 0, 0)),
            ],
            out_specs=pl.BlockSpec((1, ROWS, 256), sent),
        ),
        out_shape=jax.ShapeDtypeStruct((CHIPS, ROWS, 256), BF16),
        compiler_params=params(14, True),
        cost_estimate=pl.CostEstimate(
            flops=8 * ROWS * CH * 2048, bytes_accessed=8 * 2**20, transcendentals=0
        ),
        name="project",
    )(y_low[None], own, sib, near, far)


def swapped(value, bit):
    return lax.ppermute(value, "tp", [(i, i ^ bit) for i in range(16)])


def next_ctx(value):
    return lax.ppermute(value, "ctx", [(i, i + 1) for i in range(15)])


def between_chips(value):
    same_core = [[2 * chip + core for chip in range(CHIPS)] for core in range(CORES)]
    return lax.all_to_all(value, "tp", 0, 0, axis_index_groups=same_core)


def along_z(value, steps):
    pairs = [(i, i // Z_RING * Z_RING + (i + steps) % Z_RING) for i in range(CTX)]
    return lax.ppermute(value, "ctx", pairs)


def gathered_along_z(mine):
    rows, lanes = mine.shape
    z_place = lax.axis_index("ctx") % Z_RING
    held = jnp.zeros((Z_RING, rows, lanes), mine.dtype)

    def put(held, piece, distance, row=0):
        at = ((z_place + distance) % Z_RING, row, 0)
        return lax.dynamic_update_slice(held, piece[None], at)

    held = put(held, mine, 0)
    above, below = mine, mine
    for distance in range(1, Z_RING // 2):
        below, above = along_z(below, 1), along_z(above, -1)
        held = put(put(held, below, -distance), above, distance)
    half = rows // 2
    below, above = along_z(below[:half], 1), along_z(above[half:], -1)
    return put(put(held, below, Z_RING // 2), above, Z_RING // 2, half)


def between_slabs(value):
    return lax.all_to_all(value, "ctx", 0, 0)


def together(*values):
    return lax.optimization_barrier(values)


def pick(core, first, second):
    return jnp.where(core == 0, first, second)


def document_columns(seg_ids, ids_prior):
    ids_all = jnp.concatenate([ids_prior, seg_ids])
    prior = ids_prior[2]
    same = lambda a: (seg_ids == a).astype(F32)
    columns = [same(ids_all[tap : tap + ROWS]) for tap in range(CONV - 1)]
    columns += [same(prior), same(seg_ids[-1]), same(seg_ids[L - 1]), same(seg_ids[L - 1])]
    columns += [seg_ids.astype(F32)]
    cols = jnp.pad(jnp.stack(columns, axis=1), ((0, 0), (0, 128 - len(columns))))
    return cols, jnp.broadcast_to(seg_ids.astype(F32)[None], (8, ROWS))


def local(
    tokens,
    seg_ids,
    w_x,
    w_z,
    w_bc,
    w_dt,
    conv_x,
    conv_x_bias,
    conv_bc,
    conv_bc_bias,
    dt_bias,
    decay_rate,
    skip_gain,
    norm_weight,
    w_out,
):
    rank = lax.axis_index("tp")
    core = rank % CORES
    chip = rank // CORES
    y_low = (lax.axis_index("ctx") // Z_RING).astype(jnp.int32)

    w_cols = jnp.concatenate(
        [w_bc.T.reshape(CHIPS, 2 * N, FEAT), w_dt.T.reshape(CHIPS, 2 * HEADS, FEAT)], axis=1
    )
    ids_row = jnp.pad((seg_ids[-3:] + 1).astype(BF16), (0, FEAT - 3))[None]
    halo = next_ctx(jnp.concatenate([ids_row, tokens[1 - HALO :]], axis=0))
    ids_prior = halo[0, :3].astype(jnp.int32) - 1
    shared = jnp.concatenate([halo, tokens], axis=0)
    shared = jnp.broadcast_to(shared[None], (CHIPS, ALL_ROWS, FEAT))
    sent = jnp.concatenate([shared, w_cols], axis=1)
    sent, w_out = together(sent, w_out)
    own = between_chips(sent)

    halves = (w_out[:, :128], w_out[:, 128:])
    w_pair = jnp.concatenate(
        [pick(core, *halves), swapped(pick(core, halves[1], halves[0]), 1)], axis=0
    )
    w_near = gathered_along_z(w_pair)

    cols, seg_row = document_columns(seg_ids, ids_prior)
    taps_bc = lax.dynamic_slice_in_dim(conv_bc, chip * 2 * N, 2 * N, 1)
    bias_bc = lax.dynamic_slice_in_dim(conv_bc_bias, chip * 2 * N, 2 * N, 0)[None]
    skip = jnp.repeat(skip_gain, P_SIZE)[None]
    fixed = [cols, conv_x, conv_x_bias[None], taps_bc, bias_bc, dt_bias[None], decay_rate[None]]
    own, w_near, fixed, seg_row, skip = together(own, w_near, fixed, seg_row, skip)
    w_far = lax.ppermute(w_near, "ctx", [(i, i ^ Z_RING) for i in range(2 * Z_RING)])
    sib = swapped(own, 1)
    xc, bcc, hcol, hrow, s0, pay = scan_input(own, sib, w_x, fixed)
    own, sib, pay = together(own, sib, pay)
    pieces = between_slabs(pay)
    gates = gate(own, sib, w_z)
    pieces, gates, xc, bcc = together(pieces, gates, xc, bcc)
    state = between_slabs(prefix(pieces).reshape(CTX, 8, CH)).reshape(N, CH)
    y, cc, decays = intra(xc, bcc, hcol, hrow, s0, fixed[0], seg_row, skip)
    mine = join(y, gates, cc, decays, state, norm_weight[None])
    parts = between_chips(project(mine, swapped(mine, 1), w_near, w_far, y_low))
    total = jnp.sum(parts.astype(F32), axis=0).astype(BF16)
    parts = (total[:, :128], total[:, 128:])
    kept = pick(core, *parts)
    given = swapped(pick(core, parts[1], parts[0]), 1)
    return jnp.concatenate([pick(core, kept, given), pick(core, given, kept)], axis=1)


def solution(mesh):
    return jax.shard_map(
        local,
        mesh=mesh,
        in_specs=(
            P("ctx", "tp"),
            P("ctx"),
            P(None, "tp"),
            P(None, "tp"),
            P("tp", None),
            P("tp", None),
            P(None, "tp"),
            P("tp"),
            P(),
            P(),
            P("tp"),
            P("tp"),
            P("tp"),
            P("tp"),
            P("tp", "ctx"),
        ),
        out_specs=P("ctx", "tp"),
        check_vma=False,
    )
```

```python
import functools

import jax
import jax.numpy as jnp
from jax import lax
from jax.experimental import pallas as pl
from jax.experimental.pallas import tpu as pltpu
from jax.sharding import PartitionSpec as P

H = 128
P_SIZE = 64
N = 128
G = 8
L = 256
CONV = 4
HALO = 16
NORM_EPS = 1e-05
HIGHEST = lax.Precision.HIGHEST

CHIPS = 8
CORES = 2
HEADS = 8
CH = HEADS * P_SIZE
ROWS = 512
FEAT = 256
Z_RING = 8
CTX = 16
ALL_ROWS = HALO + ROWS
COLS = 2 * N + 2 * HEADS
VMEM = pl.BlockSpec(memory_space=pltpu.VMEM)
BF16 = jnp.bfloat16
F32 = jnp.float32


def params(mib, grid=False):
    more = {"dimension_semantics": ("arbitrary",)} if grid else {}
    return pltpu.CompilerParams(vmem_limit_bytes=mib * 2**20, **more)


def dot(a, b):
    return jnp.dot(a, b, preferred_element_type=F32)


def dot_nt(a, b):
    return lax.dot_general(a, b, (((1,), (1,)), ((), ())), preferred_element_type=F32)


def dot_tn(a, b):
    return lax.dot_general(a, b, (((0,), (0,)), ((), ())), preferred_element_type=F32)


def silu(v):
    return v / (1.0 + jnp.exp(-v))


def spread(cols, first=0, count=HEADS):
    shape = (HEADS, count * P_SIZE)
    head = lax.broadcasted_iota(jnp.int32, shape, 0)
    lane = lax.broadcasted_iota(jnp.int32, shape, 1)
    pick = (head == lane // P_SIZE + first).astype(F32)
    return jnp.dot(cols, pick, precision=HIGHEST, preferred_element_type=F32)


def my_core():
    return lax.rem(lax.axis_index("tp"), CORES)


def add_to(acc, step, value):
    @pl.when(step == 0)
    def _():
        acc[...] = value

    @pl.when(step > 0)
    def _():
        acc[...] += value


def conv_chunk(raw, at, rows, masks, taps, offsets):
    total = offsets + taps[CONV - 1 : CONV, :] * raw[at + HALO : at + HALO + rows, :]
    for tap in range(CONV - 1):
        first = at + HALO - (CONV - 1) + tap
        shifted = raw[first : first + rows, :]
        total = total + taps[tap : tap + 1, :] * (shifted * masks[:, tap : tap + 1])
    return silu(total).astype(BF16)


def rounded(ref):
    ref[...] = ref[...].astype(BF16).astype(F32)


def step_sources():
    for slot in range(2):
        for same_core in (True, False):
            yield slot, same_core


def step_tokens(own, sib, first=0):
    refs = [(own if same_core else sib, slot) for slot, same_core in step_sources()]
    return jnp.concatenate([ref[slot, first:ALL_ROWS] for ref, slot in refs], axis=1)


def step_cols(own, sib):
    refs = [(own if same_core else sib, slot) for slot, same_core in step_sources()]
    return jnp.concatenate([ref[slot, ALL_ROWS:] for ref, slot in refs], axis=1)


def step_rows(w_ref):
    core = my_core()
    parts = []
    for slot, same_core in step_sources():
        from_core = core if same_core else 1 - core
        at = pl.multiple_of((slot * CORES + from_core) * FEAT, FEAT)
        parts.append(w_ref[pl.ds(at, FEAT), :])
    return jnp.concatenate(parts, axis=0)


def scan_input_kernel(
    own,
    sib,
    w_x,
    cols,
    taps_x,
    bias_x,
    taps_bc,
    bias_bc,
    dt_bias,
    decay,
    xc,
    bcc,
    hcol,
    hrow,
    s0,
    pay,
    acc_x,
    acc_bc,
    raw_bc,
):
    step = pl.program_id(0)
    core = my_core()
    toks = step_tokens(own, sib)
    add_to(acc_x, step, dot(toks, step_rows(w_x)))
    add_to(acc_bc, step, dot_nt(toks, step_cols(own, sib)))

    @pl.when(step == pl.num_programs(0) - 1)
    def _():
        raw_dt = acc_bc[HALO:, 2 * N :]
        raw_dt = jnp.where(core == 0, raw_dt[:, :HEADS], raw_dt[:, HEADS:])
        pre = raw_dt + dt_bias[...]
        dt = jnp.maximum(pre, 0.0) + jnp.log1p(jnp.exp(-jnp.abs(pre)))
        loga = -decay[...] * dt
        acc_x[...] = acc_x[...].astype(BF16).astype(F32)
        raw_bc[...] = acc_bc[:, : 2 * N].astype(BF16).astype(F32)
        for at in range(0, ROWS, 64):
            masks = cols[at : at + 64, :]
            xc[at : at + 64, :] = conv_chunk(acc_x, at, 64, masks, taps_x, bias_x[...])
            bcc[at : at + 64, :] = conv_chunk(raw_bc, at, 64, masks, taps_bc, bias_bc[...])
        lower = (
            lax.broadcasted_iota(jnp.int32, (L, L), 0) >= lax.broadcasted_iota(jnp.int32, (L, L), 1)
        ).astype(F32)
        cum0 = jnp.dot(lower, loga[:L], precision=HIGHEST, preferred_element_type=F32)
        cum1 = jnp.dot(lower, loga[L:], precision=HIGHEST, preferred_element_type=F32)
        end0, end1 = cum0[L - 1 :], cum1[L - 1 :]
        slab = jnp.exp(jnp.concatenate([cum0, cum1 + end0], axis=0)) * cols[:, 3:4]
        inner = jnp.exp(cum1) * cols[L:, 5:6]
        tail0 = jnp.exp(end0 - cum0) * cols[:L, 6:7] * dt[:L]
        tail1 = jnp.exp(end1 - cum1) * cols[L:, 4:5] * dt[L:]
        cum = jnp.concatenate([cum0, cum1], axis=0)
        blank = jnp.zeros((ROWS, 128 - 4 * HEADS), F32)
        wide = jnp.concatenate(
            [cum, dt, slab, jnp.concatenate([inner, inner], axis=0), blank], axis=1
        )
        hcol[...] = wide
        hrow[...] = wide.T[: 2 * HEADS]
        scaled0 = (xc[:L, :].astype(F32) * spread(tail0)).astype(BF16)
        scaled1 = (xc[L:, :].astype(F32) * spread(tail1)).astype(BF16)
        state0 = dot_tn(bcc[:L, :N], scaled0)
        state1 = dot_tn(bcc[L:, :N], scaled1)
        s0[...] = state0.astype(BF16)
        ends = jnp.concatenate(
            [inner[L - 1 :], slab[ROWS - 1 :], jnp.zeros((6, HEADS), F32)], axis=0
        )
        ends = spread(ends)
        final = ends[0:1] * state0 + state1
        factor = factor_rows(ends[1:2])
        for piece in range(CTX):
            part = final[8 * piece : 8 * piece + 8]
            pay[piece] = jnp.concatenate([part, factor], axis=0).astype(BF16)


def factor_rows(factor):
    high = factor.astype(BF16).astype(F32)
    row = lax.broadcasted_iota(jnp.int32, (8, CH), 0)
    return jnp.where(row == 0, high, jnp.where(row == 1, factor - high, 0.0))


def over_chips(kernel, blocked, fixed, shapes, scratch, mib, flops, name):
    whole = lambda a: pl.BlockSpec(a.shape, lambda i: (0,) * len(a.shape))
    return pl.pallas_call(
        kernel,
        grid=(CHIPS // 2,),
        in_specs=[spec for _, spec in blocked] + [whole(a) for a in fixed],
        out_specs=[whole(a) for a in shapes],
        out_shape=[pltpu.HBM(a.shape, a.dtype) for a in shapes],
        scratch_shapes=scratch,
        compiler_params=params(mib, True),
        cost_estimate=pl.CostEstimate(
            flops=flops, bytes_accessed=8 * 2**20, transcendentals=10**6
        ),
        name=name,
    )(*[a for a, _ in blocked], *fixed)


def two_chips(a, rows):
    return a, pl.BlockSpec((2, rows, FEAT), lambda i: (i, 0, 0))


def their_rows(w):
    return w, pl.BlockSpec((4 * FEAT, CH), lambda i: (i, 0))


def scan_input(own, sib, w_x, fixed):
    shapes = [
        jax.ShapeDtypeStruct((ROWS, CH), BF16),
        jax.ShapeDtypeStruct((ROWS, 2 * N), BF16),
        jax.ShapeDtypeStruct((ROWS, 128), F32),
        jax.ShapeDtypeStruct((2 * HEADS, ROWS), F32),
        jax.ShapeDtypeStruct((N, CH), BF16),
        jax.ShapeDtypeStruct((CTX, 16, CH), BF16),
    ]
    blocked = [two_chips(a, ALL_ROWS + COLS) for a in (own, sib)]
    blocked += [their_rows(w_x)]
    scratch = [
        pltpu.VMEM((ALL_ROWS, CH), F32),
        pltpu.VMEM((ALL_ROWS, COLS), F32),
        pltpu.VMEM((ALL_ROWS, 2 * N), F32),
    ]
    flops = 2 * ALL_ROWS * 4096 * (CH + COLS)
    return over_chips(
        scan_input_kernel, blocked, fixed, shapes, scratch, 22, flops, "scan_input"
    )


def gate_kernel(own, sib, w_z, gates, acc):
    step = pl.program_id(0)
    add_to(acc, step, dot(step_tokens(own, sib, HALO), step_rows(w_z)))

    @pl.when(step == pl.num_programs(0) - 1)
    def _():
        for at in range(0, ROWS, 64):
            gates[at : at + 64, :] = silu(acc[at : at + 64, :].astype(BF16).astype(F32))


def gate(own, sib, w_z):
    shapes = [jax.ShapeDtypeStruct((ROWS, CH), F32)]
    blocked = [two_chips(a, ALL_ROWS) for a in (own, sib)] + [their_rows(w_z)]
    scratch = [pltpu.VMEM((ROWS, CH), F32)]
    flops = 2 * ROWS * 4096 * CH
    return over_chips(gate_kernel, blocked, [], shapes, scratch, 16, flops, "gate")[0]


def intra_kernel(xc, bcc, hcol, hrow, s0, cols, seg_row, skip, y, c_out, decays):
    c_out[...] = bcc[:, N:]
    decays[...] = hcol[...]
    for block in range(2):
        intra_block(block * L, xc, bcc, hcol, hrow, s0, cols, seg_row, skip, y)


def intra_block(at, xc, bcc, hcol, hrow, s0, cols, seg_row, skip, y):
    b_vals, c_vals = bcc[at : at + L, :N], bcc[at : at + L, N:]
    after = lax.broadcasted_iota(jnp.int32, (L, L), 0) >= lax.broadcasted_iota(
        jnp.int32, (L, L), 1
    )
    same = cols[at : at + L, 7:8] == seg_row[0:1, at : at + L]
    scores = jnp.where(after & same, dot_nt(c_vals, b_vals), 0.0)
    for half in range(2):
        lanes = slice(half * 256, half * 256 + 256)
        weights, values = [], []
        x_half = xc[at : at + L, lanes]
        head_of = lax.broadcasted_iota(jnp.int32, (1, 256), 1) // P_SIZE
        for part in range(4):
            head = half * 4 + part
            gap = hcol[at : at + L, head : head + 1] - hrow[head : head + 1, at : at + L]
            decay = jnp.exp(jnp.minimum(gap, 0.0))
            dt_row = hrow[HEADS + head : HEADS + head + 1, at : at + L]
            weights.append((scores * decay * dt_row).astype(BF16))
            values.append(x_half * (head_of == part).astype(BF16))
        out = dot(jnp.concatenate(weights, axis=1), jnp.concatenate(values, axis=0))
        out = out + skip[:, lanes] * x_half.astype(F32)
        if at:
            carried = spread(hcol[at : at + L, 3 * HEADS : 4 * HEADS], half * 4, 4)
            out = out + carried * dot(c_vals, s0[:, lanes])
        y[at : at + L, lanes] = out


def intra(*args):
    shapes = [((ROWS, CH), F32), ((ROWS, N), BF16), ((ROWS, 128), F32)]
    return pl.pallas_call(
        intra_kernel,
        in_specs=[VMEM] * len(args),
        out_specs=[VMEM] * len(shapes),
        out_shape=[jax.ShapeDtypeStruct(*shape) for shape in shapes],
        compiler_params=params(12),
        cost_estimate=pl.CostEstimate(
            flops=2 * ROWS * L * CH * 4, bytes_accessed=4 * 2**20, transcendentals=2 * 10**6
        ),
        name="intra",
    )(*args)


def prefix_kernel(pieces, out):
    total = jnp.zeros((8, CH), F32)
    for pair in range(8):
        held = []
        for place in (2 * pair, 2 * pair + 1):
            held.append(total)
            piece = pieces[place].astype(F32)
            total = total * (piece[8:9] + piece[9:10]) + piece[:8]
        out[16 * pair : 16 * pair + 16, :] = jnp.concatenate(held, axis=0).astype(BF16)


def prefix(pieces):
    return pl.pallas_call(
        prefix_kernel,
        in_specs=[VMEM],
        out_specs=VMEM,
        out_shape=jax.ShapeDtypeStruct((N, CH), BF16),
        compiler_params=params(8),
        name="prefix",
    )(pieces)


def join_kernel(y, gates, cc, hcol, state, gain, out):
    for at in range(0, ROWS, 128):
        c_vals = cc[at : at + 128, :]
        carried = spread(hcol[at : at + 128, 2 * HEADS : 3 * HEADS])
        total = y[at : at + 128, :] + carried * dot(c_vals, state[...])
        gated = total * gates[at : at + 128, :]
        square = jnp.sum(gated * gated, axis=1, keepdims=True)
        high = square.astype(BF16).astype(F32)
        lane = lax.broadcasted_iota(jnp.int32, (128, 128), 1)
        out[at : at + 128, :CH] = (gated * gain[...]).astype(BF16)
        out[at : at + 128, CH:] = jnp.where(lane < 64, high, square - high).astype(BF16)


def join(*args):
    return pl.pallas_call(
        join_kernel,
        in_specs=[VMEM] * len(args),
        out_specs=VMEM,
        out_shape=jax.ShapeDtypeStruct((ROWS, CH + 128), BF16),
        compiler_params=params(12),
        cost_estimate=pl.CostEstimate(
            flops=2 * ROWS * N * CH, bytes_accessed=4 * 2**20, transcendentals=0
        ),
        name="join",
    )(*args)


def project_kernel(place, own, sib, near, far_own, far_sib, out):
    del place
    square = own[:, CH:].astype(F32) + sib[:, CH:].astype(F32)
    scale = lax.rsqrt((square[:, 0:1] + square[:, 64:65]) / (2.0 * CH) + NORM_EPS)
    values = jnp.concatenate([own[:, :CH], sib[:, :CH]], axis=1)

    def send(rows):
        out[0] = (dot(values, rows) * scale).astype(BF16)

    @pl.when(pl.program_id(0) < CHIPS // 2)
    def _():
        send(jnp.concatenate([near[0], near[1]], axis=1))

    @pl.when(pl.program_id(0) >= CHIPS // 2)
    def _():
        sides = [jnp.concatenate([ref[0], ref[1]], axis=1) for ref in (far_own, far_sib)]
        send(jnp.concatenate(sides, axis=0))


def project(own, sib, w_held, w_late, y_low):
    half = CHIPS // 2
    whole = pl.BlockSpec(own.shape, lambda i, place: (0, 0))
    first = lambda i, place: (jnp.minimum(i, half - 1), 0, 0)
    then = lambda row: lambda i, place: (jnp.maximum(i - half, 0), row, 0)

    def sent(i, place):
        return lax.rem(i, half) + half * lax.rem(lax.div(i, half) + place[0], 2), 0, 0

    return pl.pallas_call(
        project_kernel,
        grid_spec=pltpu.PrefetchScalarGridSpec(
            num_scalar_prefetch=1,
            grid=(CHIPS,),
            in_specs=[
                whole,
                whole,
                pl.BlockSpec((2, 2 * CH, 128), first),
                pl.BlockSpec((2, CH, 128), then(2)),
                pl.BlockSpec((2, CH, 128), then(0)),
            ],
            out_specs=pl.BlockSpec((1, ROWS, 256), sent),
        ),
        out_shape=jax.ShapeDtypeStruct((CHIPS, ROWS, 256), BF16),
        compiler_params=params(14, True),
        cost_estimate=pl.CostEstimate(
            flops=8 * ROWS * CH * 2048, bytes_accessed=8 * 2**20, transcendentals=0
        ),
        name="project",
    )(y_low[None], own, sib, w_held, w_held, w_late)


def swapped(value, bit):
    return lax.ppermute(value, "tp", [(i, i ^ bit) for i in range(16)])


def next_ctx(value):
    return lax.ppermute(value, "ctx", [(i, i + 1) for i in range(15)])


def between_chips(value):
    same_core = [[2 * chip + core for chip in range(CHIPS)] for core in range(CORES)]
    return lax.all_to_all(value, "tp", 0, 0, axis_index_groups=same_core)


def across_y(value):
    return lax.ppermute(value, "ctx", [(i, i ^ Z_RING) for i in range(CTX)])


def along_z(value, steps):
    pairs = [(i, i // Z_RING * Z_RING + (i + steps) % Z_RING) for i in range(CTX)]
    return lax.ppermute(value, "ctx", pairs)


def gathered_along_z(mine):
    rows, lanes = mine.shape
    z_place = lax.axis_index("ctx") % Z_RING
    held = jnp.zeros((Z_RING, rows, lanes), mine.dtype)

    def put(held, piece, distance, row=0):
        at = ((z_place + distance) % Z_RING, row, 0)
        return lax.dynamic_update_slice(held, piece[None], at)

    held = put(held, mine, 0)
    above, below = mine, mine
    for distance in range(1, Z_RING // 2):
        below, above = along_z(below, 1), along_z(above, -1)
        held = put(put(held, below, -distance), above, distance)
    half = rows // 2
    below, above = along_z(below[:half], 1), along_z(above[half:], -1)
    return put(put(held, below, Z_RING // 2), above, Z_RING // 2, half)


def between_slabs(value):
    return lax.all_to_all(value, "ctx", 0, 0)


def together(*values):
    return lax.optimization_barrier(values)


def pick(core, first, second):
    return jnp.where(core == 0, first, second)


def document_columns(seg_ids, ids_prior):
    ids_all = jnp.concatenate([ids_prior, seg_ids])
    prior = ids_prior[2]
    same = lambda a: (seg_ids == a).astype(F32)
    columns = [same(ids_all[tap : tap + ROWS]) for tap in range(CONV - 1)]
    columns += [same(prior), same(seg_ids[-1]), same(seg_ids[L - 1]), same(seg_ids[L - 1])]
    columns += [seg_ids.astype(F32)]
    cols = jnp.pad(jnp.stack(columns, axis=1), ((0, 0), (0, 128 - len(columns))))
    return cols, jnp.broadcast_to(seg_ids.astype(F32)[None], (8, ROWS))


def local(
    tokens,
    seg_ids,
    w_x,
    w_z,
    w_bc,
    w_dt,
    conv_x,
    conv_x_bias,
    conv_bc,
    conv_bc_bias,
    dt_bias,
    decay_rate,
    skip_gain,
    norm_weight,
    w_out,
):
    rank = lax.axis_index("tp")
    core = rank % CORES
    chip = rank // CORES
    y_low = (lax.axis_index("ctx") // Z_RING).astype(jnp.int32)

    w_cols = jnp.concatenate(
        [w_bc.T.reshape(CHIPS, 2 * N, FEAT), w_dt.T.reshape(CHIPS, 2 * HEADS, FEAT)], axis=1
    )
    ids_row = jnp.pad((seg_ids[-3:] + 1).astype(BF16), (0, FEAT - 3))[None]
    halo = next_ctx(jnp.concatenate([ids_row, tokens[1 - HALO :]], axis=0))
    ids_prior = halo[0, :3].astype(jnp.int32) - 1
    shared = jnp.concatenate([halo, tokens], axis=0)
    shared = jnp.broadcast_to(shared[None], (CHIPS, ALL_ROWS, FEAT))
    sent = jnp.concatenate([shared, w_cols], axis=1)
    sent, w_out, seg_ids, conv_bc, conv_bc_bias, skip_gain = together(
        sent, w_out, seg_ids, conv_bc, conv_bc_bias, skip_gain
    )
    own = between_chips(sent)

    halves = (w_out[:, :128], w_out[:, 128:])
    w_kept = pick(core, *halves)
    w_own_far = across_y(w_kept)
    w_sib = swapped(pick(core, halves[1], halves[0]), 1)
    w_held = gathered_along_z(jnp.concatenate([w_kept, w_sib, w_own_far], axis=0))

    cols, seg_row = document_columns(seg_ids, ids_prior)
    taps_bc = lax.dynamic_slice_in_dim(conv_bc, chip * 2 * N, 2 * N, 1)
    bias_bc = lax.dynamic_slice_in_dim(conv_bc_bias, chip * 2 * N, 2 * N, 0)[None]
    skip = jnp.repeat(skip_gain, P_SIZE)[None]
    fixed = [cols, conv_x, conv_x_bias[None], taps_bc, bias_bc, dt_bias[None], decay_rate[None]]
    w_rest = w_held[:, CH : 2 * CH]
    own, w_held, w_rest, fixed, seg_row, skip = together(
        own, w_held, w_rest, fixed, seg_row, skip
    )
    w_late = across_y(w_rest)
    sib = swapped(own, 1)
    xc, bcc, hcol, hrow, s0, pay = scan_input(own, sib, w_x, fixed)
    own, sib, pay = together(own, sib, pay)
    pieces = between_slabs(pay)
    gates = gate(own, sib, w_z)
    pieces, gates, xc, bcc = together(pieces, gates, xc, bcc)
    state = between_slabs(prefix(pieces).reshape(CTX, 8, CH)).reshape(N, CH)
    y, cc, decays = intra(xc, bcc, hcol, hrow, s0, fixed[0], seg_row, skip)
    state, w_late, w_held = together(state, w_late, w_held)
    mine = join(y, gates, cc, decays, state, norm_weight[None])
    parts = between_chips(project(mine, swapped(mine, 1), w_held, w_late, y_low))
    total = jnp.sum(parts.astype(F32), axis=0).astype(BF16)
    parts = (total[:, :128], total[:, 128:])
    kept = pick(core, *parts)
    given = swapped(pick(core, parts[1], parts[0]), 1)
    return jnp.concatenate([pick(core, kept, given), pick(core, given, kept)], axis=1)


def solution(mesh):
    return jax.shard_map(
        local,
        mesh=mesh,
        in_specs=(
            P("ctx", "tp"),
            P("ctx"),
            P(None, "tp"),
            P(None, "tp"),
            P("tp", None),
            P("tp", None),
            P(None, "tp"),
            P("tp"),
            P(),
            P(),
            P("tp"),
            P("tp"),
            P("tp"),
            P("tp"),
            P("tp", "ctx"),
        ),
        out_specs=P("ctx", "tp"),
        check_vma=False,
    )
```

```python
import functools

import jax
import jax.numpy as jnp
from jax import lax
from jax.experimental import pallas as pl
from jax.experimental.pallas import tpu as pltpu
from jax.sharding import PartitionSpec as P

H = 128
P_SIZE = 64
N = 128
G = 8
L = 256
CONV = 4
HALO = 16
NORM_EPS = 1e-05
HIGHEST = lax.Precision.HIGHEST

CHIPS = 8
CORES = 2
HEADS = 8
CH = HEADS * P_SIZE
ROWS = 512
FEAT = 256
Z_RING = 8
CTX = 16
ALL_ROWS = HALO + ROWS
COLS = 2 * N + 2 * HEADS
VMEM = pl.BlockSpec(memory_space=pltpu.VMEM)
BF16 = jnp.bfloat16
F32 = jnp.float32


def params(mib, grid=False):
    more = {"dimension_semantics": ("arbitrary",)} if grid else {}
    return pltpu.CompilerParams(vmem_limit_bytes=mib * 2**20, **more)


def dot(a, b):
    return jnp.dot(a, b, preferred_element_type=F32)


def dot_nt(a, b):
    return lax.dot_general(a, b, (((1,), (1,)), ((), ())), preferred_element_type=F32)


def dot_tn(a, b):
    return lax.dot_general(a, b, (((0,), (0,)), ((), ())), preferred_element_type=F32)


def silu(v):
    return v / (1.0 + jnp.exp(-v))


def spread(cols, first=0, count=HEADS):
    shape = (HEADS, count * P_SIZE)
    head = lax.broadcasted_iota(jnp.int32, shape, 0)
    lane = lax.broadcasted_iota(jnp.int32, shape, 1)
    pick = (head == lane // P_SIZE + first).astype(F32)
    return jnp.dot(cols, pick, precision=HIGHEST, preferred_element_type=F32)


def my_core():
    return lax.rem(lax.axis_index("tp"), CORES)


def add_to(acc, step, value):
    @pl.when(step == 0)
    def _():
        acc[...] = value

    @pl.when(step > 0)
    def _():
        acc[...] += value


def conv_chunk(raw, at, rows, masks, taps, offsets):
    total = offsets + taps[CONV - 1 : CONV, :] * raw[at + HALO : at + HALO + rows, :]
    for tap in range(CONV - 1):
        first = at + HALO - (CONV - 1) + tap
        shifted = raw[first : first + rows, :]
        total = total + taps[tap : tap + 1, :] * (shifted * masks[:, tap : tap + 1])
    return silu(total).astype(BF16)


def rounded(ref):
    ref[...] = ref[...].astype(BF16).astype(F32)


def step_sources():
    for slot in range(2):
        for same_core in (True, False):
            yield slot, same_core


def step_tokens(own, sib, first=0):
    refs = [(own if same_core else sib, slot) for slot, same_core in step_sources()]
    return jnp.concatenate([ref[slot, first:ALL_ROWS] for ref, slot in refs], axis=1)


def step_cols(own, sib):
    refs = [(own if same_core else sib, slot) for slot, same_core in step_sources()]
    return jnp.concatenate([ref[slot, ALL_ROWS:] for ref, slot in refs], axis=1)


def step_rows(w_ref):
    core = my_core()
    parts = []
    for slot, same_core in step_sources():
        from_core = core if same_core else 1 - core
        at = pl.multiple_of((slot * CORES + from_core) * FEAT, FEAT)
        parts.append(w_ref[pl.ds(at, FEAT), :])
    return jnp.concatenate(parts, axis=0)


def scan_input_kernel(
    own,
    sib,
    w_x,
    cols,
    taps_x,
    bias_x,
    taps_bc,
    bias_bc,
    dt_bias,
    decay,
    xc,
    bcc,
    hcol,
    hrow,
    s0,
    pay,
    acc_x,
    acc_bc,
    raw_bc,
):
    step = pl.program_id(0)
    core = my_core()
    toks = step_tokens(own, sib)
    add_to(acc_x, step, dot(toks, step_rows(w_x)))
    add_to(acc_bc, step, dot_nt(toks, step_cols(own, sib)))

    @pl.when(step == pl.num_programs(0) - 1)
    def _():
        raw_dt = acc_bc[HALO:, 2 * N :]
        raw_dt = jnp.where(core == 0, raw_dt[:, :HEADS], raw_dt[:, HEADS:])
        pre = raw_dt + dt_bias[...]
        dt = jnp.maximum(pre, 0.0) + jnp.log1p(jnp.exp(-jnp.abs(pre)))
        loga = -decay[...] * dt
        acc_x[...] = acc_x[...].astype(BF16).astype(F32)
        raw_bc[...] = acc_bc[:, : 2 * N].astype(BF16).astype(F32)
        for at in range(0, ROWS, 64):
            masks = cols[at : at + 64, :]
            xc[at : at + 64, :] = conv_chunk(acc_x, at, 64, masks, taps_x, bias_x[...])
            bcc[at : at + 64, :] = conv_chunk(raw_bc, at, 64, masks, taps_bc, bias_bc[...])
        lower = (
            lax.broadcasted_iota(jnp.int32, (L, L), 0) >= lax.broadcasted_iota(jnp.int32, (L, L), 1)
        ).astype(F32)
        cum0 = jnp.dot(lower, loga[:L], precision=HIGHEST, preferred_element_type=F32)
        cum1 = jnp.dot(lower, loga[L:], precision=HIGHEST, preferred_element_type=F32)
        end0, end1 = cum0[L - 1 :], cum1[L - 1 :]
        slab = jnp.exp(jnp.concatenate([cum0, cum1 + end0], axis=0)) * cols[:, 3:4]
        inner = jnp.exp(cum1) * cols[L:, 5:6]
        tail0 = jnp.exp(end0 - cum0) * cols[:L, 6:7] * dt[:L]
        tail1 = jnp.exp(end1 - cum1) * cols[L:, 4:5] * dt[L:]
        cum = jnp.concatenate([cum0, cum1], axis=0)
        blank = jnp.zeros((ROWS, 128 - 4 * HEADS), F32)
        wide = jnp.concatenate(
            [cum, dt, slab, jnp.concatenate([inner, inner], axis=0), blank], axis=1
        )
        hcol[...] = wide
        hrow[...] = wide.T[: 2 * HEADS]
        scaled0 = (xc[:L, :].astype(F32) * spread(tail0)).astype(BF16)
        scaled1 = (xc[L:, :].astype(F32) * spread(tail1)).astype(BF16)
        state0 = dot_tn(bcc[:L, :N], scaled0)
        state1 = dot_tn(bcc[L:, :N], scaled1)
        s0[...] = state0.astype(BF16)
        ends = jnp.concatenate(
            [inner[L - 1 :], slab[ROWS - 1 :], jnp.zeros((6, HEADS), F32)], axis=0
        )
        ends = spread(ends)
        final = ends[0:1] * state0 + state1
        factor = factor_rows(ends[1:2])
        for piece in range(CTX):
            part = final[8 * piece : 8 * piece + 8]
            pay[piece] = jnp.concatenate([part, factor], axis=0).astype(BF16)


def factor_rows(factor):
    high = factor.astype(BF16).astype(F32)
    row = lax.broadcasted_iota(jnp.int32, (8, CH), 0)
    return jnp.where(row == 0, high, jnp.where(row == 1, factor - high, 0.0))


def over_chips(kernel, blocked, fixed, shapes, scratch, mib, flops, name):
    whole = lambda a: pl.BlockSpec(a.shape, lambda i: (0,) * len(a.shape))
    return pl.pallas_call(
        kernel,
        grid=(CHIPS // 2,),
        in_specs=[spec for _, spec in blocked] + [whole(a) for a in fixed],
        out_specs=[whole(a) for a in shapes],
        out_shape=[pltpu.HBM(a.shape, a.dtype) for a in shapes],
        scratch_shapes=scratch,
        compiler_params=params(mib, True),
        cost_estimate=pl.CostEstimate(
            flops=flops, bytes_accessed=8 * 2**20, transcendentals=10**6
        ),
        name=name,
    )(*[a for a, _ in blocked], *fixed)


def two_chips(a, rows):
    return a, pl.BlockSpec((2, rows, FEAT), lambda i: (i, 0, 0))


def their_rows(w):
    return w, pl.BlockSpec((4 * FEAT, CH), lambda i: (i, 0))


def scan_input(own, sib, w_x, fixed):
    shapes = [
        jax.ShapeDtypeStruct((ROWS, CH), BF16),
        jax.ShapeDtypeStruct((ROWS, 2 * N), BF16),
        jax.ShapeDtypeStruct((ROWS, 128), F32),
        jax.ShapeDtypeStruct((2 * HEADS, ROWS), F32),
        jax.ShapeDtypeStruct((N, CH), BF16),
        jax.ShapeDtypeStruct((CTX, 16, CH), BF16),
    ]
    blocked = [two_chips(a, ALL_ROWS + COLS) for a in (own, sib)]
    blocked += [their_rows(w_x)]
    scratch = [
        pltpu.VMEM((ALL_ROWS, CH), F32),
        pltpu.VMEM((ALL_ROWS, COLS), F32),
        pltpu.VMEM((ALL_ROWS, 2 * N), F32),
    ]
    flops = 2 * ALL_ROWS * 4096 * (CH + COLS)
    return over_chips(
        scan_input_kernel, blocked, fixed, shapes, scratch, 22, flops, "scan_input"
    )


def gate_kernel(own, sib, w_z, gates, acc):
    step = pl.program_id(0)
    add_to(acc, step, dot(step_tokens(own, sib, HALO), step_rows(w_z)))

    @pl.when(step == pl.num_programs(0) - 1)
    def _():
        for at in range(0, ROWS, 64):
            gates[at : at + 64, :] = silu(acc[at : at + 64, :].astype(BF16).astype(F32))


def gate(own, sib, w_z):
    shapes = [jax.ShapeDtypeStruct((ROWS, CH), F32)]
    blocked = [two_chips(a, ALL_ROWS) for a in (own, sib)] + [their_rows(w_z)]
    scratch = [pltpu.VMEM((ROWS, CH), F32)]
    flops = 2 * ROWS * 4096 * CH
    return over_chips(gate_kernel, blocked, [], shapes, scratch, 16, flops, "gate")[0]


def intra_kernel(xc, bcc, hcol, hrow, s0, cols, seg_row, skip, y, c_out, decays):
    c_out[...] = bcc[:, N:]
    decays[...] = hcol[...]
    for block in range(2):
        intra_block(block * L, xc, bcc, hcol, hrow, s0, cols, seg_row, skip, y)


def intra_block(at, xc, bcc, hcol, hrow, s0, cols, seg_row, skip, y):
    b_vals, c_vals = bcc[at : at + L, :N], bcc[at : at + L, N:]
    after = lax.broadcasted_iota(jnp.int32, (L, L), 0) >= lax.broadcasted_iota(
        jnp.int32, (L, L), 1
    )
    same = cols[at : at + L, 7:8] == seg_row[0:1, at : at + L]
    scores = jnp.where(after & same, dot_nt(c_vals, b_vals), 0.0)
    for half in range(2):
        lanes = slice(half * 256, half * 256 + 256)
        weights, values = [], []
        x_half = xc[at : at + L, lanes]
        head_of = lax.broadcasted_iota(jnp.int32, (1, 256), 1) // P_SIZE
        for part in range(4):
            head = half * 4 + part
            gap = hcol[at : at + L, head : head + 1] - hrow[head : head + 1, at : at + L]
            decay = jnp.exp(jnp.minimum(gap, 0.0))
            dt_row = hrow[HEADS + head : HEADS + head + 1, at : at + L]
            weights.append((scores * decay * dt_row).astype(BF16))
            values.append(x_half * (head_of == part).astype(BF16))
        out = dot(jnp.concatenate(weights, axis=1), jnp.concatenate(values, axis=0))
        out = out + skip[:, lanes] * x_half.astype(F32)
        if at:
            carried = spread(hcol[at : at + L, 3 * HEADS : 4 * HEADS], half * 4, 4)
            out = out + carried * dot(c_vals, s0[:, lanes])
        y[at : at + L, lanes] = out


def intra(*args):
    shapes = [((ROWS, CH), F32), ((ROWS, N), BF16), ((ROWS, 128), F32)]
    return pl.pallas_call(
        intra_kernel,
        in_specs=[VMEM] * len(args),
        out_specs=[VMEM] * len(shapes),
        out_shape=[jax.ShapeDtypeStruct(*shape) for shape in shapes],
        compiler_params=params(12),
        cost_estimate=pl.CostEstimate(
            flops=2 * ROWS * L * CH * 4, bytes_accessed=4 * 2**20, transcendentals=2 * 10**6
        ),
        name="intra",
    )(*args)


def prefix_kernel(pieces, out):
    total = jnp.zeros((8, CH), F32)
    for pair in range(8):
        held = []
        for place in (2 * pair, 2 * pair + 1):
            held.append(total)
            piece = pieces[place].astype(F32)
            total = total * (piece[8:9] + piece[9:10]) + piece[:8]
        out[16 * pair : 16 * pair + 16, :] = jnp.concatenate(held, axis=0).astype(BF16)


def prefix(pieces):
    return pl.pallas_call(
        prefix_kernel,
        in_specs=[VMEM],
        out_specs=VMEM,
        out_shape=jax.ShapeDtypeStruct((N, CH), BF16),
        compiler_params=params(8),
        name="prefix",
    )(pieces)


def join_kernel(y, gates, cc, hcol, state, gain, out):
    for at in range(0, ROWS, 128):
        c_vals = cc[at : at + 128, :]
        carried = spread(hcol[at : at + 128, 2 * HEADS : 3 * HEADS])
        total = y[at : at + 128, :] + carried * dot(c_vals, state[...])
        gated = total * gates[at : at + 128, :]
        square = jnp.sum(gated * gated, axis=1, keepdims=True)
        high = square.astype(BF16).astype(F32)
        lane = lax.broadcasted_iota(jnp.int32, (128, 128), 1)
        out[at : at + 128, :CH] = (gated * gain[...]).astype(BF16)
        out[at : at + 128, CH:] = jnp.where(lane < 64, high, square - high).astype(BF16)


def join(*args):
    return pl.pallas_call(
        join_kernel,
        in_specs=[VMEM] * len(args),
        out_specs=VMEM,
        out_shape=jax.ShapeDtypeStruct((ROWS, CH + 128), BF16),
        compiler_params=params(12),
        cost_estimate=pl.CostEstimate(
            flops=2 * ROWS * N * CH, bytes_accessed=4 * 2**20, transcendentals=0
        ),
        name="join",
    )(*args)


def project_kernel(place, own, sib, near, far_own, far_sib, out):
    del place
    square = own[:, CH:].astype(F32) + sib[:, CH:].astype(F32)
    scale = lax.rsqrt((square[:, 0:1] + square[:, 64:65]) / (2.0 * CH) + NORM_EPS)
    values = jnp.concatenate([own[:, :CH], sib[:, :CH]], axis=1)

    def send(rows):
        out[0] = (dot(values, rows) * scale).astype(BF16)

    @pl.when(pl.program_id(0) < CHIPS // 2)
    def _():
        send(jnp.concatenate([near[0], near[1]], axis=1))

    @pl.when(pl.program_id(0) >= CHIPS // 2)
    def _():
        sides = [jnp.concatenate([ref[0], ref[1]], axis=1) for ref in (far_own, far_sib)]
        send(jnp.concatenate(sides, axis=0))


def project(own, sib, w_held, w_late, y_low):
    half = CHIPS // 2
    whole = pl.BlockSpec(own.shape, lambda i, place: (0, 0))
    first = lambda i, place: (jnp.minimum(i, half - 1), 0, 0)
    then = lambda row: lambda i, place: (jnp.maximum(i - half, 0), row, 0)

    def sent(i, place):
        return lax.rem(i, half) + half * lax.rem(lax.div(i, half) + place[0], 2), 0, 0

    return pl.pallas_call(
        project_kernel,
        grid_spec=pltpu.PrefetchScalarGridSpec(
            num_scalar_prefetch=1,
            grid=(CHIPS,),
            in_specs=[
                whole,
                whole,
                pl.BlockSpec((2, 2 * CH, 128), first),
                pl.BlockSpec((2, CH, 128), then(2)),
                pl.BlockSpec((2, CH, 128), then(0)),
            ],
            out_specs=pl.BlockSpec((1, ROWS, 256), sent),
        ),
        out_shape=jax.ShapeDtypeStruct((CHIPS, ROWS, 256), BF16),
        compiler_params=params(56, True),
        cost_estimate=pl.CostEstimate(
            flops=8 * ROWS * CH * 2048, bytes_accessed=8 * 2**20, transcendentals=0
        ),
        name="project",
    )(y_low[None], own, sib, w_held, w_held, w_late)


def swapped(value, bit):
    return lax.ppermute(value, "tp", [(i, i ^ bit) for i in range(16)])


def next_ctx(value):
    return lax.ppermute(value, "ctx", [(i, i + 1) for i in range(15)])


def between_chips(value):
    same_core = [[2 * chip + core for chip in range(CHIPS)] for core in range(CORES)]
    return lax.all_to_all(value, "tp", 0, 0, axis_index_groups=same_core)


def across_y(value):
    return lax.ppermute(value, "ctx", [(i, i ^ Z_RING) for i in range(CTX)])


def along_z(value, steps):
    pairs = [(i, i // Z_RING * Z_RING + (i + steps) % Z_RING) for i in range(CTX)]
    return lax.ppermute(value, "ctx", pairs)


def gathered_along_z(mine):
    rows, lanes = mine.shape
    z_place = lax.axis_index("ctx") % Z_RING
    held = jnp.zeros((Z_RING, rows, lanes), mine.dtype)

    def put(held, piece, distance, row=0):
        at = ((z_place + distance) % Z_RING, row, 0)
        return lax.dynamic_update_slice(held, piece[None], at)

    held = put(held, mine, 0)
    above, below = mine, mine
    for distance in range(1, Z_RING // 2):
        below, above = along_z(below, 1), along_z(above, -1)
        held = put(put(held, below, -distance), above, distance)
    half = rows // 2
    below, above = along_z(below[:half], 1), along_z(above[half:], -1)
    return put(put(held, below, Z_RING // 2), above, Z_RING // 2, half)


def between_slabs(value):
    return lax.all_to_all(value, "ctx", 0, 0)


def together(*values):
    return lax.optimization_barrier(values)


def pick(core, first, second):
    return jnp.where(core == 0, first, second)


def document_columns(seg_ids, ids_prior):
    ids_all = jnp.concatenate([ids_prior, seg_ids])
    prior = ids_prior[2]
    same = lambda a: (seg_ids == a).astype(F32)
    columns = [same(ids_all[tap : tap + ROWS]) for tap in range(CONV - 1)]
    columns += [same(prior), same(seg_ids[-1]), same(seg_ids[L - 1]), same(seg_ids[L - 1])]
    columns += [seg_ids.astype(F32)]
    cols = jnp.pad(jnp.stack(columns, axis=1), ((0, 0), (0, 128 - len(columns))))
    return cols, jnp.broadcast_to(seg_ids.astype(F32)[None], (8, ROWS))


def local(
    tokens,
    seg_ids,
    w_x,
    w_z,
    w_bc,
    w_dt,
    conv_x,
    conv_x_bias,
    conv_bc,
    conv_bc_bias,
    dt_bias,
    decay_rate,
    skip_gain,
    norm_weight,
    w_out,
):
    rank = lax.axis_index("tp")
    core = rank % CORES
    chip = rank // CORES
    y_low = (lax.axis_index("ctx") // Z_RING).astype(jnp.int32)

    halves = (w_out[:, :128], w_out[:, 128:])
    w_kept, w_given = pick(core, *halves), pick(core, halves[1], halves[0])
    w_own_far = across_y(w_kept)

    w_cols = jnp.concatenate(
        [w_bc.T.reshape(CHIPS, 2 * N, FEAT), w_dt.T.reshape(CHIPS, 2 * HEADS, FEAT)], axis=1
    )
    ids_row = jnp.pad((seg_ids[-3:] + 1).astype(BF16), (0, FEAT - 3))[None]
    halo = next_ctx(jnp.concatenate([ids_row, tokens[1 - HALO :]], axis=0))
    ids_prior = halo[0, :3].astype(jnp.int32) - 1
    shared = jnp.concatenate([halo, tokens], axis=0)
    shared = jnp.broadcast_to(shared[None], (CHIPS, ALL_ROWS, FEAT))
    sent = jnp.concatenate([shared, w_cols], axis=1)
    sent, w_own_far, w_given, seg_ids, conv_bc, conv_bc_bias, skip_gain = together(
        sent, w_own_far, w_given, seg_ids, conv_bc, conv_bc_bias, skip_gain
    )
    own = between_chips(sent)

    w_sib = swapped(w_given, 1)
    w_held = gathered_along_z(jnp.concatenate([w_kept, w_sib, w_own_far], axis=0))

    cols, seg_row = document_columns(seg_ids, ids_prior)
    taps_bc = lax.dynamic_slice_in_dim(conv_bc, chip * 2 * N, 2 * N, 1)
    bias_bc = lax.dynamic_slice_in_dim(conv_bc_bias, chip * 2 * N, 2 * N, 0)[None]
    skip = jnp.repeat(skip_gain, P_SIZE)[None]
    fixed = [cols, conv_x, conv_x_bias[None], taps_bc, bias_bc, dt_bias[None], decay_rate[None]]
    w_rest = w_held[:, CH : 2 * CH]
    own, w_held, w_rest, fixed, seg_row, skip = together(
        own, w_held, w_rest, fixed, seg_row, skip
    )
    w_late = across_y(w_rest)
    sib = swapped(own, 1)
    xc, bcc, hcol, hrow, s0, pay = scan_input(own, sib, w_x, fixed)
    own, sib, pay, w_late = together(own, sib, pay, w_late)
    pieces = between_slabs(pay)
    gates = gate(own, sib, w_z)
    pieces, gates, xc, bcc = together(pieces, gates, xc, bcc)
    state = between_slabs(prefix(pieces).reshape(CTX, 8, CH)).reshape(N, CH)
    y, cc, decays = intra(xc, bcc, hcol, hrow, s0, fixed[0], seg_row, skip)
    mine = join(y, gates, cc, decays, state, norm_weight[None])
    parts = between_chips(project(mine, swapped(mine, 1), w_held, w_late, y_low))
    total = jnp.sum(parts.astype(F32), axis=0).astype(BF16)
    parts = (total[:, :128], total[:, 128:])
    kept = pick(core, *parts)
    given = swapped(pick(core, parts[1], parts[0]), 1)
    return jnp.concatenate([pick(core, kept, given), pick(core, given, kept)], axis=1)


def solution(mesh):
    return jax.shard_map(
        local,
        mesh=mesh,
        in_specs=(
            P("ctx", "tp"),
            P("ctx"),
            P(None, "tp"),
            P(None, "tp"),
            P("tp", None),
            P("tp", None),
            P(None, "tp"),
            P("tp"),
            P(),
            P(),
            P("tp"),
            P("tp"),
            P("tp"),
            P("tp"),
            P("tp", "ctx"),
        ),
        out_specs=P("ctx", "tp"),
        check_vma=False,
    )
```

```python
import functools

import jax
import jax.numpy as jnp
from jax import lax
from jax.experimental import pallas as pl
from jax.experimental.pallas import tpu as pltpu
from jax.sharding import PartitionSpec as P

H = 128
P_SIZE = 64
N = 128
G = 8
L = 256
CONV = 4
HALO = 16
NORM_EPS = 1e-05
HIGHEST = lax.Precision.HIGHEST

CHIPS = 8
CORES = 2
HEADS = 8
CH = HEADS * P_SIZE
ROWS = 512
FEAT = 256
Z_RING = 8
CTX = 16
ALL_ROWS = HALO + ROWS
COLS = 2 * N + 2 * HEADS
VMEM = pl.BlockSpec(memory_space=pltpu.VMEM)
BF16 = jnp.bfloat16
F32 = jnp.float32


def params(mib, grid=False):
    more = {"dimension_semantics": ("arbitrary",)} if grid else {}
    return pltpu.CompilerParams(vmem_limit_bytes=mib * 2**20, **more)


def dot(a, b):
    return jnp.dot(a, b, preferred_element_type=F32)


def dot_nt(a, b):
    return lax.dot_general(a, b, (((1,), (1,)), ((), ())), preferred_element_type=F32)


def dot_tn(a, b):
    return lax.dot_general(a, b, (((0,), (0,)), ((), ())), preferred_element_type=F32)


def silu(v):
    return v / (1.0 + jnp.exp(-v))


def spread(cols, first=0, count=HEADS):
    shape = (HEADS, count * P_SIZE)
    head = lax.broadcasted_iota(jnp.int32, shape, 0)
    lane = lax.broadcasted_iota(jnp.int32, shape, 1)
    pick = (head == lane // P_SIZE + first).astype(F32)
    return jnp.dot(cols, pick, precision=HIGHEST, preferred_element_type=F32)


def my_core():
    return lax.rem(lax.axis_index("tp"), CORES)


def add_to(acc, step, value):
    @pl.when(step == 0)
    def _():
        acc[...] = value

    @pl.when(step > 0)
    def _():
        acc[...] += value


def conv_chunk(raw, at, rows, masks, taps, offsets):
    total = offsets + taps[CONV - 1 : CONV, :] * raw[at + HALO : at + HALO + rows, :]
    for tap in range(CONV - 1):
        first = at + HALO - (CONV - 1) + tap
        shifted = raw[first : first + rows, :]
        total = total + taps[tap : tap + 1, :] * (shifted * masks[:, tap : tap + 1])
    return silu(total).astype(BF16)


def rounded(ref):
    ref[...] = ref[...].astype(BF16).astype(F32)


def step_sources():
    for slot in range(2):
        for same_core in (True, False):
            yield slot, same_core


def step_tokens(own, sib, first=0):
    refs = [(own if same_core else sib, slot) for slot, same_core in step_sources()]
    return jnp.concatenate([ref[slot, first:ALL_ROWS] for ref, slot in refs], axis=1)


def step_cols(own, sib):
    refs = [(own if same_core else sib, slot) for slot, same_core in step_sources()]
    return jnp.concatenate([ref[slot, ALL_ROWS:] for ref, slot in refs], axis=1)


def step_rows(w_ref):
    core = my_core()
    parts = []
    for slot, same_core in step_sources():
        from_core = core if same_core else 1 - core
        at = pl.multiple_of((slot * CORES + from_core) * FEAT, FEAT)
        parts.append(w_ref[pl.ds(at, FEAT), :])
    return jnp.concatenate(parts, axis=0)


def scan_input_kernel(
    own,
    sib,
    w_x,
    cols,
    taps_x,
    bias_x,
    taps_bc,
    bias_bc,
    dt_bias,
    decay,
    xc,
    bcc,
    hcol,
    hrow,
    s0,
    pay,
    acc_x,
    acc_bc,
    raw_bc,
):
    step = pl.program_id(0)
    core = my_core()
    toks = step_tokens(own, sib)
    add_to(acc_x, step, dot(toks, step_rows(w_x)))
    add_to(acc_bc, step, dot_nt(toks, step_cols(own, sib)))

    @pl.when(step == pl.num_programs(0) - 1)
    def _():
        raw_dt = acc_bc[HALO:, 2 * N :]
        raw_dt = jnp.where(core == 0, raw_dt[:, :HEADS], raw_dt[:, HEADS:])
        pre = raw_dt + dt_bias[...]
        dt = jnp.maximum(pre, 0.0) + jnp.log1p(jnp.exp(-jnp.abs(pre)))
        loga = -decay[...] * dt
        acc_x[...] = acc_x[...].astype(BF16).astype(F32)
        raw_bc[...] = acc_bc[:, : 2 * N].astype(BF16).astype(F32)
        for at in range(0, ROWS, 64):
            masks = cols[at : at + 64, :]
            xc[at : at + 64, :] = conv_chunk(acc_x, at, 64, masks, taps_x, bias_x[...])
            bcc[at : at + 64, :] = conv_chunk(raw_bc, at, 64, masks, taps_bc, bias_bc[...])
        lower = (
            lax.broadcasted_iota(jnp.int32, (L, L), 0) >= lax.broadcasted_iota(jnp.int32, (L, L), 1)
        ).astype(F32)
        cum0 = jnp.dot(lower, loga[:L], precision=HIGHEST, preferred_element_type=F32)
        cum1 = jnp.dot(lower, loga[L:], precision=HIGHEST, preferred_element_type=F32)
        end0, end1 = cum0[L - 1 :], cum1[L - 1 :]
        slab = jnp.exp(jnp.concatenate([cum0, cum1 + end0], axis=0)) * cols[:, 3:4]
        inner = jnp.exp(cum1) * cols[L:, 5:6]
        tail0 = jnp.exp(end0 - cum0) * cols[:L, 6:7] * dt[:L]
        tail1 = jnp.exp(end1 - cum1) * cols[L:, 4:5] * dt[L:]
        cum = jnp.concatenate([cum0, cum1], axis=0)
        blank = jnp.zeros((ROWS, 128 - 4 * HEADS), F32)
        wide = jnp.concatenate(
            [cum, dt, slab, jnp.concatenate([inner, inner], axis=0), blank], axis=1
        )
        hcol[...] = wide
        hrow[...] = wide.T[: 2 * HEADS]
        scaled0 = (xc[:L, :].astype(F32) * spread(tail0)).astype(BF16)
        scaled1 = (xc[L:, :].astype(F32) * spread(tail1)).astype(BF16)
        state0 = dot_tn(bcc[:L, :N], scaled0)
        state1 = dot_tn(bcc[L:, :N], scaled1)
        s0[...] = state0.astype(BF16)
        ends = jnp.concatenate(
            [inner[L - 1 :], slab[ROWS - 1 :], jnp.zeros((6, HEADS), F32)], axis=0
        )
        ends = spread(ends)
        final = ends[0:1] * state0 + state1
        factor = factor_rows(ends[1:2])
        for piece in range(CTX):
            part = final[8 * piece : 8 * piece + 8]
            pay[piece] = jnp.concatenate([part, factor], axis=0).astype(BF16)


def factor_rows(factor):
    high = factor.astype(BF16).astype(F32)
    row = lax.broadcasted_iota(jnp.int32, (8, CH), 0)
    return jnp.where(row == 0, high, jnp.where(row == 1, factor - high, 0.0))


def over_chips(kernel, blocked, fixed, shapes, scratch, mib, flops, name):
    whole = lambda a: pl.BlockSpec(a.shape, lambda i: (0,) * len(a.shape))
    return pl.pallas_call(
        kernel,
        grid=(CHIPS // 2,),
        in_specs=[spec for _, spec in blocked] + [whole(a) for a in fixed],
        out_specs=[whole(a) for a in shapes],
        out_shape=[pltpu.HBM(a.shape, a.dtype) for a in shapes],
        scratch_shapes=scratch,
        compiler_params=params(mib, True),
        cost_estimate=pl.CostEstimate(
            flops=flops, bytes_accessed=8 * 2**20, transcendentals=10**6
        ),
        name=name,
    )(*[a for a, _ in blocked], *fixed)


def two_chips(a, rows):
    return a, pl.BlockSpec((2, rows, FEAT), lambda i: (i, 0, 0))


def their_rows(w):
    return w, pl.BlockSpec((4 * FEAT, CH), lambda i: (i, 0))


def scan_input(own, sib, w_x, fixed):
    shapes = [
        jax.ShapeDtypeStruct((ROWS, CH), BF16),
        jax.ShapeDtypeStruct((ROWS, 2 * N), BF16),
        jax.ShapeDtypeStruct((ROWS, 128), F32),
        jax.ShapeDtypeStruct((2 * HEADS, ROWS), F32),
        jax.ShapeDtypeStruct((N, CH), BF16),
        jax.ShapeDtypeStruct((CTX, 16, CH), BF16),
    ]
    blocked = [two_chips(a, ALL_ROWS + COLS) for a in (own, sib)]
    blocked += [their_rows(w_x)]
    scratch = [
        pltpu.VMEM((ALL_ROWS, CH), F32),
        pltpu.VMEM((ALL_ROWS, COLS), F32),
        pltpu.VMEM((ALL_ROWS, 2 * N), F32),
    ]
    flops = 2 * ALL_ROWS * 4096 * (CH + COLS)
    return over_chips(
        scan_input_kernel, blocked, fixed, shapes, scratch, 22, flops, "scan_input"
    )


def gate_kernel(own, sib, w_z, gates, acc):
    step = pl.program_id(0)
    add_to(acc, step, dot(step_tokens(own, sib, HALO), step_rows(w_z)))

    @pl.when(step == pl.num_programs(0) - 1)
    def _():
        for at in range(0, ROWS, 64):
            gates[at : at + 64, :] = silu(acc[at : at + 64, :].astype(BF16).astype(F32))


def gate(own, sib, w_z):
    shapes = [jax.ShapeDtypeStruct((ROWS, CH), F32)]
    blocked = [two_chips(a, ALL_ROWS) for a in (own, sib)] + [their_rows(w_z)]
    scratch = [pltpu.VMEM((ROWS, CH), F32)]
    flops = 2 * ROWS * 4096 * CH
    return over_chips(gate_kernel, blocked, [], shapes, scratch, 16, flops, "gate")[0]


def intra_kernel(xc, bcc, hcol, hrow, s0, cols, seg_row, skip, y, c_out, decays):
    c_out[...] = bcc[:, N:]
    decays[...] = hcol[...]
    for block in range(2):
        intra_block(block * L, xc, bcc, hcol, hrow, s0, cols, seg_row, skip, y)


def intra_block(at, xc, bcc, hcol, hrow, s0, cols, seg_row, skip, y):
    b_vals, c_vals = bcc[at : at + L, :N], bcc[at : at + L, N:]
    after = lax.broadcasted_iota(jnp.int32, (L, L), 0) >= lax.broadcasted_iota(
        jnp.int32, (L, L), 1
    )
    same = cols[at : at + L, 7:8] == seg_row[0:1, at : at + L]
    scores = jnp.where(after & same, dot_nt(c_vals, b_vals), 0.0)
    for half in range(2):
        lanes = slice(half * 256, half * 256 + 256)
        weights, values = [], []
        x_half = xc[at : at + L, lanes]
        head_of = lax.broadcasted_iota(jnp.int32, (1, 256), 1) // P_SIZE
        for part in range(4):
            head = half * 4 + part
            gap = hcol[at : at + L, head : head + 1] - hrow[head : head + 1, at : at + L]
            decay = jnp.exp(jnp.minimum(gap, 0.0))
            dt_row = hrow[HEADS + head : HEADS + head + 1, at : at + L]
            weights.append((scores * decay * dt_row).astype(BF16))
            values.append(x_half * (head_of == part).astype(BF16))
        out = dot(jnp.concatenate(weights, axis=1), jnp.concatenate(values, axis=0))
        out = out + skip[:, lanes] * x_half.astype(F32)
        if at:
            carried = spread(hcol[at : at + L, 3 * HEADS : 4 * HEADS], half * 4, 4)
            out = out + carried * dot(c_vals, s0[:, lanes])
        y[at : at + L, lanes] = out


def intra(*args):
    shapes = [((ROWS, CH), F32), ((ROWS, N), BF16), ((ROWS, 128), F32)]
    return pl.pallas_call(
        intra_kernel,
        in_specs=[VMEM] * len(args),
        out_specs=[VMEM] * len(shapes),
        out_shape=[jax.ShapeDtypeStruct(*shape) for shape in shapes],
        compiler_params=params(12),
        cost_estimate=pl.CostEstimate(
            flops=2 * ROWS * L * CH * 4, bytes_accessed=4 * 2**20, transcendentals=2 * 10**6
        ),
        name="intra",
    )(*args)


def prefix_kernel(pieces, out):
    total = jnp.zeros((8, CH), F32)
    for pair in range(8):
        held = []
        for place in (2 * pair, 2 * pair + 1):
            held.append(total)
            piece = pieces[place].astype(F32)
            total = total * (piece[8:9] + piece[9:10]) + piece[:8]
        out[16 * pair : 16 * pair + 16, :] = jnp.concatenate(held, axis=0).astype(BF16)


def prefix(pieces):
    return pl.pallas_call(
        prefix_kernel,
        in_specs=[VMEM],
        out_specs=VMEM,
        out_shape=jax.ShapeDtypeStruct((N, CH), BF16),
        compiler_params=params(8),
        name="prefix",
    )(pieces)


def join_kernel(y, gates, cc, hcol, state, gain, out):
    for at in range(0, ROWS, 128):
        c_vals = cc[at : at + 128, :]
        carried = spread(hcol[at : at + 128, 2 * HEADS : 3 * HEADS])
        total = y[at : at + 128, :] + carried * dot(c_vals, state[...])
        gated = total * gates[at : at + 128, :]
        square = jnp.sum(gated * gated, axis=1, keepdims=True)
        high = square.astype(BF16).astype(F32)
        lane = lax.broadcasted_iota(jnp.int32, (128, 128), 1)
        out[at : at + 128, :CH] = (gated * gain[...]).astype(BF16)
        out[at : at + 128, CH:] = jnp.where(lane < 64, high, square - high).astype(BF16)


def join(*args):
    return pl.pallas_call(
        join_kernel,
        in_specs=[VMEM] * len(args),
        out_specs=VMEM,
        out_shape=jax.ShapeDtypeStruct((ROWS, CH + 128), BF16),
        compiler_params=params(12),
        cost_estimate=pl.CostEstimate(
            flops=2 * ROWS * N * CH, bytes_accessed=4 * 2**20, transcendentals=0
        ),
        name="join",
    )(*args)


def project_kernel(place, own, sib, w, out):
    del place
    square = own[:, CH:].astype(F32) + sib[:, CH:].astype(F32)
    scale = lax.rsqrt((square[:, 0:1] + square[:, 64:65]) / (2.0 * CH) + NORM_EPS)
    values = jnp.concatenate([own[:, :CH], sib[:, :CH]], axis=1)
    rows = jnp.concatenate([w[0], w[1]], axis=1)
    out[0] = (dot(values, rows) * scale).astype(BF16)


def project(own, sib, w_all, y_low):
    def columns(chip, place):
        return lax.rem(chip, 4), lax.rem(lax.div(chip, 4) + place[0], 2), 0

    whole = pl.BlockSpec(own.shape, lambda i, place: (0, 0))
    return pl.pallas_call(
        project_kernel,
        grid_spec=pltpu.PrefetchScalarGridSpec(
            num_scalar_prefetch=1,
            grid=(CHIPS,),
            in_specs=[whole, whole, pl.BlockSpec((2, 2 * CH, 128), columns)],
            out_specs=pl.BlockSpec((1, ROWS, 256), lambda i, place: (i, 0, 0)),
        ),
        out_shape=jax.ShapeDtypeStruct((CHIPS, ROWS, 256), BF16),
        compiler_params=params(14, True),
        cost_estimate=pl.CostEstimate(
            flops=8 * ROWS * CH * 2048, bytes_accessed=8 * 2**20, transcendentals=0
        ),
        name="project",
    )(y_low[None], own, sib, w_all)


def swapped(value, bit):
    return lax.ppermute(value, "tp", [(i, i ^ bit) for i in range(16)])


def next_ctx(value):
    return lax.ppermute(value, "ctx", [(i, i + 1) for i in range(15)])


def between_chips(value):
    same_core = [[2 * chip + core for chip in range(CHIPS)] for core in range(CORES)]
    return lax.all_to_all(value, "tp", 0, 0, axis_index_groups=same_core)


def across_y(value):
    return lax.ppermute(value, "ctx", [(i, i ^ Z_RING) for i in range(CTX)])


def along_z(value, steps):
    pairs = [(i, i // Z_RING * Z_RING + (i + steps) % Z_RING) for i in range(CTX)]
    return lax.ppermute(value, "ctx", pairs)


def put_along_z(held, piece, distance, row=0):
    place = (lax.axis_index("ctx") + distance) % Z_RING
    return lax.dynamic_update_slice(held, piece[None], (place, row, 0))


def gathered_along_z(mine):
    held = jnp.zeros((Z_RING,) + mine.shape, mine.dtype)
    held = put_along_z(held, mine, 0)
    above, below = mine, mine
    for distance in range(1, Z_RING // 2):
        below, above = along_z(below, 1), along_z(above, -1)
        held = put_along_z(put_along_z(held, below, -distance), above, distance)
    return held, below, above


def between_slabs(value):
    return lax.all_to_all(value, "ctx", 0, 0)


def together(*values):
    return lax.optimization_barrier(values)


def pick(core, first, second):
    return jnp.where(core == 0, first, second)


def document_columns(seg_ids, ids_prior):
    ids_all = jnp.concatenate([ids_prior, seg_ids])
    prior = ids_prior[2]
    same = lambda a: (seg_ids == a).astype(F32)
    columns = [same(ids_all[tap : tap + ROWS]) for tap in range(CONV - 1)]
    columns += [same(prior), same(seg_ids[-1]), same(seg_ids[L - 1]), same(seg_ids[L - 1])]
    columns += [seg_ids.astype(F32)]
    cols = jnp.pad(jnp.stack(columns, axis=1), ((0, 0), (0, 128 - len(columns))))
    return cols, jnp.broadcast_to(seg_ids.astype(F32)[None], (8, ROWS))


def local(
    tokens,
    seg_ids,
    w_x,
    w_z,
    w_bc,
    w_dt,
    conv_x,
    conv_x_bias,
    conv_bc,
    conv_bc_bias,
    dt_bias,
    decay_rate,
    skip_gain,
    norm_weight,
    w_out,
):
    rank = lax.axis_index("tp")
    core = rank % CORES
    chip = rank // CORES
    y_low = (lax.axis_index("ctx") // Z_RING).astype(jnp.int32)

    w_across = across_y(w_out)

    w_cols = jnp.concatenate(
        [w_bc.T.reshape(CHIPS, 2 * N, FEAT), w_dt.T.reshape(CHIPS, 2 * HEADS, FEAT)], axis=1
    )
    ids_row = jnp.pad((seg_ids[-3:] + 1).astype(BF16), (0, FEAT - 3))[None]
    halo = next_ctx(jnp.concatenate([ids_row, tokens[1 - HALO :]], axis=0))
    ids_prior = halo[0, :3].astype(jnp.int32) - 1
    shared = jnp.concatenate([halo, tokens], axis=0)
    shared = jnp.broadcast_to(shared[None], (CHIPS, ALL_ROWS, FEAT))
    sent = jnp.concatenate([shared, w_cols], axis=1)
    sent, w_across, w_out, seg_ids, conv_bc, conv_bc_bias, skip_gain = together(
        sent, w_across, w_out, seg_ids, conv_bc, conv_bc_bias, skip_gain
    )
    own = between_chips(sent)

    w_blocks = jnp.stack([w_out, w_across])
    halves = (w_blocks[:, :, :128], w_blocks[:, :, 128:])
    w_kept, w_sib = pick(core, *halves), swapped(pick(core, halves[1], halves[0]), 1)
    w_both = jnp.stack([w_kept, w_sib], axis=1).reshape(4 * CH, 128)
    w_held, below, above = gathered_along_z(w_both)

    cols, seg_row = document_columns(seg_ids, ids_prior)
    taps_bc = lax.dynamic_slice_in_dim(conv_bc, chip * 2 * N, 2 * N, 1)
    bias_bc = lax.dynamic_slice_in_dim(conv_bc_bias, chip * 2 * N, 2 * N, 0)[None]
    skip = jnp.repeat(skip_gain, P_SIZE)[None]
    fixed = [cols, conv_x, conv_x_bias[None], taps_bc, bias_bc, dt_bias[None], decay_rate[None]]
    own, w_held, below, above, fixed, seg_row, skip = together(
        own, w_held, below, above, fixed, seg_row, skip
    )
    last = along_z(below[: 2 * CH], 1), along_z(above[2 * CH :], -1)
    sib = swapped(own, 1)
    xc, bcc, hcol, hrow, s0, pay = scan_input(own, sib, w_x, fixed)
    own, sib, pay, last = together(own, sib, pay, last)
    w_all = put_along_z(put_along_z(w_held, last[0], 4), last[1], 4, 2 * CH)
    pieces = between_slabs(pay)
    gates = gate(own, sib, w_z)
    pieces, gates, xc, bcc = together(pieces, gates, xc, bcc)
    state = between_slabs(prefix(pieces).reshape(CTX, 8, CH)).reshape(N, CH)
    y, cc, decays = intra(xc, bcc, hcol, hrow, s0, fixed[0], seg_row, skip)
    mine = join(y, gates, cc, decays, state, norm_weight[None])
    parts = between_chips(project(mine, swapped(mine, 1), w_all, y_low))
    total = jnp.sum(parts.astype(F32), axis=0).astype(BF16)
    parts = (total[:, :128], total[:, 128:])
    kept = pick(core, *parts)
    given = swapped(pick(core, parts[1], parts[0]), 1)
    return jnp.concatenate([pick(core, kept, given), pick(core, given, kept)], axis=1)


def solution(mesh):
    return jax.shard_map(
        local,
        mesh=mesh,
        in_specs=(
            P("ctx", "tp"),
            P("ctx"),
            P(None, "tp"),
            P(None, "tp"),
            P("tp", None),
            P("tp", None),
            P(None, "tp"),
            P("tp"),
            P(),
            P(),
            P("tp"),
            P("tp"),
            P("tp"),
            P("tp"),
            P("tp", "ctx"),
        ),
        out_specs=P("ctx", "tp"),
        check_vma=False,
    )
```

```python
import functools

import jax
import jax.numpy as jnp
from jax import lax
from jax.experimental import pallas as pl
from jax.experimental.pallas import tpu as pltpu
from jax.sharding import PartitionSpec as P

H = 128
P_SIZE = 64
N = 128
G = 8
L = 256
CONV = 4
HALO = 16
NORM_EPS = 1e-05
HIGHEST = lax.Precision.HIGHEST

CHIPS = 8
CORES = 2
HEADS = 8
CH = HEADS * P_SIZE
ROWS = 512
FEAT = 256
Z_RING = 8
CTX = 16
ALL_ROWS = HALO + ROWS
COLS = 2 * N + 2 * HEADS
VMEM = pl.BlockSpec(memory_space=pltpu.VMEM)
BF16 = jnp.bfloat16
F32 = jnp.float32


def params(mib, grid=False):
    more = {"dimension_semantics": ("arbitrary",)} if grid else {}
    return pltpu.CompilerParams(vmem_limit_bytes=mib * 2**20, **more)


def dot(a, b):
    return jnp.dot(a, b, preferred_element_type=F32)


def dot_nt(a, b):
    return lax.dot_general(a, b, (((1,), (1,)), ((), ())), preferred_element_type=F32)


def dot_tn(a, b):
    return lax.dot_general(a, b, (((0,), (0,)), ((), ())), preferred_element_type=F32)


def silu(v):
    return v / (1.0 + jnp.exp(-v))


def spread(cols, first=0, count=HEADS):
    shape = (HEADS, count * P_SIZE)
    head = lax.broadcasted_iota(jnp.int32, shape, 0)
    lane = lax.broadcasted_iota(jnp.int32, shape, 1)
    pick = (head == lane // P_SIZE + first).astype(F32)
    return jnp.dot(cols, pick, precision=HIGHEST, preferred_element_type=F32)


def my_core():
    return lax.rem(lax.axis_index("tp"), CORES)


def add_to(acc, step, value):
    @pl.when(step == 0)
    def _():
        acc[...] = value

    @pl.when(step > 0)
    def _():
        acc[...] += value


def conv_chunk(raw, at, rows, masks, taps, offsets):
    total = offsets + taps[CONV - 1 : CONV, :] * raw[at + HALO : at + HALO + rows, :]
    for tap in range(CONV - 1):
        first = at + HALO - (CONV - 1) + tap
        shifted = raw[first : first + rows, :]
        total = total + taps[tap : tap + 1, :] * (shifted * masks[:, tap : tap + 1])
    return silu(total).astype(BF16)


def rounded(ref):
    ref[...] = ref[...].astype(BF16).astype(F32)


def step_sources():
    for slot in range(2):
        for same_core in (True, False):
            yield slot, same_core


def step_tokens(own, sib, first=0):
    refs = [(own if same_core else sib, slot) for slot, same_core in step_sources()]
    return jnp.concatenate([ref[slot, first:ALL_ROWS] for ref, slot in refs], axis=1)


def step_cols(own, sib):
    refs = [(own if same_core else sib, slot) for slot, same_core in step_sources()]
    return jnp.concatenate([ref[slot, ALL_ROWS:] for ref, slot in refs], axis=1)


def step_rows(w_ref):
    core = my_core()
    parts = []
    for slot, same_core in step_sources():
        from_core = core if same_core else 1 - core
        at = pl.multiple_of((slot * CORES + from_core) * FEAT, FEAT)
        parts.append(w_ref[pl.ds(at, FEAT), :])
    return jnp.concatenate(parts, axis=0)


def scan_input_kernel(
    own,
    sib,
    w_x,
    cols,
    taps_x,
    bias_x,
    taps_bc,
    bias_bc,
    dt_bias,
    decay,
    xc,
    bcc,
    hcol,
    hrow,
    s0,
    pay,
    acc_x,
    acc_bc,
    raw_bc,
):
    step = pl.program_id(0)
    core = my_core()
    toks = step_tokens(own, sib)
    add_to(acc_x, step, dot(toks, step_rows(w_x)))
    add_to(acc_bc, step, dot_nt(toks, step_cols(own, sib)))

    @pl.when(step == pl.num_programs(0) - 1)
    def _():
        raw_dt = acc_bc[HALO:, 2 * N :]
        raw_dt = jnp.where(core == 0, raw_dt[:, :HEADS], raw_dt[:, HEADS:])
        pre = raw_dt + dt_bias[...]
        dt = jnp.maximum(pre, 0.0) + jnp.log1p(jnp.exp(-jnp.abs(pre)))
        loga = -decay[...] * dt
        acc_x[...] = acc_x[...].astype(BF16).astype(F32)
        raw_bc[...] = acc_bc[:, : 2 * N].astype(BF16).astype(F32)
        for at in range(0, ROWS, 64):
            masks = cols[at : at + 64, :]
            xc[at : at + 64, :] = conv_chunk(acc_x, at, 64, masks, taps_x, bias_x[...])
            bcc[at : at + 64, :] = conv_chunk(raw_bc, at, 64, masks, taps_bc, bias_bc[...])
        lower = (
            lax.broadcasted_iota(jnp.int32, (L, L), 0) >= lax.broadcasted_iota(jnp.int32, (L, L), 1)
        ).astype(F32)
        cum0 = jnp.dot(lower, loga[:L], precision=HIGHEST, preferred_element_type=F32)
        cum1 = jnp.dot(lower, loga[L:], precision=HIGHEST, preferred_element_type=F32)
        end0, end1 = cum0[L - 1 :], cum1[L - 1 :]
        slab = jnp.exp(jnp.concatenate([cum0, cum1 + end0], axis=0)) * cols[:, 3:4]
        inner = jnp.exp(cum1) * cols[L:, 5:6]
        tail0 = jnp.exp(end0 - cum0) * cols[:L, 6:7] * dt[:L]
        tail1 = jnp.exp(end1 - cum1) * cols[L:, 4:5] * dt[L:]
        cum = jnp.concatenate([cum0, cum1], axis=0)
        blank = jnp.zeros((ROWS, 128 - 4 * HEADS), F32)
        wide = jnp.concatenate(
            [cum, dt, slab, jnp.concatenate([inner, inner], axis=0), blank], axis=1
        )
        hcol[...] = wide
        hrow[...] = wide.T[: 2 * HEADS]
        scaled0 = (xc[:L, :].astype(F32) * spread(tail0)).astype(BF16)
        scaled1 = (xc[L:, :].astype(F32) * spread(tail1)).astype(BF16)
        state0 = dot_tn(bcc[:L, :N], scaled0)
        state1 = dot_tn(bcc[L:, :N], scaled1)
        s0[...] = state0.astype(BF16)
        ends = jnp.concatenate(
            [inner[L - 1 :], slab[ROWS - 1 :], jnp.zeros((6, HEADS), F32)], axis=0
        )
        ends = spread(ends)
        final = ends[0:1] * state0 + state1
        factor = factor_rows(ends[1:2])
        for piece in range(CTX):
            part = final[8 * piece : 8 * piece + 8]
            pay[piece] = jnp.concatenate([part, factor], axis=0).astype(BF16)


def factor_rows(factor):
    high = factor.astype(BF16).astype(F32)
    row = lax.broadcasted_iota(jnp.int32, (8, CH), 0)
    return jnp.where(row == 0, high, jnp.where(row == 1, factor - high, 0.0))


def over_chips(kernel, blocked, fixed, shapes, scratch, mib, flops, name):
    whole = lambda a: pl.BlockSpec(a.shape, lambda i: (0,) * len(a.shape))
    return pl.pallas_call(
        kernel,
        grid=(CHIPS // 2,),
        in_specs=[spec for _, spec in blocked] + [whole(a) for a in fixed],
        out_specs=[whole(a) for a in shapes],
        out_shape=[pltpu.HBM(a.shape, a.dtype) for a in shapes],
        scratch_shapes=scratch,
        compiler_params=params(mib, True),
        cost_estimate=pl.CostEstimate(
            flops=flops, bytes_accessed=8 * 2**20, transcendentals=10**6
        ),
        name=name,
    )(*[a for a, _ in blocked], *fixed)


def two_chips(a, rows):
    return a, pl.BlockSpec((2, rows, FEAT), lambda i: (i, 0, 0))


def their_rows(w):
    return w, pl.BlockSpec((4 * FEAT, CH), lambda i: (i, 0))


def scan_input(own, sib, w_x, fixed):
    shapes = [
        jax.ShapeDtypeStruct((ROWS, CH), BF16),
        jax.ShapeDtypeStruct((ROWS, 2 * N), BF16),
        jax.ShapeDtypeStruct((ROWS, 128), F32),
        jax.ShapeDtypeStruct((2 * HEADS, ROWS), F32),
        jax.ShapeDtypeStruct((N, CH), BF16),
        jax.ShapeDtypeStruct((CTX, 16, CH), BF16),
    ]
    blocked = [two_chips(a, ALL_ROWS + COLS) for a in (own, sib)]
    blocked += [their_rows(w_x)]
    scratch = [
        pltpu.VMEM((ALL_ROWS, CH), F32),
        pltpu.VMEM((ALL_ROWS, COLS), F32),
        pltpu.VMEM((ALL_ROWS, 2 * N), F32),
    ]
    flops = 2 * ALL_ROWS * 4096 * (CH + COLS)
    return over_chips(
        scan_input_kernel, blocked, fixed, shapes, scratch, 22, flops, "scan_input"
    )


def gate_kernel(own, sib, w_z, gates, acc):
    step = pl.program_id(0)
    add_to(acc, step, dot(step_tokens(own, sib, HALO), step_rows(w_z)))

    @pl.when(step == pl.num_programs(0) - 1)
    def _():
        for at in range(0, ROWS, 64):
            gates[at : at + 64, :] = silu(acc[at : at + 64, :].astype(BF16).astype(F32))


def gate(own, sib, w_z):
    shapes = [jax.ShapeDtypeStruct((ROWS, CH), F32)]
    blocked = [two_chips(a, ALL_ROWS) for a in (own, sib)] + [their_rows(w_z)]
    scratch = [pltpu.VMEM((ROWS, CH), F32)]
    flops = 2 * ROWS * 4096 * CH
    return over_chips(gate_kernel, blocked, [], shapes, scratch, 16, flops, "gate")[0]


def intra_kernel(xc, bcc, hcol, hrow, s0, cols, seg_row, skip, y, c_out, decays):
    c_out[...] = bcc[:, N:]
    decays[...] = hcol[...]
    for block in range(2):
        intra_block(block * L, xc, bcc, hcol, hrow, s0, cols, seg_row, skip, y)


def intra_block(at, xc, bcc, hcol, hrow, s0, cols, seg_row, skip, y):
    b_vals, c_vals = bcc[at : at + L, :N], bcc[at : at + L, N:]
    after = lax.broadcasted_iota(jnp.int32, (L, L), 0) >= lax.broadcasted_iota(
        jnp.int32, (L, L), 1
    )
    same = cols[at : at + L, 7:8] == seg_row[0:1, at : at + L]
    scores = jnp.where(after & same, dot_nt(c_vals, b_vals), 0.0)
    for half in range(2):
        lanes = slice(half * 256, half * 256 + 256)
        weights, values = [], []
        x_half = xc[at : at + L, lanes]
        head_of = lax.broadcasted_iota(jnp.int32, (1, 256), 1) // P_SIZE
        for part in range(4):
            head = half * 4 + part
            gap = hcol[at : at + L, head : head + 1] - hrow[head : head + 1, at : at + L]
            decay = jnp.exp(jnp.minimum(gap, 0.0))
            dt_row = hrow[HEADS + head : HEADS + head + 1, at : at + L]
            weights.append((scores * decay * dt_row).astype(BF16))
            values.append(x_half * (head_of == part).astype(BF16))
        out = dot(jnp.concatenate(weights, axis=1), jnp.concatenate(values, axis=0))
        out = out + skip[:, lanes] * x_half.astype(F32)
        if at:
            carried = spread(hcol[at : at + L, 3 * HEADS : 4 * HEADS], half * 4, 4)
            out = out + carried * dot(c_vals, s0[:, lanes])
        y[at : at + L, lanes] = out


def intra(*args):
    shapes = [((ROWS, CH), F32), ((ROWS, N), BF16), ((ROWS, 128), F32)]
    return pl.pallas_call(
        intra_kernel,
        in_specs=[VMEM] * len(args),
        out_specs=[VMEM] * len(shapes),
        out_shape=[jax.ShapeDtypeStruct(*shape) for shape in shapes],
        compiler_params=params(12),
        cost_estimate=pl.CostEstimate(
            flops=2 * ROWS * L * CH * 4, bytes_accessed=4 * 2**20, transcendentals=2 * 10**6
        ),
        name="intra",
    )(*args)


def prefix_kernel(pieces, out):
    total = jnp.zeros((8, CH), F32)
    for pair in range(8):
        held = []
        for place in (2 * pair, 2 * pair + 1):
            held.append(total)
            piece = pieces[place].astype(F32)
            total = total * (piece[8:9] + piece[9:10]) + piece[:8]
        out[16 * pair : 16 * pair + 16, :] = jnp.concatenate(held, axis=0).astype(BF16)


def prefix(pieces):
    return pl.pallas_call(
        prefix_kernel,
        in_specs=[VMEM],
        out_specs=VMEM,
        out_shape=jax.ShapeDtypeStruct((N, CH), BF16),
        compiler_params=params(8),
        name="prefix",
    )(pieces)


def join_kernel(y, gates, cc, hcol, state, gain, out):
    for at in range(0, ROWS, 128):
        c_vals = cc[at : at + 128, :]
        carried = spread(hcol[at : at + 128, 2 * HEADS : 3 * HEADS])
        total = y[at : at + 128, :] + carried * dot(c_vals, state[...])
        gated = total * gates[at : at + 128, :]
        square = jnp.sum(gated * gated, axis=1, keepdims=True)
        high = square.astype(BF16).astype(F32)
        lane = lax.broadcasted_iota(jnp.int32, (128, 128), 1)
        out[at : at + 128, :CH] = (gated * gain[...]).astype(BF16)
        out[at : at + 128, CH:] = jnp.where(lane < 64, high, square - high).astype(BF16)


def join(*args):
    return pl.pallas_call(
        join_kernel,
        in_specs=[VMEM] * len(args),
        out_specs=VMEM,
        out_shape=jax.ShapeDtypeStruct((ROWS, CH + 128), BF16),
        compiler_params=params(12),
        cost_estimate=pl.CostEstimate(
            flops=2 * ROWS * N * CH, bytes_accessed=4 * 2**20, transcendentals=0
        ),
        name="join",
    )(*args)


def project_kernel(place, own, sib, w, out):
    del place
    square = own[:, CH:].astype(F32) + sib[:, CH:].astype(F32)
    scale = lax.rsqrt((square[:, 0:1] + square[:, 64:65]) / (2.0 * CH) + NORM_EPS)
    values = jnp.concatenate([own[:, :CH], sib[:, :CH]], axis=1)
    rows = jnp.concatenate([w[0], w[1]], axis=1)
    out[0] = (dot(values, rows) * scale).astype(BF16)


def project(own, sib, w_all, y_low):
    def columns(chip, place):
        return lax.rem(chip, 4), lax.rem(lax.div(chip, 4) + place[0], 2), 0

    whole = pl.BlockSpec(own.shape, lambda i, place: (0, 0))
    return pl.pallas_call(
        project_kernel,
        grid_spec=pltpu.PrefetchScalarGridSpec(
            num_scalar_prefetch=1,
            grid=(CHIPS,),
            in_specs=[whole, whole, pl.BlockSpec((2, 2 * CH, 128), columns)],
            out_specs=pl.BlockSpec((1, ROWS, 256), lambda i, place: (i, 0, 0)),
        ),
        out_shape=jax.ShapeDtypeStruct((CHIPS, ROWS, 256), BF16),
        compiler_params=params(14, True),
        cost_estimate=pl.CostEstimate(
            flops=8 * ROWS * CH * 2048, bytes_accessed=8 * 2**20, transcendentals=0
        ),
        name="project",
    )(y_low[None], own, sib, w_all)


def swapped(value, bit):
    return lax.ppermute(value, "tp", [(i, i ^ bit) for i in range(16)])


def next_ctx(value):
    return lax.ppermute(value, "ctx", [(i, i + 1) for i in range(15)])


def between_chips(value):
    same_core = [[2 * chip + core for chip in range(CHIPS)] for core in range(CORES)]
    return lax.all_to_all(value, "tp", 0, 0, axis_index_groups=same_core)


def across_y(value):
    return lax.ppermute(value, "ctx", [(i, i ^ Z_RING) for i in range(CTX)])


def along_z(value, steps):
    pairs = [(i, i // Z_RING * Z_RING + (i + steps) % Z_RING) for i in range(CTX)]
    return lax.ppermute(value, "ctx", pairs)


def put_along_z(held, piece, distance):
    place = (lax.axis_index("ctx") + distance) % Z_RING
    return lax.dynamic_update_slice(held, piece[None], (place, 0, 0))


def gathered_along_z(mine):
    held = jnp.zeros((Z_RING,) + mine.shape, mine.dtype)
    held = put_along_z(held, mine, 0)
    above, below = mine, mine
    for distance in range(1, Z_RING // 2):
        below, above = along_z(below, 1), along_z(above, -1)
        held = put_along_z(put_along_z(held, below, -distance), above, distance)
    return held, below


def between_slabs(value):
    return lax.all_to_all(value, "ctx", 0, 0)


def together(*values):
    return lax.optimization_barrier(values)


def pick(core, first, second):
    return jnp.where(core == 0, first, second)


def document_columns(seg_ids, ids_prior):
    ids_all = jnp.concatenate([ids_prior, seg_ids])
    prior = ids_prior[2]
    same = lambda a: (seg_ids == a).astype(F32)
    columns = [same(ids_all[tap : tap + ROWS]) for tap in range(CONV - 1)]
    columns += [same(prior), same(seg_ids[-1]), same(seg_ids[L - 1]), same(seg_ids[L - 1])]
    columns += [seg_ids.astype(F32)]
    cols = jnp.pad(jnp.stack(columns, axis=1), ((0, 0), (0, 128 - len(columns))))
    return cols, jnp.broadcast_to(seg_ids.astype(F32)[None], (8, ROWS))


def local(
    tokens,
    seg_ids,
    w_x,
    w_z,
    w_bc,
    w_dt,
    conv_x,
    conv_x_bias,
    conv_bc,
    conv_bc_bias,
    dt_bias,
    decay_rate,
    skip_gain,
    norm_weight,
    w_out,
):
    rank = lax.axis_index("tp")
    core = rank % CORES
    chip = rank // CORES
    y_low = (lax.axis_index("ctx") // Z_RING).astype(jnp.int32)

    w_across = across_y(w_out)

    w_cols = jnp.concatenate(
        [w_bc.T.reshape(CHIPS, 2 * N, FEAT), w_dt.T.reshape(CHIPS, 2 * HEADS, FEAT)], axis=1
    )
    ids_row = jnp.pad((seg_ids[-3:] + 1).astype(BF16), (0, FEAT - 3))[None]
    halo = next_ctx(jnp.concatenate([ids_row, tokens[1 - HALO :]], axis=0))
    ids_prior = halo[0, :3].astype(jnp.int32) - 1
    shared = jnp.concatenate([halo, tokens], axis=0)
    shared = jnp.broadcast_to(shared[None], (CHIPS, ALL_ROWS, FEAT))
    sent = jnp.concatenate([shared, w_cols], axis=1)
    sent, w_across, w_out, seg_ids, conv_bc, conv_bc_bias, skip_gain = together(
        sent, w_across, w_out, seg_ids, conv_bc, conv_bc_bias, skip_gain
    )
    own = between_chips(sent)

    w_blocks = jnp.stack([w_out, w_across])
    halves = (w_blocks[:, :, :128], w_blocks[:, :, 128:])
    w_kept, w_sib = pick(core, *halves), swapped(pick(core, halves[1], halves[0]), 1)
    w_both = jnp.stack([w_kept, w_sib], axis=1).reshape(4 * CH, 128)
    w_held, below = gathered_along_z(w_both)

    cols, seg_row = document_columns(seg_ids, ids_prior)
    taps_bc = lax.dynamic_slice_in_dim(conv_bc, chip * 2 * N, 2 * N, 1)
    bias_bc = lax.dynamic_slice_in_dim(conv_bc_bias, chip * 2 * N, 2 * N, 0)[None]
    skip = jnp.repeat(skip_gain, P_SIZE)[None]
    fixed = [cols, conv_x, conv_x_bias[None], taps_bc, bias_bc, dt_bias[None], decay_rate[None]]
    own, w_held, below, fixed, seg_row, skip = together(
        own, w_held, below, fixed, seg_row, skip
    )
    last = along_z(below, 1)
    sib = swapped(own, 1)
    xc, bcc, hcol, hrow, s0, pay = scan_input(own, sib, w_x, fixed)
    own, sib, pay, last = together(own, sib, pay, last)
    w_all = put_along_z(w_held, last, 4)
    pieces = between_slabs(pay)
    gates = gate(own, sib, w_z)
    pieces, gates, xc, bcc = together(pieces, gates, xc, bcc)
    state = between_slabs(prefix(pieces).reshape(CTX, 8, CH)).reshape(N, CH)
    y, cc, decays = intra(xc, bcc, hcol, hrow, s0, fixed[0], seg_row, skip)
    mine = join(y, gates, cc, decays, state, norm_weight[None])
    parts = between_chips(project(mine, swapped(mine, 1), w_all, y_low))
    total = jnp.sum(parts.astype(F32), axis=0).astype(BF16)
    parts = (total[:, :128], total[:, 128:])
    kept = pick(core, *parts)
    given = swapped(pick(core, parts[1], parts[0]), 1)
    return jnp.concatenate([pick(core, kept, given), pick(core, given, kept)], axis=1)


def solution(mesh):
    return jax.shard_map(
        local,
        mesh=mesh,
        in_specs=(
            P("ctx", "tp"),
            P("ctx"),
            P(None, "tp"),
            P(None, "tp"),
            P("tp", None),
            P("tp", None),
            P(None, "tp"),
            P("tp"),
            P(),
            P(),
            P("tp"),
            P("tp"),
            P("tp"),
            P("tp"),
            P("tp", "ctx"),
        ),
        out_specs=P("ctx", "tp"),
        check_vma=False,
    )
```
